32 devices in a mesh: pole: 2 (over y), row: 16 (over z, x, core).
Axes of the slice: x: 2, y: 2, z: 4, core: 2. Of those that a mesh axis runs over, the one named last changes fastest.
Arguments:
- anc_blocks: float32 [32, 384, 96], P(('pole', 'row')), parts along dimension 0, may hold values from -1 to 18, as said below
- anc_links: float32 [1536, 8, 256], P(('pole', 'row')), parts along dimension 0, may hold values from -0.21875 to 0.21875
- parent_links: float32 [14, 256, 256], P('pole'), parts along dimension 0, may hold values from -0.375 to 0.375
- pivot_inverse: float32 [16, 256, 256], P('pole'), parts along dimension 0, may hold values from -1 to 18, as said below
- pattern: int32 [8, 6], replicated, may hold values 0 or 1
Outputs:
- anc_panels: float32 [1536, 8, 256], P(('pole', 'row')), parts along dimension 0
- parent_blocks: float32 [14, 256, 256], P('pole'), parts along dimension 0
- diagonal_blocks: float32 [16, 256, 256], P('pole'), parts along dimension 0
The draws below stay inside these ranges and needn't reach their ends.
There are 2 independent parts, one for each index of `pole`. The reference program is written for one: setup_inputs(seed, part) draws one part's arguments, and reference() takes and returns one part's arrays. A program takes and returns all parts, laid end to end along the dimension named above; an argument that names none is the same for every part. Nothing has to cross between parts.
Inputs may be any that keep to these rules, and one draw needn't show every extreme that they name: `anc_blocks`: the matrix S that the blocks form is symmetric and positive definite. `pivot_inverse`: each block is symmetric and positive definite.
All inputs are finite; a program needn't handle non-finite values.
Results may differ from the reference program's by a relative error of at most 0.0001.
Values sent between devices are 32-bit elements; how exact they have to be, the bound alone decides.
No kernel may reach another device: no remote copies, remote signals or barrier semaphores. Data moves between devices by JAX's collectives and lax.ppermute only.
A program may use at most 128 MiB of HBM per device.

```python
import math
import jax
import jax.numpy as jnp
from jax import lax

RP = 48
W = 256
NS = 8
PCOL = 8
TILE = 128
PROWS = 2
NC = 768
NT = 6


def symmetric_matrix(noise_field, diagonal, factor):
    order = noise_field.shape[-1]
    symmetric = (noise_field + jnp.swapaxes(noise_field, -1, -2)) * factor
    indices = jnp.arange(order)
    identity_mask = (indices[:, None] == indices[None, :]).astype(jnp.float32)
    return symmetric * (1.0 - identity_mask) + identity_mask * diagonal[..., :, None]


def draw_anc_blocks(key, part):
    key = jax.random.fold_in(key, 11)
    first_key, second_key = jax.random.split(key, 2)
    noise_field = jnp.clip(jax.random.normal(first_key, (NC, NC), jnp.float32), -6.0, 6.0)
    diagonal = jax.random.uniform(second_key, (NC,), jnp.float32, 1.0, 2.0)
    assembled = symmetric_matrix(noise_field, diagonal, 0.35 / math.sqrt(2.0 * NC))
    grid_view = assembled.reshape(PROWS, PCOL * RP, PROWS, PCOL, RP)
    return jnp.transpose(grid_view, (0, 3, 1, 2, 4)).reshape(PROWS * PCOL, PCOL * RP, PROWS * RP)


def draw_pivot_inverse(key, part):
    key = jax.random.fold_in(key, 23)
    first_key, second_key = jax.random.split(key, 2)
    noise_field = jnp.clip(jax.random.normal(first_key, (NS, W, W), jnp.float32), -6.0, 6.0)
    diagonal = jax.random.uniform(second_key, (NS, W), jnp.float32, 0.5, 2.0)
    assembled = symmetric_matrix(noise_field, diagonal, 0.2 / math.sqrt(2.0 * W))
    return assembled


def touch_ends(values, own_key, low, top_value):
    extent = values.shape
    spot = [jax.random.randint(jax.random.fold_in(own_key, axis), (), 0, extent[axis]) for axis in range(len(extent))]
    values = values.at[tuple(spot)].set(low)
    longest = extent.index(max(extent))
    spot[longest] = (spot[longest] + 1) % extent[longest]
    return values.at[tuple(spot)].set(top_value)


def block_scale(rng, dims, shards, low, high):
    loudness, own = 1.0, jax.random.fold_in(rng, 6)
    for dim, parts in shards:
        draws = jnp.exp(jax.random.uniform(jax.random.fold_in(own, dim), (parts,), jnp.float32, low / len(shards), high / len(shards)))
        loudness = loudness * jnp.repeat(draws, dims[dim] // parts).reshape([-1 if axis == dim else 1 for axis in range(len(dims))])
    return loudness


def gaussian(stream_key, shape, spread, reach, pieces=(), held_as=jnp.bfloat16):
    entries = spread * jax.random.normal(stream_key, shape, jnp.float32)
    if pieces:
        entries = entries * block_scale(stream_key, shape, pieces, -0.22, 0.18)
    return jnp.clip(entries, -reach, reach).astype(held_as)


def setup_inputs(seed: int = 0, part: int = 0) -> dict:
    splits = jax.random.split(jax.random.key(seed), 6)
    part_keys = jax.random.split(jax.random.fold_in(splits[5], part), 6)
    anc_blocks = draw_anc_blocks(jax.random.fold_in(jax.random.fold_in(splits[5], part), 71), part)
    anc_links = gaussian(part_keys[1], (NC, NS, W), NC ** -0.5, 0.21875, ((0, 16),), jnp.float32)
    parent_links = gaussian(part_keys[2], (NS - 1, W, W), W ** -0.5, 0.375, (), jnp.float32)
    pivot_inverse = draw_pivot_inverse(jax.random.fold_in(jax.random.fold_in(splits[5], part), 71), part)
    pattern = touch_ends((jax.random.randint(splits[4], (NS, NT), 0, 4) < 3).astype(jnp.int32), jax.random.fold_in(splits[4], 1), 0, 1)
    return {"anc_blocks": anc_blocks, "anc_links": anc_links, "parent_links": parent_links, "pivot_inverse": pivot_inverse, "pattern": pattern}


def unblock(anc_blocks):
    grid_view = anc_blocks.reshape(PROWS, PCOL, PCOL * RP, PROWS, RP)
    return jnp.transpose(grid_view, (0, 2, 3, 1, 4)).reshape(NC, NC)


def product(left, right):
    return jnp.dot(left, right, precision=lax.Precision.HIGHEST, preferred_element_type=jnp.float32)


def reference(anc_blocks, anc_links, parent_links, pivot_inverse, pattern):
    ancestor = unblock(anc_blocks)
    row_keep = jnp.repeat(pattern, TILE, axis=1).astype(jnp.float32)
    panels = []
    parents = []
    diagonals = []
    for super_node in range(NS):
        link_panel = anc_links[:, super_node, :] * row_keep[super_node][:, None]
        image_rows = product(ancestor, link_panel)
        if super_node > 0:
            parent_link = parent_links[super_node - 1]
            inverse_panel = -(image_rows + product(panels[-1], parent_link))
            parent_block = -(product(panels[-1].T, link_panel) + product(diagonals[-1], parent_link))
            diagonal = pivot_inverse[super_node] - product(link_panel.T, inverse_panel) - product(parent_link.T, parent_block)
            parents.append(parent_block)
        else:
            inverse_panel = -image_rows
            diagonal = pivot_inverse[super_node] - product(link_panel.T, inverse_panel)
        panels.append(inverse_panel)
        diagonals.append(diagonal)
    return jnp.stack(panels, axis=1), jnp.stack(parents), jnp.stack(diagonals)
```

```python
import jax
import jax.numpy as jnp
from jax import lax
from jax.sharding import PartitionSpec as P

PCOL = 8
TILE = 128
GATHER_LIMIT = 16 * 2**20


def product(left, right):
    return jnp.dot(left, right, precision=lax.Precision.HIGH, preferred_element_type=jnp.float32)


def inner_product(left, right):
    return lax.dot_general(
        left,
        right,
        (((0,), (0,)), ((), ())),
        precision=lax.Precision.HIGH,
        preferred_element_type=jnp.float32,
    )


def swap_bit(value, bit):
    mask = 2**bit
    return lax.ppermute(value, "row", [(i, i ^ mask) for i in range(lax.axis_size("row"))])


def ring_chips(count):
    return list(range(0, count, 2)) + list(range(count - 1, 0, -2))


def ring_pairs(count, shift):
    order = ring_chips(count)
    pairs = []
    for place, chip in enumerate(order):
        target = order[(place + shift) % count]
        pairs += [(2 * chip + core, 2 * target + core) for core in range(2)]
    return pairs


def ring_place(chip, count):
    return jnp.where(chip % 2 == 0, chip // 2, count - 1 - chip // 2)


def ring_chip(place, count):
    return jnp.where(place < count // 2, 2 * place, 2 * (count - 1 - place) + 1)


def masked_links(my_index, anc_links, pattern):
    rows_here = anc_links.shape[0]
    tile_index = (my_index * rows_here + jnp.arange(rows_here, dtype=jnp.int32)) // TILE
    row_keep = jnp.take(pattern, tile_index, axis=1) != 0
    return jnp.where(row_keep[:, :, None], jnp.swapaxes(anc_links, 0, 1), 0.0)


def reduced_links(links, parent_links):
    reduced = [links[0]]
    for node in range(1, links.shape[0]):
        reduced.append(links[node] - product(reduced[-1], parent_links[node - 1]))
    return reduced


def local_chain(parent_links, pivot_inverse):
    inner = [pivot_inverse[0]]
    cross = []
    for node in range(1, pivot_inverse.shape[0]):
        link = parent_links[node - 1]
        cross.append(product(inner[-1], link))
        inner.append(pivot_inverse[node] + inner_product(link, cross[-1]))
    return inner, cross


def gather_rounds(message, my_index, count):
    core = my_index % 2
    place = ring_place(my_index // 2, count)

    def owner(shift, other):
        chip = ring_chip((place + shift + count) % count, count)
        return 2 * chip + jnp.where(other, 1 - core, core)

    ahead, behind = ring_pairs(count, 1), ring_pairs(count, -1)
    arrivals = [(owner(0, False), message), (owner(0, True), swap_bit(message, 0))]
    upward = downward = message
    for step in range(1, (count + 1) // 2):
        upward = lax.ppermute(upward, "row", ahead)
        downward = lax.ppermute(downward, "row", behind)
        arrivals += [(owner(-step, False), upward), (owner(step, False), downward)]
        arrivals += [(owner(-step, True), swap_bit(upward, 0)), (owner(step, True), swap_bit(downward, 0))]
    if count % 2 == 0 and count > 1:
        pairs = [p for p in ahead if p[0] % 2 == 0] + [p for p in behind if p[0] % 2 == 1]
        last = lax.ppermute(jnp.where(core == 0, upward, downward), "row", pairs)
        arrivals += [(owner(count // 2, False), last), (owner(count // 2, True), swap_bit(last, 0))]
    return arrivals


def gather_plan(anc_blocks, anc_links, parent_links, pivot_inverse, pattern):
    my_index = lax.axis_index("row")
    size = lax.axis_size("row")
    rows, nodes, width = anc_links.shape
    order = rows * size
    half = my_index // PCOL
    block = anc_blocks[0].T.reshape(2, rows, order // 2)
    mine = lax.dynamic_index_in_dim(block, half, 0, False)
    theirs = swap_bit(lax.dynamic_index_in_dim(block, 1 - half, 0, False), PCOL.bit_length() - 1)
    low, high = jnp.where(half == 0, mine, theirs), jnp.where(half == 0, theirs, mine)
    links = masked_links(my_index, anc_links, pattern)
    message = jnp.concatenate(reduced_links(links, parent_links) + [low, high], axis=1)
    inner, cross = local_chain(parent_links, pivot_inverse)
    whole = jnp.zeros((order, message.shape[1]), jnp.float32)
    for owner, part in gather_rounds(message, my_index, size // 2):
        whole = lax.dynamic_update_slice(whole, part, (owner * rows, 0))
    links, ancestor = whole[:, : nodes * width], whole[:, nodes * width :]
    image = product(ancestor, links)
    panels = -lax.dynamic_slice_in_dim(image, my_index * rows, rows, 0).reshape(rows, nodes, width)
    column = lambda array, node: array[:, node * width : (node + 1) * width]
    diagonals = [
        inner[node] + inner_product(column(links, node), column(image, node)) for node in range(nodes)
    ]
    parents = [
        inner_product(column(links, node - 1), column(image, node)) - cross[node - 1]
        for node in range(1, nodes)
    ]
    return panels, jnp.stack(parents), jnp.stack(diagonals)


def spread_plan(anc_blocks, anc_links, parent_links, pivot_inverse, pattern):
    my_index = lax.axis_index("row")
    total_bits = lax.axis_size("row").bit_length() - 1
    low_bits = PCOL.bit_length() - 1
    rows, nodes, width = anc_links.shape
    links = jnp.concatenate(reduced_links(masked_links(my_index, anc_links, pattern), parent_links), axis=1)
    segment = links
    for bit in range(low_bits, total_bits):
        partner = swap_bit(segment, bit)
        upper = my_index >> bit & 1
        segment = lax.dynamic_update_slice_in_dim(
            jnp.concatenate([partner, partner], 0), segment, upper * segment.shape[0], 0
        )
    image = product(anc_blocks[0], segment)
    for bit in reversed(range(low_bits)):
        half_rows = image.shape[0] // 2
        upper = my_index >> bit & 1
        retained = lax.dynamic_slice_in_dim(image, upper * half_rows, half_rows, 0)
        outgoing = lax.dynamic_slice_in_dim(image, (1 - upper) * half_rows, half_rows, 0)
        image = retained + swap_bit(outgoing, bit)
    column = lambda array, node: array[:, node * width : (node + 1) * width]
    terms = [inner_product(column(links, node), column(image, node)) for node in range(nodes)]
    terms += [inner_product(column(links, node - 1), column(image, node)) for node in range(1, nodes)]
    totals = lax.psum(jnp.stack(terms), "row")
    inner, cross = local_chain(parent_links, pivot_inverse)
    diagonals = jnp.stack(inner) + totals[:nodes]
    parents = totals[nodes:] - jnp.stack(cross)
    return -image.reshape(rows, nodes, width), parents, diagonals


def on_device(anc_blocks, anc_links, parent_links, pivot_inverse, pattern):
    size = lax.axis_size("row")
    rows, nodes, width = anc_links.shape
    whole_bytes = 4 * size * rows * (nodes * width + size * rows)
    plan = gather_plan if size == 2 * PCOL and whole_bytes <= GATHER_LIMIT else spread_plan
    return plan(anc_blocks, anc_links, parent_links, pivot_inverse, pattern)


def solution(mesh):
    return jax.shard_map(
        on_device,
        mesh=mesh,
        in_specs=(
            P(("pole", "row"), None, None),
            P(("pole", "row"), None, None),
            P("pole", None, None),
            P("pole", None, None),
            P(),
        ),
        out_specs=(P(("pole", "row"), None, None), P("pole", None, None), P("pole", None, None)),
        check_vma=False,
    )
```

```python
import jax
import jax.numpy as jnp
from jax import lax
from jax.experimental import pallas as pl
from jax.experimental.pallas import tpu as pltpu
from jax.sharding import PartitionSpec as P

PCOL = 8
TILE = 128
GATHER_LIMIT = 16 * 2**20
VMEM_LIMIT = 28 * 2**20


def product(left, right):
    return jnp.dot(left, right, precision=lax.Precision.HIGH, preferred_element_type=jnp.float32)


def inner_product(left, right):
    return lax.dot_general(
        left,
        right,
        (((0,), (0,)), ((), ())),
        precision=lax.Precision.HIGH,
        preferred_element_type=jnp.float32,
    )


def swap_bit(value, bit):
    mask = 2**bit
    return lax.ppermute(value, "row", [(i, i ^ mask) for i in range(lax.axis_size("row"))])


def ring_chips(count):
    return list(range(0, count, 2)) + list(range(count - 1, 0, -2))


def ring_pairs(count, shift):
    order = ring_chips(count)
    pairs = []
    for place, chip in enumerate(order):
        target = order[(place + shift) % count]
        pairs += [(2 * chip + core, 2 * target + core) for core in range(2)]
    return pairs


def ring_place(chip, count):
    return jnp.where(chip % 2 == 0, chip // 2, count - 1 - chip // 2)


def ring_chip(place, count):
    return jnp.where(place < count // 2, 2 * place, 2 * (count - 1 - place) + 1)


def masked_links(my_index, anc_links, pattern):
    rows_here = anc_links.shape[0]
    tile_index = (my_index * rows_here + jnp.arange(rows_here, dtype=jnp.int32)) // TILE
    row_keep = jnp.take(pattern, tile_index, axis=1) != 0
    return jnp.where(row_keep[:, :, None], jnp.swapaxes(anc_links, 0, 1), 0.0)


def reduced_links(links, parent_links):
    reduced = [links[0]]
    for node in range(1, links.shape[0]):
        reduced.append(links[node] - product(reduced[-1], parent_links[node - 1]))
    return reduced


def local_chain(parent_links, pivot_inverse):
    inner = [pivot_inverse[0]]
    cross = []
    for node in range(1, pivot_inverse.shape[0]):
        link = parent_links[node - 1]
        cross.append(product(inner[-1], link))
        inner.append(pivot_inverse[node] + inner_product(link, cross[-1]))
    return inner, cross


def halves(value):
    high = value.astype(jnp.bfloat16)
    return high, (value - high.astype(jnp.float32)).astype(jnp.bfloat16)


def dot_halves(left, right, dims=((1,), (0,))):
    def one(a, b):
        return lax.dot_general(a, b, (dims, ((), ())), preferred_element_type=jnp.float32)

    return one(left[0], right[0]) + (one(left[0], right[1]) + one(left[1], right[0]))


def kernel_params(flops, moved, **more):
    return dict(
        compiler_params=pltpu.CompilerParams(vmem_limit_bytes=VMEM_LIMIT, **more),
        cost_estimate=pl.CostEstimate(flops=flops, bytes_accessed=moved, transcendentals=0),
    )


def transposed_block(block):
    def kernel(block_ref, out_ref):
        out_ref[...] = block_ref[...].T

    shape = (block.shape[1], block.shape[0])
    return pl.pallas_call(
        kernel,
        out_shape=jax.ShapeDtypeStruct(shape, jnp.float32),
        name="turn_block",
        **kernel_params(block.size, 8 * block.size),
    )(block)


def link_chain(anc_links, parent_links, pattern):
    rows, nodes, width = anc_links.shape
    tiles = pattern.shape[1]

    def kernel(links_ref, parent_ref, pattern_ref, out_ref):
        first = lax.axis_index("row") * rows
        tile = first // TILE
        next_tile = jnp.minimum(tile + 1, tiles - 1)
        row = first + lax.broadcasted_iota(jnp.int32, (rows, width), 0)
        in_first = row < (tile + 1) * TILE
        reduced = None
        for node in range(nodes):
            keep = jnp.where(in_first, pattern_ref[node, tile], pattern_ref[node, next_tile])
            links = jnp.where(keep != 0, links_ref[:, node, :], 0.0)
            if node > 0:
                links = links - dot_halves(halves(reduced), halves(parent_ref[node - 1]))
            out_ref[:, node * width : (node + 1) * width] = links
            reduced = links

    return pl.pallas_call(
        kernel,
        out_shape=jax.ShapeDtypeStruct((rows, nodes * width), jnp.float32),
        in_specs=[
            pl.BlockSpec(memory_space=pltpu.VMEM),
            pl.BlockSpec(memory_space=pltpu.VMEM),
            pl.BlockSpec(memory_space=pltpu.SMEM),
        ],
        out_specs=pl.BlockSpec(memory_space=pltpu.VMEM),
        name="link_chain",
        **kernel_params(12 * rows * nodes * width * width, 4 * parent_links.size),
    )(anc_links, parent_links, pattern)


def inner_chain(parent_links, pivot_inverse):
    nodes, width, _ = pivot_inverse.shape

    def kernel(parent_ref, pivot_ref, cross_ref, inner_ref, inner):
        node = pl.program_id(0)

        @pl.when(node == 0)
        def _():
            inner[...] = pivot_ref[0]

        @pl.when(node > 0)
        def _():
            link = halves(parent_ref[0])
            cross = dot_halves(halves(inner[...]), link)
            cross_ref[0] = -cross
            inner[...] = pivot_ref[0] + dot_halves(link, halves(cross), ((0,), (0,)))

        inner_ref[0] = inner[...]

    below = pl.BlockSpec((1, width, width), lambda node: (jnp.maximum(node - 1, 0), 0, 0))
    own = pl.BlockSpec((1, width, width), lambda node: (node, 0, 0))
    return pl.pallas_call(
        kernel,
        grid=(nodes,),
        out_shape=[
            jax.ShapeDtypeStruct(parent_links.shape, jnp.float32),
            jax.ShapeDtypeStruct(pivot_inverse.shape, jnp.float32),
        ],
        in_specs=[below, own],
        out_specs=[below, own],
        scratch_shapes=[pltpu.VMEM((width, width), jnp.float32)],
        name="inner_chain",
        **kernel_params(12 * nodes * width**3, 16 * pivot_inverse.size),
    )(parent_links, pivot_inverse)


def assemble(parts):
    owners = jnp.stack([owner for owner, _ in parts])
    arrays = [array for _, array in parts]
    rows, columns = arrays[0].shape[0] // 2, arrays[0].shape[1]
    count = len(arrays)

    def kernel(owner_ref, *refs):
        sources, out_ref, sems = refs[:count], refs[count], refs[count + 1]
        copies = []
        for place, source in enumerate(sources):
            owner = owner_ref[place]
            for piece in range(2):
                row = (owner % PCOL + PCOL * piece) * rows
                copies.append(
                    pltpu.make_async_copy(
                        source.at[pl.ds(piece * rows, rows), :],
                        out_ref.at[
                            pl.ds(pl.multiple_of(row, 8), rows),
                            pl.ds(pl.multiple_of(owner // PCOL * columns, 128), columns),
                        ],
                        sems.at[2 * place + piece],
                    )
                )
        for copy in copies:
            copy.start()
        for copy in copies:
            copy.wait()

    order = 2 * columns
    return pl.pallas_call(
        kernel,
        out_shape=jax.ShapeDtypeStruct((order, order), jnp.float32),
        in_specs=[pl.BlockSpec(memory_space=pltpu.SMEM)] + [pl.BlockSpec(memory_space=pl.ANY)] * count,
        out_specs=pl.BlockSpec(memory_space=pl.ANY),
        scratch_shapes=[pltpu.SemaphoreType.DMA((2 * count,))],
        name="assemble",
        **kernel_params(order * order, 8 * order * order),
    )(owners, *arrays)


def border(parts, ancestor, state, parents, diagonals, my_index=None):
    owners = jnp.stack([owner for owner, _ in parts] + ([my_index] if my_index is not None else []))
    arrays = [array for _, array in parts]
    count, last, start = len(arrays), my_index is not None, state is None
    nodes, width, _ = diagonals.shape
    rows = arrays[0].shape[0]
    fresh, order = rows * count, ancestor.shape[0]
    taken = count + last
    bf16 = jnp.bfloat16

    def kernel(owner_ref, *refs):
        refs = list(refs)
        take = lambda number: [refs.pop(0) for _ in range(number)]
        new_refs = take(count)
        (ancestor_ref,) = take(1)
        state_refs = take(0 if start else 2)
        parents_ref, diagonals_ref = take(2)
        parents_out, diagonals_out = take(2)
        held = take(2)
        panel_out = take(1)[0] if last else None
        ancestor_rows, rows_high, rows_low, turned_high, turned_low, total, sems = refs
        node = pl.program_id(0)

        @pl.when(node == 0)
        def _():
            copies = [
                pltpu.make_async_copy(
                    ancestor_ref.at[pl.ds(pl.multiple_of(owner_ref[place] * rows, 8), rows), :],
                    ancestor_rows.at[pl.ds(place * rows, rows), :],
                    sems.at[place],
                )
                for place in range(taken)
            ]
            for copy in copies:
                copy.start()
            piece = lax.broadcasted_iota(jnp.int32, (1, order), 1) // rows
            weight = jnp.ones((1, order), jnp.float32)
            for place in range(count):
                weight = jnp.where(piece == owner_ref[place], 0.5, weight)
            for copy in copies:
                copy.wait()
            values = ancestor_rows[0:fresh, :] * weight
            rows_high[0:fresh, :], rows_low[0:fresh, :] = halves(values)
            if last:
                rows_high[fresh:, :], rows_low[fresh:, :] = halves(ancestor_rows[fresh:, :])
            turned_high[1] = jnp.zeros(turned_high.shape[1:], bf16)
            turned_low[1] = jnp.zeros(turned_low.shape[1:], bf16)

        new = jnp.concatenate([ref[...] for ref in new_refs], axis=0)
        new_high, new_low = halves(new)
        for part, values in zip(range(2), (new_high, new_low)):
            held[part][...] = jnp.zeros((order, width), bf16) if start else state_refs[part][...]
            for place in range(count):
                row = pl.multiple_of(owner_ref[place] * rows, 16)
                held[part][pl.ds(row, rows), :] = values[place * rows : (place + 1) * rows, :]
        image = dot_halves((rows_high[...], rows_low[...]), (held[0][...], held[1][...]))
        if last:
            panel_out[:, pl.ds(node, 1), :] = -image[fresh:, :].reshape(rows, 1, width)
            image = image[:fresh, :]
        image_high, image_low = halves(image)
        slot = lax.rem(node, 2)
        turned = jnp.concatenate([new, image], axis=0).T
        turned_high[slot], turned_low[slot] = halves(turned)
        left = tuple(ref[...].reshape(2 * width, 2 * fresh) for ref in (turned_high, turned_low))
        right = (
            jnp.concatenate([image_high, new_high], axis=0),
            jnp.concatenate([image_low, new_low], axis=0),
        )
        total[...] = dot_halves(left, right).reshape(2, width, width)
        diagonals_out[0] = diagonals_ref[0] + total[slot]
        parents_out[0] = parents_ref[0] + total[1 - slot]

    column = lambda height: pl.BlockSpec((height, width), lambda node: (0, node))
    below = pl.BlockSpec((1, width, width), lambda node: (jnp.maximum(node - 1, 0), 0, 0))
    own = pl.BlockSpec((1, width, width), lambda node: (node, 0, 0))
    any_place = pl.BlockSpec(memory_space=pl.ANY)
    in_specs = [pl.BlockSpec(memory_space=pltpu.SMEM)] + [column(rows)] * count + [any_place]
    operands = [owners, *arrays, ancestor]
    if not start:
        in_specs += [column(order)] * 2
        operands += list(state)
    aliases = {len(operands): 0, len(operands) + 1: 1}
    in_specs += [below, own]
    operands += [parents, diagonals]
    out_specs = [below, own]
    out_shape = [
        jax.ShapeDtypeStruct(parents.shape, jnp.float32),
        jax.ShapeDtypeStruct(diagonals.shape, jnp.float32),
    ]
    scratch = []
    if last:
        out_specs.append(pl.BlockSpec((rows, nodes, width), lambda node: (0, 0, 0)))
        out_shape.append(jax.ShapeDtypeStruct((rows, nodes, width), jnp.float32))
        scratch += [pltpu.VMEM((order, width), bf16)] * 2
    else:
        out_specs += [column(order)] * 2
        out_shape += [jax.ShapeDtypeStruct((order, nodes * width), bf16)] * 2
    scratch += [
        pltpu.VMEM((taken * rows, order), jnp.float32),
        pltpu.VMEM((taken * rows, order), bf16),
        pltpu.VMEM((taken * rows, order), bf16),
        pltpu.VMEM((2, width, 2 * fresh), bf16),
        pltpu.VMEM((2, width, 2 * fresh), bf16),
        pltpu.VMEM((2, width, width), jnp.float32),
        pltpu.SemaphoreType.DMA((taken,)),
    ]

    def ordered(owner_ref, *refs):
        refs = list(refs)
        inputs = len(operands) - 1
        outputs = refs[inputs : inputs + len(out_shape)]
        rest = refs[inputs + len(out_shape) :]
        if last:
            outputs = outputs[:2] + rest[:2] + outputs[2:]
            rest = rest[2:]
        kernel(owner_ref, *refs[:inputs], *outputs, *rest)

    flops = 6 * nodes * (taken * rows * order * width + 4 * fresh * width * width)
    moved = 16 * diagonals.size + 8 * order * nodes * width
    parents, diagonals, *others = pl.pallas_call(
        ordered,
        grid=(nodes,),
        out_shape=out_shape,
        in_specs=in_specs,
        out_specs=out_specs,
        scratch_shapes=scratch,
        input_output_aliases=aliases,
        name="border_" + str(count),
        **kernel_params(flops, moved),
    )(*operands)
    return parents, diagonals, others


def ring(message, my_index, count):
    core = my_index % 2
    place = ring_place(my_index // 2, count)

    def pair(shift, mine):
        chip = ring_chip((place + shift + count) % count, count)
        return [(2 * chip + core, mine), (2 * chip + 1 - core, swap_bit(mine, 0))]

    ahead, behind = ring_pairs(count, 1), ring_pairs(count, -1)
    yield pair(0, message)
    upward = downward = message
    for step in range(1, (count + 1) // 2):
        upward = lax.ppermute(upward, "row", ahead)
        downward = lax.ppermute(downward, "row", behind)
        yield pair(-step, upward) + pair(step, downward)
    if count % 2 == 0:
        pairs = [p for p in ahead if p[0] % 2 == 0] + [p for p in behind if p[0] % 2 == 1]
        yield pair(count // 2, lax.ppermute(jnp.where(core == 0, upward, downward), "row", pairs))


def gather_plan(anc_blocks, anc_links, parent_links, pivot_inverse, pattern):
    my_index = lax.axis_index("row")
    chips = lax.axis_size("row") // 2
    blocks = list(ring(transposed_block(anc_blocks[0]), my_index, chips))
    links = list(ring(link_chain(anc_links, parent_links, pattern), my_index, chips))
    parents, diagonals = inner_chain(parent_links, pivot_inverse)
    ancestor = assemble(sum(blocks, []))
    groups = [sum(links[:-2], []), links[-2], links[-1]]
    state = None
    for group in groups[:-1]:
        parents, diagonals, state = border(group, ancestor, state, parents, diagonals)
    parents, diagonals, panels = border(groups[-1], ancestor, state, parents, diagonals, my_index)
    return panels[0], parents, diagonals


def spread_plan(anc_blocks, anc_links, parent_links, pivot_inverse, pattern):
    my_index = lax.axis_index("row")
    total_bits = lax.axis_size("row").bit_length() - 1
    low_bits = PCOL.bit_length() - 1
    rows, nodes, width = anc_links.shape
    links = jnp.concatenate(reduced_links(masked_links(my_index, anc_links, pattern), parent_links), axis=1)
    segment = links
    for bit in range(low_bits, total_bits):
        partner = swap_bit(segment, bit)
        upper = my_index >> bit & 1
        segment = lax.dynamic_update_slice_in_dim(
            jnp.concatenate([partner, partner], 0), segment, upper * segment.shape[0], 0
        )
    image = product(anc_blocks[0], segment)
    for bit in reversed(range(low_bits)):
        half_rows = image.shape[0] // 2
        upper = my_index >> bit & 1
        retained = lax.dynamic_slice_in_dim(image, upper * half_rows, half_rows, 0)
        outgoing = lax.dynamic_slice_in_dim(image, (1 - upper) * half_rows, half_rows, 0)
        image = retained + swap_bit(outgoing, bit)
    column = lambda array, node: array[:, node * width : (node + 1) * width]
    terms = [inner_product(column(links, node), column(image, node)) for node in range(nodes)]
    terms += [inner_product(column(links, node - 1), column(image, node)) for node in range(1, nodes)]
    totals = lax.psum(jnp.stack(terms), "row")
    inner, cross = local_chain(parent_links, pivot_inverse)
    diagonals = jnp.stack(inner) + totals[:nodes]
    parents = totals[nodes:] - jnp.stack(cross)
    return -image.reshape(rows, nodes, width), parents, diagonals


def on_device(anc_blocks, anc_links, parent_links, pivot_inverse, pattern):
    size = lax.axis_size("row")
    rows, nodes, width = anc_links.shape
    whole_bytes = 4 * size * rows * (nodes * width + size * rows)
    plan = gather_plan if size == 2 * PCOL and whole_bytes <= GATHER_LIMIT else spread_plan
    return plan(anc_blocks, anc_links, parent_links, pivot_inverse, pattern)


def solution(mesh):
    return jax.shard_map(
        on_device,
        mesh=mesh,
        in_specs=(
            P(("pole", "row"), None, None),
            P(("pole", "row"), None, None),
            P("pole", None, None),
            P("pole", None, None),
            P(),
        ),
        out_specs=(P(("pole", "row"), None, None), P("pole", None, None), P("pole", None, None)),
        check_vma=False,
    )
```

```python
import jax
import jax.numpy as jnp
from jax import lax
from jax.experimental import pallas as pl
from jax.experimental.pallas import tpu as pltpu
from jax.sharding import PartitionSpec as P

PCOL = 8
TILE = 128
GATHER_LIMIT = 16 * 2**20


def product(left, right):
    return jnp.dot(left, right, precision=lax.Precision.HIGH, preferred_element_type=jnp.float32)


def inner_product(left, right):
    return lax.dot_general(
        left,
        right,
        (((0,), (0,)), ((), ())),
        precision=lax.Precision.HIGH,
        preferred_element_type=jnp.float32,
    )


def swap_bit(value, bit):
    mask = 2**bit
    return lax.ppermute(value, "row", [(i, i ^ mask) for i in range(lax.axis_size("row"))])


def ring_chips(count):
    return list(range(0, count, 2)) + list(range(count - 1, 0, -2))


def ring_pairs(count, shift):
    order = ring_chips(count)
    pairs = []
    for place, chip in enumerate(order):
        target = order[(place + shift) % count]
        pairs += [(2 * chip + core, 2 * target + core) for core in range(2)]
    return pairs


def masked_links(my_index, anc_links, pattern):
    rows_here = anc_links.shape[0]
    tile_index = (my_index * rows_here + jnp.arange(rows_here, dtype=jnp.int32)) // TILE
    row_keep = jnp.take(pattern, tile_index, axis=1) != 0
    return jnp.where(row_keep[:, :, None], jnp.swapaxes(anc_links, 0, 1), 0.0)


def reduced_links(links, parent_links):
    reduced = [links[0]]
    for node in range(1, links.shape[0]):
        reduced.append(links[node] - product(reduced[-1], parent_links[node - 1]))
    return reduced


def local_chain(parent_links, pivot_inverse):
    inner = [pivot_inverse[0]]
    cross = []
    for node in range(1, pivot_inverse.shape[0]):
        link = parent_links[node - 1]
        cross.append(product(inner[-1], link))
        inner.append(pivot_inverse[node] + inner_product(link, cross[-1]))
    return inner, cross


def halves(value):
    high = value.astype(jnp.bfloat16)
    return high, (value - high.astype(jnp.float32)).astype(jnp.bfloat16)


def dot_halves(left, right, dims=((1,), (0,))):
    def one(a, b):
        return lax.dot_general(a, b, (dims, ((), ())), preferred_element_type=jnp.float32)

    return one(left[0], right[0]) + (one(left[0], right[1]) + one(left[1], right[0]))


def stacked_dot(left, right):
    height = left[0].shape[0]
    both = jnp.dot(jnp.concatenate(left, axis=0), right[0], preferred_element_type=jnp.float32)
    cross = jnp.dot(left[0], right[1], preferred_element_type=jnp.float32)
    return both[:height] + (both[height:] + cross)


def kernel_call(kernel, name, flops, moved, limit=16 * 2**20, **more):
    return pl.pallas_call(
        kernel,
        name=name,
        compiler_params=pltpu.CompilerParams(vmem_limit_bytes=limit),
        cost_estimate=pl.CostEstimate(flops=flops, bytes_accessed=moved, transcendentals=0),
        **more,
    )


def in_vmem(count):
    return [pl.BlockSpec(memory_space=pltpu.VMEM)] * count


def after(value, *others):
    return lax.optimization_barrier((value, *others))[0]


def turned_block(block):
    def kernel(block_ref, out_ref):
        out_ref[...] = block_ref[...].T

    shape = (block.shape[1], block.shape[0])
    return kernel_call(
        kernel, "turn_block", block.size, 8 * block.size, out_shape=jax.ShapeDtypeStruct(shape, jnp.float32)
    )(block)


def link_chain(anc_links, parent_links, pattern):
    rows, nodes, width = anc_links.shape
    tiles = pattern.shape[1]

    def kernel(links_ref, parent_ref, pattern_ref, out_ref):
        first = lax.axis_index("row") * rows
        tile = first // TILE
        next_tile = jnp.minimum(tile + 1, tiles - 1)
        row = first + lax.broadcasted_iota(jnp.int32, (rows, width), 0)
        in_first = row < (tile + 1) * TILE
        reduced = None
        for node in range(nodes):
            keep = jnp.where(in_first, pattern_ref[node, tile], pattern_ref[node, next_tile])
            links = jnp.where(keep != 0, links_ref[:, node, :], 0.0)
            if node > 0:
                links = links - dot_halves(halves(reduced), halves(parent_ref[node - 1]))
            out_ref[:, node * width : (node + 1) * width] = links
            reduced = links

    return kernel_call(
        kernel,
        "link_chain",
        12 * rows * nodes * width * width,
        4 * parent_links.size,
        out_shape=jax.ShapeDtypeStruct((rows, nodes * width), jnp.float32),
        in_specs=in_vmem(2) + [pl.BlockSpec(memory_space=pltpu.SMEM)],
        out_specs=in_vmem(1)[0],
    )(anc_links, parent_links, pattern)


def inner_chain(parent_links, pivot_inverse):
    nodes, width, _ = pivot_inverse.shape

    def kernel(parent_ref, pivot_ref, cross_ref, inner_ref):
        inner = pivot_ref[0]
        inner_ref[0] = inner
        for node in range(1, nodes):
            link = halves(parent_ref[node - 1])
            cross = dot_halves(halves(inner), link)
            cross_ref[node - 1] = -cross
            inner = pivot_ref[node] + dot_halves(link, halves(cross), ((0,), (0,)))
            inner_ref[node] = inner

    return kernel_call(
        kernel,
        "inner_chain",
        12 * nodes * width**3,
        16 * pivot_inverse.size,
        out_shape=[
            jax.ShapeDtypeStruct(parent_links.shape, jnp.float32),
            jax.ShapeDtypeStruct(pivot_inverse.shape, jnp.float32),
        ],
        in_specs=in_vmem(2),
        out_specs=in_vmem(2),
    )(parent_links, pivot_inverse)


def ring_owner(my_index, count, shift, other):
    core = lax.rem(my_index, 2)
    chip = my_index // 2
    place = jnp.where(lax.rem(chip, 2) == 0, chip // 2, count - 1 - chip // 2)
    place = lax.rem(place + shift + count, count)
    chip = jnp.where(place < count // 2, 2 * place, 2 * (count - 1 - place) + 1)
    return 2 * chip + (1 - core if other else core)


def opening(blocks, links, parents, diagonals, chips):
    nodes, width, _ = diagonals.shape
    rows = links[0][2].shape[0]
    half_columns = blocks[0][2].shape[1]
    order, fresh = 2 * half_columns, rows * len(links)
    bf16 = jnp.bfloat16

    def kernel(*refs):
        block_refs, refs = refs[: len(blocks)], refs[len(blocks) :]
        link_refs, refs = refs[: len(links)], refs[len(links) :]
        parents_ref, diagonals_ref, parents_out, diagonals_out = refs[:4]
        ancestor, held = refs[4:6], refs[6:8]
        turned = refs[8:10]
        me = lax.axis_index("row")
        for (shift, other, _), ref in zip(blocks, block_refs):
            owner = ring_owner(me, chips, shift, other)
            place = pl.multiple_of(owner // PCOL * half_columns, 128)
            parts = halves(ref[...])
            for piece in range(2):
                row = pl.multiple_of((lax.rem(owner, PCOL) + PCOL * piece) * rows, 16)
                for whole, part in zip(ancestor, parts):
                    whole[pl.ds(row, rows), pl.ds(place, half_columns)] = part[piece * rows : (piece + 1) * rows]
        starts = [pl.multiple_of(ring_owner(me, chips, s, o) * rows, 16) for s, o, _ in links]
        for whole in held:
            whole[...] = jnp.zeros(whole.shape, bf16)
        for start, ref in zip(starts, link_refs):
            for whole, part in zip(held, halves(ref[...])):
                whole[pl.ds(start, rows), :] = part
        left = [jnp.concatenate([whole[pl.ds(start, rows), :] for start in starts]) for whole in ancestor]
        for node in range(nodes):
            columns = slice(node * width, (node + 1) * width)
            new = jnp.concatenate([ref[:, columns] for ref in link_refs], axis=0).T
            for whole, part in zip(turned, halves(new)):
                whole[columns, :] = part
        for node in range(nodes):
            columns = slice(node * width, (node + 1) * width)
            image = halves(stacked_dot(left, [whole[:, columns] for whole in held]))
            lower = max(node - 1, 0) * width
            total = stacked_dot([whole[lower : (node + 1) * width, :] for whole in turned], image)
            diagonals_out[node] = diagonals_ref[node] + total[-width:]
            if node > 0:
                parents_out[node - 1] = parents_ref[node - 1] + total[:width]

    operands = [array for _, _, array in blocks + links] + [parents, diagonals]
    results = kernel_call(
        kernel,
        "opening",
        6 * nodes * fresh * width * (order + 2 * width),
        4 * sum(array.size for array in operands),
        out_shape=[jax.ShapeDtypeStruct(array.shape, jnp.float32) for array in (parents, diagonals)]
        + [jax.ShapeDtypeStruct((order, order), bf16)] * 2
        + [jax.ShapeDtypeStruct((order, nodes * width), bf16)] * 2,
        in_specs=in_vmem(len(operands)),
        out_specs=in_vmem(6),
        scratch_shapes=[pltpu.VMEM((nodes * width, fresh), bf16)] * 2,
    )(*operands)
    return results[:2], results[2:4], results[4:]


def border(links, ancestor, held, parents, diagonals, chips, last):
    nodes, width, _ = diagonals.shape
    rows = links[0][2].shape[0]
    order, fresh = ancestor[0].shape[0], rows * len(links)
    bf16 = jnp.bfloat16

    def kernel(*refs):
        link_refs, refs = refs[: len(links)], refs[len(links) :]
        whole_ancestor, held_before = refs[:2], refs[2:4]
        parents_ref, diagonals_ref, parents_out, diagonals_out = refs[4:8]
        copies = []

        def finish(place, source, target):
            if last:
                copies.append(pltpu.make_async_copy(source, target, sems.at[place]))
                copies[-1].start()

        if last:
            panel_out, refs = refs[8], refs[9:]
            parents_end, diagonals_end, panel_end = parents_out, diagonals_out, panel_out
            parents_out, diagonals_out, panel_out, sems = refs[4:8]
        else:
            refs = refs[8:]
            parents_end, diagonals_end = parents_out, diagonals_out
        held, turned = refs[:2], refs[2:4]
        me = lax.axis_index("row")
        owners = [ring_owner(me, chips, shift, other) for shift, other, _ in links]
        starts = [pl.multiple_of(owner * rows, 16) for owner in owners]
        for whole, before in zip(held, held_before):
            whole[...] = before[...]
        for start, ref in zip(starts, link_refs):
            for whole, part in zip(held, halves(ref[...])):
                whole[pl.ds(start, rows), :] = part
        piece = lax.broadcasted_iota(jnp.int32, (1, order), 1) // rows
        weight = jnp.ones((1, order), jnp.float32)
        for owner in owners:
            weight = jnp.where(piece == owner, 0.5, weight)
        weight = weight.astype(bf16)
        left = [
            jnp.concatenate([whole[pl.ds(start, rows), :] for start in starts], axis=0) * weight
            for whole in whole_ancestor
        ]
        if last:
            own = pl.multiple_of(me * rows, 16)
            left = [
                jnp.concatenate([part, whole[pl.ds(own, rows), :]], axis=0)
                for part, whole in zip(left, whole_ancestor)
            ]
        right = []
        for node in range(nodes):
            columns = slice(node * width, (node + 1) * width)
            image = stacked_dot(left, [whole[:, columns] for whole in held])
            if last:
                panel_out[:, node, :] = -image[fresh:]
            image = image[:fresh]
            new = jnp.concatenate([ref[:, columns] for ref in link_refs], axis=0)
            for whole, part in zip(turned, halves(jnp.concatenate([new, image], axis=0).T)):
                whole[columns, :] = part
            right.append([jnp.concatenate(pair, axis=0) for pair in zip(halves(image), halves(new))])
        if last:
            finish(2 * nodes, panel_out, panel_end)
        for node in range(nodes):
            lower = max(node - 1, 0) * width
            total = stacked_dot([whole[lower : (node + 1) * width, :] for whole in turned], right[node])
            diagonals_out[node] = diagonals_ref[node] + total[-width:]
            finish(node, diagonals_out.at[node], diagonals_end.at[node])
            if node > 0:
                parents_out[node - 1] = parents_ref[node - 1] + total[:width]
                finish(nodes + node, parents_out.at[node - 1], parents_end.at[node - 1])
        for copy in copies:
            copy.wait()

    operands = [array for _, _, array in links] + [*ancestor, *held, parents, diagonals]
    count = len(links)
    shapes = [jax.ShapeDtypeStruct(array.shape, jnp.float32) for array in (parents, diagonals)]
    scratch = [pltpu.VMEM((nodes * width, 2 * fresh), bf16)] * 2
    if last:
        shapes.append(jax.ShapeDtypeStruct((rows, nodes, width), jnp.float32))
        scratch = [pltpu.VMEM(array.shape, bf16) for array in held] + scratch
        scratch += [pltpu.VMEM(array.shape, jnp.float32) for array in shapes]
        scratch.append(pltpu.SemaphoreType.DMA((2 * nodes + 1,)))
    else:
        shapes += [jax.ShapeDtypeStruct(array.shape, bf16) for array in held]
    results = kernel_call(
        kernel,
        "border_" + str(count),
        6 * nodes * fresh * width * (order + 4 * width),
        4 * sum(array.size for array in operands),
        out_shape=shapes,
        in_specs=in_vmem(len(operands)),
        out_specs=[pl.BlockSpec(memory_space=pl.ANY)] * len(shapes) if last else in_vmem(len(shapes)),
        scratch_shapes=scratch,
        limit=24 * 2**20,
    )(*operands)
    return results[:2], results[2:]


def gather_plan(anc_blocks, anc_links, parent_links, pivot_inverse, pattern):
    my_index = lax.axis_index("row")
    chips = lax.axis_size("row") // 2
    ahead, behind = ring_pairs(chips, 1), ring_pairs(chips, -1)
    across = [p for p in ahead if p[0] % 2 == 0] + [p for p in behind if p[0] % 2 == 1]
    far = chips // 2

    def move(pair):
        return [lax.ppermute(value, "row", way) for value, way in zip(pair, (ahead, behind))]

    def turn(pair):
        return lax.ppermute(jnp.where(my_index % 2 == 0, *pair), "row", across)

    def both(shift, value):
        return [(shift, False, value), (shift, True, swap_bit(value, 0))]

    def sides(step, pair):
        return both(-step, pair[0]) + both(step, pair[1])

    blocks = [turned_block(anc_blocks[0])]
    blocks.append(move(blocks * 2))
    links = [link_chain(after(anc_links, blocks[0]), parent_links, pattern)]
    links.append(move(links * 2))
    totals = inner_chain(after(parent_links, links[0]), pivot_inverse)
    blocks[1] = list(lax.optimization_barrier((*blocks[1], *totals))[:2])
    for step in range(2, far):
        blocks.append(move(blocks[-1]))
        links.append(move(links[-1]))
    blocks.append(turn(blocks[-1]))
    links.append(turn(links[-1]))

    parts = both(0, blocks[0]) + both(far, blocks[-1])
    for step in range(1, far):
        parts += sides(step, blocks[step])
    first = both(0, links[0])
    for step in range(1, far - 1):
        first += sides(step, links[step])
    totals, ancestor, held = opening(parts, first, *totals, chips)
    totals, held = border(sides(far - 1, links[far - 1]), ancestor, held, *totals, chips, False)
    totals, panels = border(both(far, links[far]), ancestor, held, *totals, chips, True)
    return panels[0], *totals


def spread_plan(anc_blocks, anc_links, parent_links, pivot_inverse, pattern):
    my_index = lax.axis_index("row")
    total_bits = lax.axis_size("row").bit_length() - 1
    low_bits = PCOL.bit_length() - 1
    rows, nodes, width = anc_links.shape
    links = jnp.concatenate(reduced_links(masked_links(my_index, anc_links, pattern), parent_links), axis=1)
    segment = links
    for bit in range(low_bits, total_bits):
        partner = swap_bit(segment, bit)
        upper = my_index >> bit & 1
        segment = lax.dynamic_update_slice_in_dim(
            jnp.concatenate([partner, partner], 0), segment, upper * segment.shape[0], 0
        )
    image = product(anc_blocks[0], segment)
    for bit in reversed(range(low_bits)):
        half_rows = image.shape[0] // 2
        upper = my_index >> bit & 1
        retained = lax.dynamic_slice_in_dim(image, upper * half_rows, half_rows, 0)
        outgoing = lax.dynamic_slice_in_dim(image, (1 - upper) * half_rows, half_rows, 0)
        image = retained + swap_bit(outgoing, bit)
    column = lambda array, node: array[:, node * width : (node + 1) * width]
    terms = [inner_product(column(links, node), column(image, node)) for node in range(nodes)]
    terms += [inner_product(column(links, node - 1), column(image, node)) for node in range(1, nodes)]
    totals = lax.psum(jnp.stack(terms), "row")
    inner, cross = local_chain(parent_links, pivot_inverse)
    diagonals = jnp.stack(inner) + totals[:nodes]
    parents = totals[nodes:] - jnp.stack(cross)
    return -image.reshape(rows, nodes, width), parents, diagonals


def on_device(anc_blocks, anc_links, parent_links, pivot_inverse, pattern):
    size = lax.axis_size("row")
    rows, nodes, width = anc_links.shape
    whole_bytes = 4 * size * rows * (nodes * width + size * rows)
    plan = gather_plan if size == 2 * PCOL and whole_bytes <= GATHER_LIMIT else spread_plan
    return plan(anc_blocks, anc_links, parent_links, pivot_inverse, pattern)


def solution(mesh):
    return jax.shard_map(
        on_device,
        mesh=mesh,
        in_specs=(
            P(("pole", "row"), None, None),
            P(("pole", "row"), None, None),
            P("pole", None, None),
            P("pole", None, None),
            P(),
        ),
        out_specs=(P(("pole", "row"), None, None), P("pole", None, None), P("pole", None, None)),
        check_vma=False,
    )
```

```python
import jax
import jax.numpy as jnp
from jax import lax
from jax.experimental import pallas as pl
from jax.experimental.pallas import tpu as pltpu
from jax.sharding import PartitionSpec as P

PCOL = 8
TILE = 128
LEAD = 2
GATHER_LIMIT = 16 * 2**20


def product(left, right):
    return jnp.dot(left, right, precision=lax.Precision.HIGH, preferred_element_type=jnp.float32)


def inner_product(left, right):
    return lax.dot_general(
        left,
        right,
        (((0,), (0,)), ((), ())),
        precision=lax.Precision.HIGH,
        preferred_element_type=jnp.float32,
    )


def swap_bit(value, bit):
    mask = 2**bit
    return lax.ppermute(value, "row", [(i, i ^ mask) for i in range(lax.axis_size("row"))])


def ring_chips(count):
    return list(range(0, count, 2)) + list(range(count - 1, 0, -2))


def ring_pairs(count, shift):
    order = ring_chips(count)
    pairs = []
    for place, chip in enumerate(order):
        target = order[(place + shift) % count]
        pairs += [(2 * chip + core, 2 * target + core) for core in range(2)]
    return pairs


def masked_links(my_index, anc_links, pattern):
    rows_here = anc_links.shape[0]
    tile_index = (my_index * rows_here + jnp.arange(rows_here, dtype=jnp.int32)) // TILE
    row_keep = jnp.take(pattern, tile_index, axis=1) != 0
    return jnp.where(row_keep[:, :, None], jnp.swapaxes(anc_links, 0, 1), 0.0)


def reduced_links(links, parent_links):
    reduced = [links[0]]
    for node in range(1, links.shape[0]):
        reduced.append(links[node] - product(reduced[-1], parent_links[node - 1]))
    return reduced


def local_chain(parent_links, pivot_inverse):
    inner = [pivot_inverse[0]]
    cross = []
    for node in range(1, pivot_inverse.shape[0]):
        link = parent_links[node - 1]
        cross.append(product(inner[-1], link))
        inner.append(pivot_inverse[node] + inner_product(link, cross[-1]))
    return inner, cross


def halves(value):
    high = value.astype(jnp.bfloat16)
    return high, (value - high.astype(jnp.float32)).astype(jnp.bfloat16)


def dot_halves(left, right, dims=((1,), (0,))):
    def one(a, b):
        return lax.dot_general(a, b, (dims, ((), ())), preferred_element_type=jnp.float32)

    return one(left[0], right[0]) + (one(left[0], right[1]) + one(left[1], right[0]))


def stacked_dot(left, right):
    height = left[0].shape[0]
    both = jnp.dot(jnp.concatenate(left, axis=0), right[0], preferred_element_type=jnp.float32)
    cross = jnp.dot(left[0], right[1], preferred_element_type=jnp.float32)
    return both[:height] + (both[height:] + cross)


def kernel_call(kernel, name, flops, moved, limit=16 * 2**20, **more):
    return pl.pallas_call(
        kernel,
        name=name,
        compiler_params=pltpu.CompilerParams(vmem_limit_bytes=limit),
        cost_estimate=pl.CostEstimate(flops=flops, bytes_accessed=moved, transcendentals=0),
        **more,
    )


def in_vmem(count):
    return [pl.BlockSpec(memory_space=pltpu.VMEM)] * count


def after(value, *others):
    return lax.optimization_barrier((value, *others))[0]


def at_home(count):
    return [pl.BlockSpec(memory_space=pltpu.HBM)] * count


def turned_rows(block):
    columns, both = block.shape
    rows = both // 2

    def kernel(block_ref, mine_ref, theirs_ref, here, sem):
        fetch = pltpu.make_async_copy(block_ref, here, sem)
        fetch.start()
        fetch.wait()
        turned = here[...].T
        low = lax.axis_index("row") < PCOL
        mine_ref[...] = jnp.where(low, turned[:rows], turned[rows:])
        theirs_ref[...] = jnp.where(low, turned[rows:], turned[:rows])

    return kernel_call(
        kernel,
        "turned_rows",
        block.size,
        8 * block.size,
        limit=63 * 2**20,
        out_shape=[jax.ShapeDtypeStruct((rows, columns), jnp.float32)] * 2,
        in_specs=at_home(1),
        out_specs=in_vmem(2),
        scratch_shapes=[pltpu.VMEM(block.shape, jnp.float32), pltpu.SemaphoreType.DMA],
    )(block)


def link_chain(anc_links, parent_links, pattern):
    rows, nodes, width = anc_links.shape
    tiles = pattern.shape[1]

    def kernel(links_home, parent_home, pattern_ref, first_ref, rest_ref, links_ref, parent_ref, sems):
        fetches = [pltpu.make_async_copy(links_home, links_ref, sems.at[0])]
        for node in range(1, nodes):
            fetches.append(
                pltpu.make_async_copy(parent_home.at[node - 1], parent_ref.at[node - 1], sems.at[node])
            )
        for fetch in fetches:
            fetch.start()
        first = lax.axis_index("row") * rows
        tile = first // TILE
        next_tile = jnp.minimum(tile + 1, tiles - 1)
        row = first + lax.broadcasted_iota(jnp.int32, (rows, width), 0)
        in_first = row < (tile + 1) * TILE
        reduced = None
        for node in range(nodes):
            fetches[node].wait()
            keep = jnp.where(in_first, pattern_ref[node, tile], pattern_ref[node, next_tile])
            links = jnp.where(keep != 0, links_ref[:, node, :], 0.0)
            if node > 0:
                links = links - dot_halves(halves(reduced), halves(parent_ref[node - 1]))
            target, place = (first_ref, node) if node < LEAD else (rest_ref, node - LEAD)
            target[:, place * width : (place + 1) * width] = links
            reduced = links

    return kernel_call(
        kernel,
        "link_chain",
        12 * rows * nodes * width * width,
        4 * parent_links.size,
        limit=63 * 2**20,
        out_shape=[
            jax.ShapeDtypeStruct((rows, LEAD * width), jnp.float32),
            jax.ShapeDtypeStruct((rows, (nodes - LEAD) * width), jnp.float32),
        ],
        in_specs=at_home(2) + [pl.BlockSpec(memory_space=pltpu.SMEM)],
        out_specs=in_vmem(2),
        scratch_shapes=[
            pltpu.VMEM(anc_links.shape, jnp.float32),
            pltpu.VMEM(parent_links.shape, jnp.float32),
            pltpu.SemaphoreType.DMA((nodes,)),
        ],
    )(anc_links, parent_links, pattern)


def lead_message(mine, theirs, first):
    rows, columns = mine.shape

    def kernel(mine_ref, theirs_ref, first_ref, out_ref):
        low = lax.axis_index("row") < PCOL
        out_ref[:, :columns] = jnp.where(low, mine_ref[...], theirs_ref[...])
        out_ref[:, columns : 2 * columns] = jnp.where(low, theirs_ref[...], mine_ref[...])
        out_ref[:, 2 * columns :] = first_ref[...]

    return kernel_call(
        kernel,
        "lead_message",
        mine.size,
        8 * (mine.size + theirs.size + first.size),
        out_shape=jax.ShapeDtypeStruct((rows, 2 * columns + first.shape[1]), jnp.float32),
        in_specs=in_vmem(3),
        out_specs=in_vmem(1)[0],
    )(mine, theirs, first)


def inner_chain(parent_links, pivot_inverse):
    nodes, width, _ = pivot_inverse.shape

    def kernel(parent_home, pivot_home, cross_ref, inner_ref, parent_ref, pivot_ref, sems):
        fetches = [pltpu.make_async_copy(pivot_home.at[0], pivot_ref.at[0], sems.at[0, 0])]
        for node in range(1, nodes):
            for place, home, here, piece in (
                (1, parent_home, parent_ref, node - 1),
                (0, pivot_home, pivot_ref, node),
            ):
                fetches.append(pltpu.make_async_copy(home.at[piece], here.at[piece], sems.at[place, node]))
        for fetch in fetches:
            fetch.start()
        fetches[0].wait()
        inner = pivot_ref[0]
        inner_ref[0] = inner
        for node in range(1, nodes):
            fetches[2 * node - 1].wait()
            link = halves(parent_ref[node - 1])
            cross = dot_halves(halves(inner), link)
            cross_ref[node - 1] = -cross
            fetches[2 * node].wait()
            inner = pivot_ref[node] + dot_halves(link, halves(cross), ((0,), (0,)))
            inner_ref[node] = inner

    shapes = [jax.ShapeDtypeStruct(array.shape, jnp.float32) for array in (parent_links, pivot_inverse)]
    return kernel_call(
        kernel,
        "inner_chain",
        12 * nodes * width**3,
        16 * pivot_inverse.size,
        out_shape=shapes,
        in_specs=at_home(2),
        out_specs=in_vmem(2),
        scratch_shapes=[pltpu.VMEM(shape.shape, jnp.float32) for shape in shapes]
        + [pltpu.SemaphoreType.DMA((2, nodes))],
    )(parent_links, pivot_inverse)


def ring_owner(my_index, count, shift, other):
    core = lax.rem(my_index, 2)
    chip = my_index // 2
    place = jnp.where(lax.rem(chip, 2) == 0, chip // 2, count - 1 - chip // 2)
    place = lax.rem(place + shift + count, count)
    chip = jnp.where(place < count // 2, 2 * place, 2 * (count - 1 - place) + 1)
    return 2 * chip + (1 - core if other else core)


def border(arrivals, held, parents, diagonals, chips, last=False):
    nodes, width, _ = diagonals.shape
    rows = arrivals[0][2].shape[0]
    order = arrivals[0][2].shape[1] - LEAD * width
    count = len(arrivals)
    fresh = rows * count
    bf16 = jnp.bfloat16

    def kernel(*refs):
        refs = list(refs)
        take = lambda number: [refs.pop(0) for _ in range(number)]
        lead_refs, rest_refs = take(count), take(count)
        own_ref = take(1)[0] if last else None
        held_before = take(2) if held else None
        parents_ref, diagonals_ref, parents_out, diagonals_out = take(4)
        copies = []

        def finish(place, source, target):
            if last:
                copies.append(pltpu.make_async_copy(source, target, sems.at[place]))
                copies[-1].start()

        parents_end, diagonals_end = parents_out, diagonals_out
        if last:
            (panel_end,) = take(1)
        held_now = take(2)
        turned = take(2)
        if last:
            parents_out, diagonals_out, panel_out, sems = take(4)
        me = lax.axis_index("row")
        owners = [ring_owner(me, chips, shift, other) for shift, other, _, _ in arrivals]

        for part, whole in enumerate(held_now):
            whole[...] = held_before[part][...] if held else jnp.zeros(whole.shape, bf16)
        for owner, lead, rest in zip(owners, lead_refs, rest_refs):
            start = pl.multiple_of(owner * rows, 16)
            for whole, part in zip(held_now, halves(lead[:, order:])):
                whole[pl.ds(start, rows), : LEAD * width] = part
            for whole, part in zip(held_now, halves(rest[...])):
                whole[pl.ds(start, rows), LEAD * width :] = part
        piece = lax.broadcasted_iota(jnp.int32, (1, order), 1) // rows
        weight = jnp.ones((1, order), jnp.float32)
        for owner in owners:
            weight = jnp.where(piece == owner, 0.5, weight)
        left = [ref[:, :order] * weight for ref in lead_refs]
        if last:
            left.append(own_ref[:, :order])
        left = halves(jnp.concatenate(left, axis=0))
        right = []
        for node in range(nodes):
            columns = slice(node * width, (node + 1) * width)
            image = stacked_dot(left, [whole[:, columns] for whole in held_now])
            if last:
                panel_out[:, node, :] = -image[fresh:]
            image = image[:fresh]
            if node < LEAD:
                new = [ref[:, order + node * width : order + (node + 1) * width] for ref in lead_refs]
            else:
                new = [ref[:, (node - LEAD) * width : (node - LEAD + 1) * width] for ref in rest_refs]
            new = jnp.concatenate(new, axis=0)
            for whole, part in zip(turned, halves(jnp.concatenate([new, image], axis=0).T)):
                whole[columns, :] = part
            right.append([jnp.concatenate(pair, axis=0) for pair in zip(halves(image), halves(new))])
        if last:
            finish(2 * nodes, panel_out, panel_end)
        for node in range(nodes):
            lower = max(node - 1, 0) * width
            total = stacked_dot([whole[lower : (node + 1) * width, :] for whole in turned], right[node])
            diagonals_out[node] = diagonals_ref[node] + total[-width:]
            finish(node, diagonals_out.at[node], diagonals_end.at[node])
            if node > 0:
                parents_out[node - 1] = parents_ref[node - 1] + total[:width]
                finish(nodes + node, parents_out.at[node - 1], parents_end.at[node - 1])
        for copy in copies:
            copy.wait()

    operands = [lead for _, _, lead, _ in arrivals] + [rest for _, _, _, rest in arrivals]
    operands += [last] if last is not False else []
    operands += [*(held or []), parents, diagonals]
    last = last is not False
    state = [(order, nodes * width)] * 2
    shapes = [jax.ShapeDtypeStruct(array.shape, jnp.float32) for array in (parents, diagonals)]
    scratch = [pltpu.VMEM((nodes * width, 2 * fresh), bf16)] * 2
    if last:
        shapes.append(jax.ShapeDtypeStruct((rows, nodes, width), jnp.float32))
        scratch = [pltpu.VMEM(shape, bf16) for shape in state] + scratch
        scratch += [pltpu.VMEM(array.shape, jnp.float32) for array in shapes]
        scratch.append(pltpu.SemaphoreType.DMA((2 * nodes + 1,)))
    else:
        shapes += [jax.ShapeDtypeStruct(shape, bf16) for shape in state]
    results = kernel_call(
        kernel,
        "border" + ("_end" if last else "" if held else "_start"),
        6 * nodes * fresh * width * (order + 4 * width),
        4 * sum(array.size for array in operands),
        out_shape=shapes,
        in_specs=in_vmem(len(operands)),
        out_specs=at_home(len(shapes)) if last else in_vmem(len(shapes)),
        scratch_shapes=scratch,
        limit=24 * 2**20 if last else 16 * 2**20,
    )(*operands)
    return results[:2], results[2:]


def gather_plan(anc_blocks, anc_links, parent_links, pivot_inverse, pattern):
    my_index = lax.axis_index("row")
    chips = lax.axis_size("row") // 2
    far = chips // 2
    ahead, behind = ring_pairs(chips, 1), ring_pairs(chips, -1)
    across = [p for p in ahead if p[0] % 2 == 0] + [p for p in behind if p[0] % 2 == 1]

    def move(pair):
        return [lax.ppermute(value, "row", way) for value, way in zip(pair, (ahead, behind))]

    def turn(pair):
        return lax.ppermute(jnp.where(my_index % 2 == 0, *pair), "row", across)

    def both(shift, lead, rest):
        return [(shift, False, lead, rest), (shift, True, swap_bit(lead, 0), swap_bit(rest, 0))]

    mine, theirs = turned_rows(anc_blocks[0])
    theirs = swap_bit(theirs, PCOL.bit_length() - 1)
    first, rest = link_chain(after(anc_links, mine), parent_links, pattern)
    lead = lead_message(mine, theirs, first)
    totals = inner_chain(after(parent_links, lead), pivot_inverse)
    leads, rests = [lead] * 2, [rest] * 2
    arrivals, held = both(0, lead, rest), None
    for step in range(1, far):
        leads, totals = lax.optimization_barrier((move(leads), totals))
        totals, held = border(arrivals, held, *totals, chips)
        rests, totals = lax.optimization_barrier((move(rests), totals))
        arrivals = both(-step, leads[0], rests[0]) + both(step, leads[1], rests[1])
    totals, held = border(arrivals, held, *totals, chips)
    totals, panels = border(both(far, turn(leads), turn(rests)), held, *totals, chips, last=lead)
    return panels[0], *totals


def spread_plan(anc_blocks, anc_links, parent_links, pivot_inverse, pattern):
    my_index = lax.axis_index("row")
    total_bits = lax.axis_size("row").bit_length() - 1
    low_bits = PCOL.bit_length() - 1
    rows, nodes, width = anc_links.shape
    links = jnp.concatenate(reduced_links(masked_links(my_index, anc_links, pattern), parent_links), axis=1)
    segment = links
    for bit in range(low_bits, total_bits):
        partner = swap_bit(segment, bit)
        upper = my_index >> bit & 1
        segment = lax.dynamic_update_slice_in_dim(
            jnp.concatenate([partner, partner], 0), segment, upper * segment.shape[0], 0
        )
    image = product(anc_blocks[0], segment)
    for bit in reversed(range(low_bits)):
        half_rows = image.shape[0] // 2
        upper = my_index >> bit & 1
        retained = lax.dynamic_slice_in_dim(image, upper * half_rows, half_rows, 0)
        outgoing = lax.dynamic_slice_in_dim(image, (1 - upper) * half_rows, half_rows, 0)
        image = retained + swap_bit(outgoing, bit)
    column = lambda array, node: array[:, node * width : (node + 1) * width]
    terms = [inner_product(column(links, node), column(image, node)) for node in range(nodes)]
    terms += [inner_product(column(links, node - 1), column(image, node)) for node in range(1, nodes)]
    totals = lax.psum(jnp.stack(terms), "row")
    inner, cross = local_chain(parent_links, pivot_inverse)
    diagonals = jnp.stack(inner) + totals[:nodes]
    parents = totals[nodes:] - jnp.stack(cross)
    return -image.reshape(rows, nodes, width), parents, diagonals


def on_device(anc_blocks, anc_links, parent_links, pivot_inverse, pattern):
    size = lax.axis_size("row")
    rows, nodes, width = anc_links.shape
    whole_bytes = 4 * size * rows * (nodes * width + size * rows)
    plan = gather_plan if size == 2 * PCOL and whole_bytes <= GATHER_LIMIT else spread_plan
    return plan(anc_blocks, anc_links, parent_links, pivot_inverse, pattern)


def solution(mesh):
    return jax.shard_map(
        on_device,
        mesh=mesh,
        in_specs=(
            P(("pole", "row"), None, None),
            P(("pole", "row"), None, None),
            P("pole", None, None),
            P("pole", None, None),
            P(),
        ),
        out_specs=(P(("pole", "row"), None, None), P("pole", None, None), P("pole", None, None)),
        check_vma=False,
    )
```

```python
import jax
import jax.numpy as jnp
from jax import lax
from jax.experimental import pallas as pl
from jax.experimental.pallas import tpu as pltpu
from jax.sharding import PartitionSpec as P

PCOL = 8
TILE = 128
LEAD = 2
GATHER_LIMIT = 16 * 2**20
VMEM_LIMIT = 63 * 2**20


def product(left, right):
    return jnp.dot(left, right, precision=lax.Precision.HIGH, preferred_element_type=jnp.float32)


def inner_product(left, right):
    return lax.dot_general(
        left,
        right,
        (((0,), (0,)), ((), ())),
        precision=lax.Precision.HIGH,
        preferred_element_type=jnp.float32,
    )


def swap_bit(value, bit):
    mask = 2**bit
    return lax.ppermute(value, "row", [(i, i ^ mask) for i in range(lax.axis_size("row"))])


def ring_chips(count):
    return list(range(0, count, 2)) + list(range(count - 1, 0, -2))


def ring_pairs(count, shift):
    order = ring_chips(count)
    pairs = []
    for place, chip in enumerate(order):
        target = order[(place + shift) % count]
        pairs += [(2 * chip + core, 2 * target + core) for core in range(2)]
    return pairs


def masked_links(my_index, anc_links, pattern):
    rows_here = anc_links.shape[0]
    tile_index = (my_index * rows_here + jnp.arange(rows_here, dtype=jnp.int32)) // TILE
    row_keep = jnp.take(pattern, tile_index, axis=1) != 0
    return jnp.where(row_keep[:, :, None], jnp.swapaxes(anc_links, 0, 1), 0.0)


def reduced_links(links, parent_links):
    reduced = [links[0]]
    for node in range(1, links.shape[0]):
        reduced.append(links[node] - product(reduced[-1], parent_links[node - 1]))
    return reduced


def local_chain(parent_links, pivot_inverse):
    inner = [pivot_inverse[0]]
    cross = []
    for node in range(1, pivot_inverse.shape[0]):
        link = parent_links[node - 1]
        cross.append(product(inner[-1], link))
        inner.append(pivot_inverse[node] + inner_product(link, cross[-1]))
    return inner, cross


def halves(value):
    high = value.astype(jnp.bfloat16)
    return high, (value - high.astype(jnp.float32)).astype(jnp.bfloat16)


def dot_halves(left, right, dims=((1,), (0,))):
    def one(a, b):
        return lax.dot_general(a, b, (dims, ((), ())), preferred_element_type=jnp.float32)

    return one(left[0], right[0]) + (one(left[0], right[1]) + one(left[1], right[0]))


def stacked_dot(left, right):
    height = left[0].shape[0]
    both = jnp.dot(jnp.concatenate(left, axis=0), right[0], preferred_element_type=jnp.float32)
    cross = jnp.dot(left[0], right[1], preferred_element_type=jnp.float32)
    return both[:height] + (both[height:] + cross)


def kernel_call(kernel, name, operands, out_shape, scratch, small=0, aliases=None):
    home = pl.BlockSpec(memory_space=pltpu.HBM)
    scalars = pl.BlockSpec(memory_space=pltpu.SMEM)
    return pl.pallas_call(
        kernel,
        name=name,
        out_shape=[jax.ShapeDtypeStruct(shape, dtype) for shape, dtype in out_shape],
        in_specs=[home] * (len(operands) - small) + [scalars] * small,
        out_specs=[home] * len(out_shape),
        scratch_shapes=scratch,
        input_output_aliases=aliases or {},
        compiler_params=pltpu.CompilerParams(vmem_limit_bytes=VMEM_LIMIT),
        cost_estimate=pl.CostEstimate(flops=0, bytes_accessed=0, transcendentals=0),
    )(*operands)


def after(value, *others):
    return lax.optimization_barrier((value, *others))[0]


class Copies:
    def __init__(self, sems):
        self.sems, self.running = sems, {}

    def start(self, name, source, target):
        copy = pltpu.make_async_copy(source, target, self.sems.at[len(self.running)])
        copy.start()
        self.running[name] = copy

    def wait(self, *names):
        for name in names:
            copy = self.running[name]
            if copy is not None:
                copy.wait()
            self.running[name] = None

    def finish(self):
        self.wait(*self.running)


def partner_rows(turned):
    rows, columns = turned.shape[0] // 2, turned.shape[1]

    def kernel(turned_ref, out_ref, sem):
        place = jnp.where(lax.axis_index("row") < PCOL, rows, 0)
        copy = pltpu.make_async_copy(turned_ref.at[pl.ds(pl.multiple_of(place, 8), rows), :], out_ref, sem)
        copy.start()
        copy.wait()

    shape = [((rows, columns), jnp.float32)]
    return kernel_call(kernel, "partner_rows", [turned], shape, [pltpu.SemaphoreType.DMA])[0]


def lead_message(turned, theirs, first):
    rows, columns = theirs.shape

    def kernel(turned_ref, theirs_ref, first_ref, out_ref, sems):
        half = jnp.where(lax.axis_index("row") < PCOL, 0, 1)
        copies = Copies(sems)
        own = pl.ds(pl.multiple_of(half * rows, 8), rows)
        at = lambda half: out_ref.at[:, pl.ds(pl.multiple_of(half * columns, 128), columns)]
        copies.start("own", turned_ref.at[own, :], at(half))
        copies.start("partner", theirs_ref, at(1 - half))
        copies.start("links", first_ref, out_ref.at[:, 2 * columns :])
        copies.finish()

    shape = [((rows, 2 * columns + first.shape[1]), jnp.float32)]
    scratch = [pltpu.SemaphoreType.DMA((3,))]
    return kernel_call(kernel, "lead_message", [turned, theirs, first], shape, scratch)[0]


def link_chain(anc_links, parent_links, pattern):
    rows, nodes, width = anc_links.shape
    tiles = pattern.shape[1]

    def kernel(links_home, parent_home, pattern_ref, first_home, rest_home, links_ref, parent_ref, out_ref, sems):
        copies = Copies(sems)
        copies.start(0, links_home, links_ref)
        for node in range(1, nodes):
            copies.start(node, parent_home.at[node - 1], parent_ref.at[node - 1])
        first = lax.axis_index("row") * rows
        tile = first // TILE
        next_tile = jnp.minimum(tile + 1, tiles - 1)
        row = first + lax.broadcasted_iota(jnp.int32, (rows, width), 0)
        in_first = row < (tile + 1) * TILE
        reduced = None
        for node in range(nodes):
            copies.wait(node)
            keep = jnp.where(in_first, pattern_ref[node, tile], pattern_ref[node, next_tile])
            links = jnp.where(keep != 0, links_ref[:, node, :], 0.0)
            if node > 0:
                links = links - dot_halves(halves(reduced), halves(parent_ref[node - 1]))
            here = slice(node * width, (node + 1) * width)
            out_ref[:, here] = links
            home, place = (first_home, node) if node < LEAD else (rest_home, node - LEAD)
            copies.start(("out", node), out_ref.at[:, here], home.at[:, place * width : (place + 1) * width])
            reduced = links
        copies.finish()

    shapes = [((rows, LEAD * width), jnp.float32), ((rows, (nodes - LEAD) * width), jnp.float32)]
    scratch = [
        pltpu.VMEM(anc_links.shape, jnp.float32),
        pltpu.VMEM(parent_links.shape, jnp.float32),
        pltpu.VMEM((rows, nodes * width), jnp.float32),
        pltpu.SemaphoreType.DMA((2 * nodes,)),
    ]
    return kernel_call(kernel, "link_chain", [anc_links, parent_links, pattern], shapes, scratch, small=1)


def inner_chain(parent_links, pivot_inverse):
    nodes, width, _ = pivot_inverse.shape

    def kernel(parent_home, pivot_home, cross_home, inner_home, parent_ref, pivot_ref, sems):
        copies = Copies(sems)
        copies.start(("pivot", 0), pivot_home.at[0], pivot_ref.at[0])
        for node in range(1, nodes):
            copies.start(("parent", node), parent_home.at[node - 1], parent_ref.at[node - 1])
            copies.start(("pivot", node), pivot_home.at[node], pivot_ref.at[node])
        copies.wait(("pivot", 0))
        inner = pivot_ref[0]
        copies.start(("inner", 0), pivot_ref.at[0], inner_home.at[0])
        for node in range(1, nodes):
            copies.wait(("parent", node))
            link = halves(parent_ref[node - 1])
            cross = dot_halves(halves(inner), link)
            parent_ref[node - 1] = -cross
            copies.start(("cross", node), parent_ref.at[node - 1], cross_home.at[node - 1])
            copies.wait(("pivot", node))
            inner = pivot_ref[node] + dot_halves(link, halves(cross), ((0,), (0,)))
            pivot_ref[node] = inner
            copies.start(("inner", node), pivot_ref.at[node], inner_home.at[node])
        copies.finish()

    shapes = [(array.shape, jnp.float32) for array in (parent_links, pivot_inverse)]
    scratch = [pltpu.VMEM(*shape) for shape in shapes] + [pltpu.SemaphoreType.DMA((4 * nodes,))]
    return kernel_call(kernel, "inner_chain", [parent_links, pivot_inverse], shapes, scratch)


def ring_owner(my_index, count, shift, other):
    core = lax.rem(my_index, 2)
    chip = my_index // 2
    place = jnp.where(lax.rem(chip, 2) == 0, chip // 2, count - 1 - chip // 2)
    place = lax.rem(place + shift + count, count)
    chip = jnp.where(place < count // 2, 2 * place, 2 * (count - 1 - place) + 1)
    return 2 * chip + (1 - core if other else core)


def border(arrivals, held, parents, diagonals, chips, own_lead=None):
    last, start = own_lead is not None, held is None
    nodes, width, _ = diagonals.shape
    rows = arrivals[0][2].shape[0]
    order = arrivals[0][2].shape[1] - LEAD * width
    count = len(arrivals)
    fresh = rows * count
    bf16, f32 = jnp.bfloat16, jnp.float32
    leads, rests = [lead for _, _, lead, _ in arrivals], [rest for _, _, _, rest in arrivals]

    def kernel(*refs):
        refs = list(refs)
        take = lambda number: [refs.pop(0) for _ in range(number)]
        lead_homes, rest_homes, own_home = take(count), take(count), take(last)
        held_homes = [] if start else take(2)
        parents_home, diagonals_home, parents_end, diagonals_end = take(4)
        (panel_end,) = take(1) if last else [None]
        held_ends = [] if last else take(2)
        lead_refs, rest_refs, parents_ref, diagonals_ref, *held_refs = take(6)
        *turned, panel_ref, sems = refs
        me = lax.axis_index("row")
        owners = [ring_owner(me, chips, shift, other) for shift, other, _, _ in arrivals]
        places = [pl.multiple_of(owner * rows, 16) for owner in owners]
        spans = [slice(node * width, (node + 1) * width) for node in range(nodes)]

        copies = Copies(sems)
        for place, home in enumerate(lead_homes + own_home):
            copies.start(("lead", place), home, lead_refs.at[place])
        for place, home in enumerate(rest_homes):
            copies.start(("rest", place), home, rest_refs.at[place])
        for node, span in enumerate(spans):
            for part, home in enumerate(held_homes):
                copies.start(("held", part, node), home.at[:, span], held_refs[part].at[:, span])
        for node in range(nodes):
            copies.start(("diagonal", node), diagonals_home.at[node], diagonals_ref.at[node])
            if node > 0:
                copies.start(("parent", node), parents_home.at[node - 1], parents_ref.at[node - 1])

        if start:
            for whole in held_refs:
                whole[...] = jnp.zeros(whole.shape, bf16)
        piece = lax.broadcasted_iota(jnp.int32, (1, order), 1) // rows
        weight = jnp.ones((1, order), f32)
        for owner in owners:
            weight = jnp.where(piece == owner, 0.5, weight)
        copies.wait(*[("lead", place) for place in range(count + last)])
        left = [lead_refs[place, :, :order] * weight for place in range(count)]
        if last:
            left.append(lead_refs[count, :, :order])
        left = halves(jnp.concatenate(left, axis=0))
        right = []
        for node, span in enumerate(spans):
            if node == LEAD:
                copies.wait(*[("rest", place) for place in range(count)])
            if node < LEAD:
                new = [lead_refs[place, :, order + span.start : order + span.stop] for place in range(count)]
            else:
                skip = LEAD * width
                new = [rest_refs[place, :, span.start - skip : span.stop - skip] for place in range(count)]
            new = jnp.concatenate(new, axis=0)
            new_parts = halves(new)
            for part, whole in enumerate(held_refs):
                if not start:
                    copies.wait(("held", part, node))
                for index, place in enumerate(places):
                    whole[pl.ds(place, rows), span] = new_parts[part][index * rows : (index + 1) * rows]
            image = stacked_dot(left, [whole[:, span] for whole in held_refs])
            if last:
                panel_ref[:, node, :] = -image[fresh:]
            image = image[:fresh]
            for whole, part in zip(turned, halves(jnp.concatenate([new, image], axis=0).T)):
                whole[span, :] = part
            right.append([jnp.concatenate(pair, axis=0) for pair in zip(halves(image), new_parts)])
        if last:
            copies.start("panels", panel_ref, panel_end)
        for part, home in enumerate(held_ends):
            if start:
                copies.start(("keep", part), held_refs[part], home)
            else:
                for index, place in enumerate(places):
                    there = pl.ds(place, rows)
                    copies.start(("keep", part, index), held_refs[part].at[there, :], home.at[there, :])
        for node in range(nodes):
            lower = max(node - 1, 0) * width
            total = stacked_dot([whole[lower : (node + 1) * width, :] for whole in turned], right[node])
            copies.wait(("diagonal", node))
            diagonals_ref[node] += total[-width:]
            copies.start(("diagonal out", node), diagonals_ref.at[node], diagonals_end.at[node])
            if node > 0:
                copies.wait(("parent", node))
                parents_ref[node - 1] += total[:width]
                copies.start(("parent out", node), parents_ref.at[node - 1], parents_end.at[node - 1])
        copies.finish()

    operands = leads + rests + ([own_lead] if last else []) + list(held or []) + [parents, diagonals]
    state = [((order, nodes * width), bf16)] * 2
    panels = ((rows, nodes, width), f32)
    shapes = [(parents.shape, f32), (diagonals.shape, f32)] + ([panels] if last else state)
    aliases = {len(operands) - 2: 0, len(operands) - 1: 1}
    if held and not last:
        aliases |= {len(operands) - 4: 2, len(operands) - 3: 3}
    scratch = [((count + last, *leads[0].shape), f32), ((count, *rests[0].shape), f32)]
    scratch += [(parents.shape, f32), (diagonals.shape, f32), *state]
    scratch += [((nodes * width, 2 * fresh), bf16)] * 2 + [panels if last else ((8, 128), f32)]
    sems = pltpu.SemaphoreType.DMA((3 * count + 8 * nodes + 8,))
    name = "border" + ("_end" if last else "_start" if start else "")
    scratch = [pltpu.VMEM(*shape) for shape in scratch] + [sems]
    parents, diagonals, *others = kernel_call(kernel, name, operands, shapes, scratch, aliases=aliases)
    return (parents, diagonals), others


def gather_plan(anc_blocks, anc_links, parent_links, pivot_inverse, pattern):
    my_index = lax.axis_index("row")
    chips = lax.axis_size("row") // 2
    far = chips // 2
    ahead, behind = ring_pairs(chips, 1), ring_pairs(chips, -1)
    across = [p for p in ahead if p[0] % 2 == 0] + [p for p in behind if p[0] % 2 == 1]

    def move(pair):
        return [lax.ppermute(value, "row", way) for value, way in zip(pair, (ahead, behind))]

    def turn(pair):
        return lax.ppermute(jnp.where(my_index % 2 == 0, *pair), "row", across)

    def both(shift, lead, rest):
        return [(shift, False, lead, rest), (shift, True, swap_bit(lead, 0), swap_bit(rest, 0))]

    turned = anc_blocks[0].T
    theirs = partner_rows(turned)
    first, rest = link_chain(after(anc_links, theirs), parent_links, pattern)
    lead = lead_message(turned, swap_bit(theirs, PCOL.bit_length() - 1), first)
    totals = inner_chain(after(parent_links, lead), pivot_inverse)
    leads, rests = [lead] * 2, [rest] * 2
    arrivals, held = both(0, lead, rest), None
    for step in range(1, far):
        leads, totals = lax.optimization_barrier((move(leads), totals))
        totals, held = border(arrivals, held, *totals, chips)
        rests, totals = lax.optimization_barrier((move(rests), totals))
        arrivals = both(-step, leads[0], rests[0]) + both(step, leads[1], rests[1])
    totals, held = border(arrivals, held, *totals, chips)
    totals, panels = border(both(far, turn(leads), turn(rests)), held, *totals, chips, lead)
    return panels[0], *totals


def spread_plan(anc_blocks, anc_links, parent_links, pivot_inverse, pattern):
    my_index = lax.axis_index("row")
    total_bits = lax.axis_size("row").bit_length() - 1
    low_bits = PCOL.bit_length() - 1
    rows, nodes, width = anc_links.shape
    links = jnp.concatenate(reduced_links(masked_links(my_index, anc_links, pattern), parent_links), axis=1)
    segment = links
    for bit in range(low_bits, total_bits):
        partner = swap_bit(segment, bit)
        upper = my_index >> bit & 1
        segment = lax.dynamic_update_slice_in_dim(
            jnp.concatenate([partner, partner], 0), segment, upper * segment.shape[0], 0
        )
    image = product(anc_blocks[0], segment)
    for bit in reversed(range(low_bits)):
        half_rows = image.shape[0] // 2
        upper = my_index >> bit & 1
        retained = lax.dynamic_slice_in_dim(image, upper * half_rows, half_rows, 0)
        outgoing = lax.dynamic_slice_in_dim(image, (1 - upper) * half_rows, half_rows, 0)
        image = retained + swap_bit(outgoing, bit)
    column = lambda array, node: array[:, node * width : (node + 1) * width]
    terms = [inner_product(column(links, node), column(image, node)) for node in range(nodes)]
    terms += [inner_product(column(links, node - 1), column(image, node)) for node in range(1, nodes)]
    totals = lax.psum(jnp.stack(terms), "row")
    inner, cross = local_chain(parent_links, pivot_inverse)
    diagonals = jnp.stack(inner) + totals[:nodes]
    parents = totals[nodes:] - jnp.stack(cross)
    return -image.reshape(rows, nodes, width), parents, diagonals


def on_device(anc_blocks, anc_links, parent_links, pivot_inverse, pattern):
    size = lax.axis_size("row")
    rows, nodes, width = anc_links.shape
    whole_bytes = 4 * size * rows * (nodes * width + size * rows)
    plan = gather_plan if size == 2 * PCOL and whole_bytes <= GATHER_LIMIT else spread_plan
    return plan(anc_blocks, anc_links, parent_links, pivot_inverse, pattern)


def solution(mesh):
    return jax.shard_map(
        on_device,
        mesh=mesh,
        in_specs=(
            P(("pole", "row"), None, None),
            P(("pole", "row"), None, None),
            P("pole", None, None),
            P("pole", None, None),
            P(),
        ),
        out_specs=(P(("pole", "row"), None, None), P("pole", None, None), P("pole", None, None)),
        check_vma=False,
    )
```

```python
import jax
import jax.numpy as jnp
from jax import lax
from jax.experimental import pallas as pl
from jax.experimental.pallas import tpu as pltpu
from jax.sharding import PartitionSpec as P

PCOL = 8
TILE = 128
LEAD = 2
GATHER_LIMIT = 16 * 2**20
LINK_LIMIT = 65_600_000


def product(left, right):
    return jnp.dot(left, right, precision=lax.Precision.HIGH, preferred_element_type=jnp.float32)


def inner_product(left, right):
    return lax.dot_general(
        left,
        right,
        (((0,), (0,)), ((), ())),
        precision=lax.Precision.HIGH,
        preferred_element_type=jnp.float32,
    )


def swap_bit(value, bit):
    mask = 2**bit
    return lax.ppermute(value, "row", [(i, i ^ mask) for i in range(lax.axis_size("row"))])


def ring_chips(count):
    return list(range(0, count, 2)) + list(range(count - 1, 0, -2))


def ring_pairs(count, shift):
    order = ring_chips(count)
    pairs = []
    for place, chip in enumerate(order):
        target = order[(place + shift) % count]
        pairs += [(2 * chip + core, 2 * target + core) for core in range(2)]
    return pairs


def masked_links(my_index, anc_links, pattern):
    rows_here = anc_links.shape[0]
    tile_index = (my_index * rows_here + jnp.arange(rows_here, dtype=jnp.int32)) // TILE
    row_keep = jnp.take(pattern, tile_index, axis=1) != 0
    return jnp.where(row_keep[:, :, None], jnp.swapaxes(anc_links, 0, 1), 0.0)


def reduced_links(links, parent_links):
    reduced = [links[0]]
    for node in range(1, links.shape[0]):
        reduced.append(links[node] - product(reduced[-1], parent_links[node - 1]))
    return reduced


def local_chain(parent_links, pivot_inverse):
    inner = [pivot_inverse[0]]
    cross = []
    for node in range(1, pivot_inverse.shape[0]):
        link = parent_links[node - 1]
        cross.append(product(inner[-1], link))
        inner.append(pivot_inverse[node] + inner_product(link, cross[-1]))
    return inner, cross


def halves(value):
    high = value.astype(jnp.bfloat16)
    return high, (value - high.astype(jnp.float32)).astype(jnp.bfloat16)


def dot_halves(left, right, dims=((1,), (0,))):
    def one(a, b):
        return lax.dot_general(a, b, (dims, ((), ())), preferred_element_type=jnp.float32)

    return one(left[0], right[0]) + (one(left[0], right[1]) + one(left[1], right[0]))


def stacked_dot(left, right):
    height = left[0].shape[0]
    both = jnp.dot(jnp.concatenate(left, axis=0), right[0], preferred_element_type=jnp.float32)
    cross = jnp.dot(left[0], right[1], preferred_element_type=jnp.float32)
    return both[:height] + (both[height:] + cross)


def kernel_call(kernel, name, limit=16 * 2**20, **more):
    return pl.pallas_call(
        kernel,
        name=name,
        compiler_params=pltpu.CompilerParams(vmem_limit_bytes=limit),
        cost_estimate=pl.CostEstimate(flops=0, bytes_accessed=0, transcendentals=0),
        **more,
    )


def in_vmem(count):
    return [pl.BlockSpec(memory_space=pltpu.VMEM)] * count


def after(value, *others):
    return lax.optimization_barrier((value, *others))[0]


def at_home(count):
    return [pl.BlockSpec(memory_space=pltpu.HBM)] * count


def partner_rows(turned):
    rows, columns = turned.shape[0] // 2, turned.shape[1]

    def kernel(turned_ref, out_ref):
        out_ref[...] = jnp.where(lax.axis_index("row") < PCOL, turned_ref[rows:], turned_ref[:rows])

    return kernel_call(
        kernel,
        "partner_rows",
        out_shape=jax.ShapeDtypeStruct((rows, columns), jnp.float32),
        in_specs=in_vmem(1),
        out_specs=in_vmem(1)[0],
    )(turned)


def pick(pair):
    def kernel(first_ref, second_ref, out_ref):
        out_ref[...] = jnp.where(lax.rem(lax.axis_index("row"), 2) == 0, first_ref[...], second_ref[...])

    return kernel_call(
        kernel,
        "pick",
        out_shape=jax.ShapeDtypeStruct(pair[0].shape, jnp.float32),
        in_specs=in_vmem(2),
        out_specs=in_vmem(1)[0],
    )(*pair)


def link_chain(anc_links, parent_links, pattern):
    rows, nodes, width = anc_links.shape
    tiles = pattern.shape[1]

    def kernel(links_home, parent_home, pattern_ref, first_ref, rest_ref, links_ref, parent_ref, sems):
        fetches = [pltpu.make_async_copy(links_home, links_ref, sems.at[0])]
        for node in range(1, nodes):
            fetches.append(
                pltpu.make_async_copy(parent_home.at[node - 1], parent_ref.at[node - 1], sems.at[node])
            )
        for fetch in fetches:
            fetch.start()
        first = lax.axis_index("row") * rows
        tile = first // TILE
        next_tile = jnp.minimum(tile + 1, tiles - 1)
        row = first + lax.broadcasted_iota(jnp.int32, (rows, width), 0)
        in_first = row < (tile + 1) * TILE
        reduced = None
        for node in range(nodes):
            fetches[node].wait()
            keep = jnp.where(in_first, pattern_ref[node, tile], pattern_ref[node, next_tile])
            links = jnp.where(keep != 0, links_ref[:, node, :], 0.0)
            if node > 0:
                links = links - dot_halves(halves(reduced), halves(parent_ref[node - 1]))
            target, place = (first_ref, node) if node < LEAD else (rest_ref, node - LEAD)
            target[:, place * width : (place + 1) * width] = links
            reduced = links

    return kernel_call(
        kernel,
        "link_chain",
        limit=LINK_LIMIT,
        out_shape=[
            jax.ShapeDtypeStruct((rows, LEAD * width), jnp.float32),
            jax.ShapeDtypeStruct((rows, (nodes - LEAD) * width), jnp.float32),
        ],
        in_specs=at_home(2) + [pl.BlockSpec(memory_space=pltpu.SMEM)],
        out_specs=in_vmem(2),
        scratch_shapes=[
            pltpu.VMEM(anc_links.shape, jnp.float32),
            pltpu.VMEM(parent_links.shape, jnp.float32),
            pltpu.SemaphoreType.DMA((nodes,)),
        ],
    )(anc_links, parent_links, pattern)


def lead_message(turned, theirs, first):
    rows, columns = theirs.shape

    def kernel(turned_ref, theirs_ref, first_ref, out_ref):
        low = lax.axis_index("row") < PCOL
        out_ref[:, :columns] = jnp.where(low, turned_ref[:rows], theirs_ref[...])
        out_ref[:, columns : 2 * columns] = jnp.where(low, theirs_ref[...], turned_ref[rows:])
        out_ref[:, 2 * columns :] = first_ref[...]

    return kernel_call(
        kernel,
        "lead_message",
        out_shape=jax.ShapeDtypeStruct((rows, 2 * columns + first.shape[1]), jnp.float32),
        in_specs=in_vmem(3),
        out_specs=in_vmem(1)[0],
    )(turned, theirs, first)


def inner_chain(parent_links, pivot_inverse):
    nodes, width, _ = pivot_inverse.shape

    def kernel(parent_ref, pivot_ref, cross_ref, inner_ref):
        inner = pivot_ref[0]
        inner_ref[0] = inner
        for node in range(1, nodes):
            link = halves(parent_ref[node - 1])
            cross = dot_halves(halves(inner), link)
            cross_ref[node - 1] = -cross
            inner = pivot_ref[node] + dot_halves(link, halves(cross), ((0,), (0,)))
            inner_ref[node] = inner

    return kernel_call(
        kernel,
        "inner_chain",
        out_shape=[jax.ShapeDtypeStruct(array.shape, jnp.float32) for array in (parent_links, pivot_inverse)],
        in_specs=in_vmem(2),
        out_specs=in_vmem(2),
    )(parent_links, pivot_inverse)


def ring_owner(my_index, count, shift, other):
    core = lax.rem(my_index, 2)
    chip = my_index // 2
    place = jnp.where(lax.rem(chip, 2) == 0, chip // 2, count - 1 - chip // 2)
    place = lax.rem(place + shift + count, count)
    chip = jnp.where(place < count // 2, 2 * place, 2 * (count - 1 - place) + 1)
    return 2 * chip + (1 - core if other else core)


def border(arrivals, held, parents, diagonals, chips, last=False):
    nodes, width, _ = diagonals.shape
    rows = arrivals[0][2].shape[0]
    order = arrivals[0][2].shape[1] - LEAD * width
    count = len(arrivals)
    fresh = rows * count
    bf16 = jnp.bfloat16

    def kernel(*refs):
        refs = list(refs)
        take = lambda number: [refs.pop(0) for _ in range(number)]
        lead_refs, rest_refs = take(count), take(count)
        own_ref = take(1)[0] if last else None
        held_before = take(2) if held else None
        parents_ref, diagonals_ref, parents_out, diagonals_out = take(4)
        copies = []

        def finish(place, source, target):
            if last:
                copies.append(pltpu.make_async_copy(source, target, sems.at[place]))
                copies[-1].start()

        parents_end, diagonals_end = parents_out, diagonals_out
        if last:
            (panel_end,) = take(1)
        held_now = take(2)
        turned = take(2)
        if last:
            parents_out, diagonals_out, panel_out, sems = take(4)
        me = lax.axis_index("row")
        owners = [ring_owner(me, chips, shift, other) for shift, other, _, _ in arrivals]

        for part, whole in enumerate(held_now):
            whole[...] = held_before[part][...] if held else jnp.zeros(whole.shape, bf16)
        for owner, lead, rest in zip(owners, lead_refs, rest_refs):
            start = pl.multiple_of(owner * rows, 16)
            for whole, part in zip(held_now, halves(lead[:, order:])):
                whole[pl.ds(start, rows), : LEAD * width] = part
            for whole, part in zip(held_now, halves(rest[...])):
                whole[pl.ds(start, rows), LEAD * width :] = part
        piece = lax.broadcasted_iota(jnp.int32, (1, order), 1) // rows
        weight = jnp.ones((1, order), jnp.float32)
        for owner in owners:
            weight = jnp.where(piece == owner, 0.5, weight)
        left = [ref[:, :order] * weight for ref in lead_refs]
        if last:
            left.append(own_ref[:, :order])
        left = halves(jnp.concatenate(left, axis=0))
        right = []
        for node in range(nodes):
            columns = slice(node * width, (node + 1) * width)
            image = stacked_dot(left, [whole[:, columns] for whole in held_now])
            if last:
                panel_out[:, node, :] = -image[fresh:]
            image = image[:fresh]
            if node < LEAD:
                new = [ref[:, order + node * width : order + (node + 1) * width] for ref in lead_refs]
            else:
                new = [ref[:, (node - LEAD) * width : (node - LEAD + 1) * width] for ref in rest_refs]
            new = jnp.concatenate(new, axis=0)
            for whole, part in zip(turned, halves(jnp.concatenate([new, image], axis=0).T)):
                whole[columns, :] = part
            right.append([jnp.concatenate(pair, axis=0) for pair in zip(halves(image), halves(new))])
        if last:
            finish(2 * nodes, panel_out, panel_end)
        for node in range(nodes):
            lower = max(node - 1, 0) * width
            total = stacked_dot([whole[lower : (node + 1) * width, :] for whole in turned], right[node])
            diagonals_out[node] = diagonals_ref[node] + total[-width:]
            finish(node, diagonals_out.at[node], diagonals_end.at[node])
            if node > 0:
                parents_out[node - 1] = parents_ref[node - 1] + total[:width]
                finish(nodes + node, parents_out.at[node - 1], parents_end.at[node - 1])
        for copy in copies:
            copy.wait()

    operands = [lead for _, _, lead, _ in arrivals] + [rest for _, _, _, rest in arrivals]
    operands += [last] if last is not False else []
    operands += [*(held or []), parents, diagonals]
    last = last is not False
    state = [(order, nodes * width)] * 2
    shapes = [jax.ShapeDtypeStruct(array.shape, jnp.float32) for array in (parents, diagonals)]
    scratch = [pltpu.VMEM((nodes * width, 2 * fresh), bf16)] * 2
    if last:
        shapes.append(jax.ShapeDtypeStruct((rows, nodes, width), jnp.float32))
        scratch = [pltpu.VMEM(shape, bf16) for shape in state] + scratch
        scratch += [pltpu.VMEM(array.shape, jnp.float32) for array in shapes]
        scratch.append(pltpu.SemaphoreType.DMA((2 * nodes + 1,)))
    else:
        shapes += [jax.ShapeDtypeStruct(shape, bf16) for shape in state]
    results = kernel_call(
        kernel,
        "border" + ("_end" if last else "" if held else "_start"),
        out_shape=shapes,
        in_specs=in_vmem(len(operands)),
        out_specs=at_home(len(shapes)) if last else in_vmem(len(shapes)),
        scratch_shapes=scratch,
        limit=24 * 2**20 if last else 16 * 2**20,
    )(*operands)
    return results[:2], results[2:]


def gather_plan(anc_blocks, anc_links, parent_links, pivot_inverse, pattern):
    chips = lax.axis_size("row") // 2
    far = chips // 2
    ahead, behind = ring_pairs(chips, 1), ring_pairs(chips, -1)
    across = [p for p in ahead if p[0] % 2 == 0] + [p for p in behind if p[0] % 2 == 1]

    def move(pair):
        return [lax.ppermute(value, "row", way) for value, way in zip(pair, (ahead, behind))]

    def both(shift, lead, rest):
        return [(shift, False, lead, rest), (shift, True, swap_bit(lead, 0), swap_bit(rest, 0))]

    turned = anc_blocks[0].T
    theirs = partner_rows(turned)
    first, rest = link_chain(after(anc_links, theirs), parent_links, pattern)
    lead = lead_message(turned, swap_bit(theirs, PCOL.bit_length() - 1), first)
    totals = inner_chain(after(parent_links, lead), pivot_inverse)
    leads, rests = [lead] * 2, [rest] * 2
    arrivals, held = both(0, lead, rest), None
    for step in range(1, far):
        leads = move(leads)
        last_lead = pick(leads) if step == far - 1 else lead
        leads, last_lead, totals = lax.optimization_barrier((leads, last_lead, totals))
        totals, held = border(arrivals, held, *totals, chips)
        rests, totals = lax.optimization_barrier((move(rests), totals))
        arrivals = both(-step, leads[0], rests[0]) + both(step, leads[1], rests[1])
    last_rest, totals = lax.optimization_barrier((pick(rests), totals))
    totals, held = border(arrivals, held, *totals, chips)
    last = [lax.ppermute(value, "row", across) for value in (last_lead, last_rest)]
    last, totals = lax.optimization_barrier((last, totals))
    totals, panels = border(both(far, *last), held, *totals, chips, last=lead)
    return panels[0], *totals


def spread_plan(anc_blocks, anc_links, parent_links, pivot_inverse, pattern):
    my_index = lax.axis_index("row")
    total_bits = lax.axis_size("row").bit_length() - 1
    low_bits = PCOL.bit_length() - 1
    rows, nodes, width = anc_links.shape
    links = jnp.concatenate(reduced_links(masked_links(my_index, anc_links, pattern), parent_links), axis=1)
    segment = links
    for bit in range(low_bits, total_bits):
        partner = swap_bit(segment, bit)
        upper = my_index >> bit & 1
        segment = lax.dynamic_update_slice_in_dim(
            jnp.concatenate([partner, partner], 0), segment, upper * segment.shape[0], 0
        )
    image = product(anc_blocks[0], segment)
    for bit in reversed(range(low_bits)):
        half_rows = image.shape[0] // 2
        upper = my_index >> bit & 1
        retained = lax.dynamic_slice_in_dim(image, upper * half_rows, half_rows, 0)
        outgoing = lax.dynamic_slice_in_dim(image, (1 - upper) * half_rows, half_rows, 0)
        image = retained + swap_bit(outgoing, bit)
    column = lambda array, node: array[:, node * width : (node + 1) * width]
    terms = [inner_product(column(links, node), column(image, node)) for node in range(nodes)]
    terms += [inner_product(column(links, node - 1), column(image, node)) for node in range(1, nodes)]
    totals = lax.psum(jnp.stack(terms), "row")
    inner, cross = local_chain(parent_links, pivot_inverse)
    diagonals = jnp.stack(inner) + totals[:nodes]
    parents = totals[nodes:] - jnp.stack(cross)
    return -image.reshape(rows, nodes, width), parents, diagonals


def on_device(anc_blocks, anc_links, parent_links, pivot_inverse, pattern):
    size = lax.axis_size("row")
    rows, nodes, width = anc_links.shape
    whole_bytes = 4 * size * rows * (nodes * width + size * rows)
    plan = gather_plan if size == 2 * PCOL and whole_bytes <= GATHER_LIMIT else spread_plan
    return plan(anc_blocks, anc_links, parent_links, pivot_inverse, pattern)


def solution(mesh):
    return jax.shard_map(
        on_device,
        mesh=mesh,
        in_specs=(
            P(("pole", "row"), None, None),
            P(("pole", "row"), None, None),
            P("pole", None, None),
            P("pole", None, None),
            P(),
        ),
        out_specs=(P(("pole", "row"), None, None), P("pole", None, None), P("pole", None, None)),
        check_vma=False,
    )
```

```python
import jax
import jax.numpy as jnp
from jax import lax
from jax.experimental import pallas as pl
from jax.experimental.pallas import tpu as pltpu
from jax.sharding import PartitionSpec as P

PCOL = 8
TILE = 128
BORDER_FLOPS = 0
GATHER_LIMIT = 16 * 2**20
LINK_LIMIT = 65_600_000


def product(left, right):
    return jnp.dot(left, right, precision=lax.Precision.HIGH, preferred_element_type=jnp.float32)


def inner_product(left, right):
    return lax.dot_general(
        left,
        right,
        (((0,), (0,)), ((), ())),
        precision=lax.Precision.HIGH,
        preferred_element_type=jnp.float32,
    )


def swap_bit(value, bit):
    mask = 2**bit
    return lax.ppermute(value, "row", [(i, i ^ mask) for i in range(lax.axis_size("row"))])


def ring_chips(count):
    return list(range(0, count, 2)) + list(range(count - 1, 0, -2))


def ring_pairs(count, shift):
    order = ring_chips(count)
    pairs = []
    for place, chip in enumerate(order):
        target = order[(place + shift) % count]
        pairs += [(2 * chip + core, 2 * target + core) for core in range(2)]
    return pairs


def masked_links(my_index, anc_links, pattern):
    rows_here = anc_links.shape[0]
    tile_index = (my_index * rows_here + jnp.arange(rows_here, dtype=jnp.int32)) // TILE
    row_keep = jnp.take(pattern, tile_index, axis=1) != 0
    return jnp.where(row_keep[:, :, None], jnp.swapaxes(anc_links, 0, 1), 0.0)


def reduced_links(links, parent_links):
    reduced = [links[0]]
    for node in range(1, links.shape[0]):
        reduced.append(links[node] - product(reduced[-1], parent_links[node - 1]))
    return reduced


def local_chain(parent_links, pivot_inverse):
    inner = [pivot_inverse[0]]
    cross = []
    for node in range(1, pivot_inverse.shape[0]):
        link = parent_links[node - 1]
        cross.append(product(inner[-1], link))
        inner.append(pivot_inverse[node] + inner_product(link, cross[-1]))
    return inner, cross


def halves(value):
    high = value.astype(jnp.bfloat16)
    return high, (value - high.astype(jnp.float32)).astype(jnp.bfloat16)


def dot_halves(left, right, dims=((1,), (0,))):
    def one(a, b):
        return lax.dot_general(a, b, (dims, ((), ())), preferred_element_type=jnp.float32)

    return one(left[0], right[0]) + (one(left[0], right[1]) + one(left[1], right[0]))


def stacked_dot(left, right):
    height = left[0].shape[0]
    both = jnp.dot(jnp.concatenate(left, axis=0), right[0], preferred_element_type=jnp.float32)
    cross = jnp.dot(left[0], right[1], preferred_element_type=jnp.float32)
    return both[:height] + (both[height:] + cross)


def kernel_call(kernel, name, limit=16 * 2**20, flops=0, **more):
    return pl.pallas_call(
        kernel,
        name=name,
        compiler_params=pltpu.CompilerParams(vmem_limit_bytes=limit),
        cost_estimate=pl.CostEstimate(flops=flops, bytes_accessed=0, transcendentals=0),
        **more,
    )


def in_vmem(count):
    return [pl.BlockSpec(memory_space=pltpu.VMEM)] * count


def after(value, *others):
    return lax.optimization_barrier((value, *others))[0]


def at_home(count):
    return [pl.BlockSpec(memory_space=pltpu.HBM)] * count


def partner_rows(turned):
    rows, columns = turned.shape[0] // 2, turned.shape[1]

    def kernel(turned_ref, out_ref):
        out_ref[...] = jnp.where(lax.axis_index("row") < PCOL, turned_ref[rows:], turned_ref[:rows])

    return kernel_call(
        kernel,
        "partner_rows",
        out_shape=jax.ShapeDtypeStruct((rows, columns), jnp.float32),
        in_specs=in_vmem(1),
        out_specs=in_vmem(1)[0],
    )(turned)


def pick(pair):
    def kernel(first_ref, second_ref, out_ref):
        out_ref[...] = jnp.where(lax.rem(lax.axis_index("row"), 2) == 0, first_ref[...], second_ref[...])

    return kernel_call(
        kernel,
        "pick",
        out_shape=jax.ShapeDtypeStruct(pair[0].shape, jnp.float32),
        in_specs=in_vmem(2),
        out_specs=in_vmem(1)[0],
    )(*pair)


def link_chain(anc_links, parent_links, pattern):
    rows, nodes, width = anc_links.shape
    tiles = pattern.shape[1]

    def kernel(links_home, parent_home, pattern_ref, out_ref, links_ref, parent_ref, sems):
        fetches = [pltpu.make_async_copy(links_home, links_ref, sems.at[0])]
        for node in range(1, nodes):
            fetches.append(
                pltpu.make_async_copy(parent_home.at[node - 1], parent_ref.at[node - 1], sems.at[node])
            )
        for fetch in fetches:
            fetch.start()
        first = lax.axis_index("row") * rows
        tile = first // TILE
        next_tile = jnp.minimum(tile + 1, tiles - 1)
        row = first + lax.broadcasted_iota(jnp.int32, (rows, width), 0)
        in_first = row < (tile + 1) * TILE
        reduced = None
        for node in range(nodes):
            fetches[node].wait()
            keep = jnp.where(in_first, pattern_ref[node, tile], pattern_ref[node, next_tile])
            links = jnp.where(keep != 0, links_ref[:, node, :], 0.0)
            if node > 0:
                links = links - dot_halves(halves(reduced), halves(parent_ref[node - 1]))
            out_ref[:, node * width : (node + 1) * width] = links
            reduced = links

    return kernel_call(
        kernel,
        "link_chain",
        limit=LINK_LIMIT,
        out_shape=jax.ShapeDtypeStruct((rows, nodes * width), jnp.float32),
        in_specs=at_home(2) + [pl.BlockSpec(memory_space=pltpu.SMEM)],
        out_specs=in_vmem(1)[0],
        scratch_shapes=[
            pltpu.VMEM(anc_links.shape, jnp.float32),
            pltpu.VMEM(parent_links.shape, jnp.float32),
            pltpu.SemaphoreType.DMA((nodes,)),
        ],
    )(anc_links, parent_links, pattern)


def whole_message(turned, theirs, links):
    rows, columns = theirs.shape

    def kernel(turned_ref, theirs_ref, links_ref, out_ref):
        low = lax.axis_index("row") < PCOL
        out_ref[:, :columns] = jnp.where(low, turned_ref[:rows], theirs_ref[...])
        out_ref[:, columns : 2 * columns] = jnp.where(low, theirs_ref[...], turned_ref[rows:])
        out_ref[:, 2 * columns :] = links_ref[...]

    return kernel_call(
        kernel,
        "whole_message",
        out_shape=jax.ShapeDtypeStruct((rows, 2 * columns + links.shape[1]), jnp.float32),
        in_specs=in_vmem(3),
        out_specs=in_vmem(1)[0],
    )(turned, theirs, links)


def inner_chain(parent_links, pivot_inverse):
    nodes, width, _ = pivot_inverse.shape

    def kernel(parent_ref, pivot_ref, cross_ref, inner_ref):
        inner = pivot_ref[0]
        inner_ref[0] = inner
        for node in range(1, nodes):
            link = halves(parent_ref[node - 1])
            cross = dot_halves(halves(inner), link)
            cross_ref[node - 1] = -cross
            inner = pivot_ref[node] + dot_halves(link, halves(cross), ((0,), (0,)))
            inner_ref[node] = inner

    return kernel_call(
        kernel,
        "inner_chain",
        out_shape=[jax.ShapeDtypeStruct(array.shape, jnp.float32) for array in (parent_links, pivot_inverse)],
        in_specs=in_vmem(2),
        out_specs=in_vmem(2),
    )(parent_links, pivot_inverse)


def ring_owner(my_index, count, shift, other):
    core = lax.rem(my_index, 2)
    chip = my_index // 2
    place = jnp.where(lax.rem(chip, 2) == 0, chip // 2, count - 1 - chip // 2)
    place = lax.rem(place + shift + count, count)
    chip = jnp.where(place < count // 2, 2 * place, 2 * (count - 1 - place) + 1)
    return 2 * chip + (1 - core if other else core)


def border(arrivals, held, parents, diagonals, chips, last=False):
    nodes, width, _ = diagonals.shape
    rows = arrivals[0][2].shape[0]
    order = arrivals[0][2].shape[1] - nodes * width
    count = len(arrivals)
    fresh = rows * count
    bf16 = jnp.bfloat16

    def kernel(*refs):
        refs = list(refs)
        take = lambda number: [refs.pop(0) for _ in range(number)]
        part_refs = take(count)
        own_ref = take(1)[0] if last else None
        held_before = take(2) if held else None
        parents_ref, diagonals_ref, parents_out, diagonals_out = take(4)
        copies = []

        def finish(place, source, target):
            if last:
                copies.append(pltpu.make_async_copy(source, target, sems.at[place]))
                copies[-1].start()

        parents_end, diagonals_end = parents_out, diagonals_out
        if last:
            (panel_end,) = take(1)
        held_now = take(2)
        turned = take(2)
        if last:
            parents_out, diagonals_out, panel_out, sems = take(4)
        me = lax.axis_index("row")
        owners = [ring_owner(me, chips, shift, other) for shift, other, _ in arrivals]

        for part, whole in enumerate(held_now):
            whole[...] = held_before[part][...] if held else jnp.zeros(whole.shape, bf16)
        for owner, ref in zip(owners, part_refs):
            start = pl.multiple_of(owner * rows, 16)
            for whole, part in zip(held_now, halves(ref[:, order:])):
                whole[pl.ds(start, rows), :] = part
        piece = lax.broadcasted_iota(jnp.int32, (1, order), 1) // rows
        weight = jnp.ones((1, order), jnp.float32)
        for owner in owners:
            weight = jnp.where(piece == owner, 0.5, weight)
        left = [ref[:, :order] * weight for ref in part_refs]
        if last:
            left.append(own_ref[:, :order])
        left = halves(jnp.concatenate(left, axis=0))
        right = []
        for node in range(nodes):
            columns = slice(node * width, (node + 1) * width)
            image = stacked_dot(left, [whole[:, columns] for whole in held_now])
            if last:
                panel_out[:, node, :] = -image[fresh:]
            image = image[:fresh]
            there = slice(order + node * width, order + (node + 1) * width)
            new = jnp.concatenate([ref[:, there] for ref in part_refs], axis=0)
            for whole, part in zip(turned, halves(jnp.concatenate([new, image], axis=0).T)):
                whole[columns, :] = part
            right.append([jnp.concatenate(pair, axis=0) for pair in zip(halves(image), halves(new))])
        if last:
            finish(2 * nodes, panel_out, panel_end)
        for node in range(nodes):
            lower = max(node - 1, 0) * width
            total = stacked_dot([whole[lower : (node + 1) * width, :] for whole in turned], right[node])
            diagonals_out[node] = diagonals_ref[node] + total[-width:]
            finish(node, diagonals_out.at[node], diagonals_end.at[node])
            if node > 0:
                parents_out[node - 1] = parents_ref[node - 1] + total[:width]
                finish(nodes + node, parents_out.at[node - 1], parents_end.at[node - 1])
        for copy in copies:
            copy.wait()

    operands = [part for _, _, part in arrivals]
    operands += [last] if last is not False else []
    operands += [*(held or []), parents, diagonals]
    last = last is not False
    state = [(order, nodes * width)] * 2
    shapes = [jax.ShapeDtypeStruct(array.shape, jnp.float32) for array in (parents, diagonals)]
    scratch = [pltpu.VMEM((nodes * width, 2 * fresh), bf16)] * 2
    if last:
        shapes.append(jax.ShapeDtypeStruct((rows, nodes, width), jnp.float32))
        scratch = [pltpu.VMEM(shape, bf16) for shape in state] + scratch
        scratch += [pltpu.VMEM(array.shape, jnp.float32) for array in shapes]
        scratch.append(pltpu.SemaphoreType.DMA((2 * nodes + 1,)))
    else:
        shapes += [jax.ShapeDtypeStruct(shape, bf16) for shape in state]
    results = kernel_call(
        kernel,
        "border" + ("_end" if last else "" if held else "_start"),
        out_shape=shapes,
        in_specs=in_vmem(len(operands)),
        out_specs=at_home(len(shapes)) if last else in_vmem(len(shapes)),
        scratch_shapes=scratch,
        limit=24 * 2**20 if last else 16 * 2**20,
        flops=BORDER_FLOPS,
    )(*operands)
    return results[:2], results[2:]


def gather_plan(anc_blocks, anc_links, parent_links, pivot_inverse, pattern):
    chips = lax.axis_size("row") // 2
    far = chips // 2
    ahead, behind = ring_pairs(chips, 1), ring_pairs(chips, -1)
    across = [p for p in ahead if p[0] % 2 == 0] + [p for p in behind if p[0] % 2 == 1]

    def move(pair):
        return [lax.ppermute(value, "row", way) for value, way in zip(pair, (ahead, behind))]

    def both(shift, value):
        return [(shift, False, value), (shift, True, swap_bit(value, 0))]

    turned = anc_blocks[0].T
    theirs = partner_rows(turned)
    links = link_chain(after(anc_links, theirs), parent_links, pattern)
    own = whole_message(turned, swap_bit(theirs, PCOL.bit_length() - 1), links)
    totals, held = inner_chain(after(parent_links, own), pivot_inverse), None
    arrivals, pair = both(0, own), [own] * 2
    for step in range(1, far):
        pair = move(pair)
        totals, held = border(arrivals, held, *totals, chips)
        pair, totals = lax.optimization_barrier((pair, totals))
        arrivals = both(-step, pair[0]) + both(step, pair[1])
    last, totals = lax.optimization_barrier((pick(pair), totals))
    totals, held = border(arrivals, held, *totals, chips)
    last, totals = lax.optimization_barrier((lax.ppermute(last, "row", across), totals))
    totals, panels = border(both(far, last), held, *totals, chips, last=own)
    return panels[0], *totals


def spread_plan(anc_blocks, anc_links, parent_links, pivot_inverse, pattern):
    my_index = lax.axis_index("row")
    total_bits = lax.axis_size("row").bit_length() - 1
    low_bits = PCOL.bit_length() - 1
    rows, nodes, width = anc_links.shape
    links = jnp.concatenate(reduced_links(masked_links(my_index, anc_links, pattern), parent_links), axis=1)
    segment = links
    for bit in range(low_bits, total_bits):
        partner = swap_bit(segment, bit)
        upper = my_index >> bit & 1
        segment = lax.dynamic_update_slice_in_dim(
            jnp.concatenate([partner, partner], 0), segment, upper * segment.shape[0], 0
        )
    image = product(anc_blocks[0], segment)
    for bit in reversed(range(low_bits)):
        half_rows = image.shape[0] // 2
        upper = my_index >> bit & 1
        retained = lax.dynamic_slice_in_dim(image, upper * half_rows, half_rows, 0)
        outgoing = lax.dynamic_slice_in_dim(image, (1 - upper) * half_rows, half_rows, 0)
        image = retained + swap_bit(outgoing, bit)
    column = lambda array, node: array[:, node * width : (node + 1) * width]
    terms = [inner_product(column(links, node), column(image, node)) for node in range(nodes)]
    terms += [inner_product(column(links, node - 1), column(image, node)) for node in range(1, nodes)]
    totals = lax.psum(jnp.stack(terms), "row")
    inner, cross = local_chain(parent_links, pivot_inverse)
    diagonals = jnp.stack(inner) + totals[:nodes]
    parents = totals[nodes:] - jnp.stack(cross)
    return -image.reshape(rows, nodes, width), parents, diagonals


def on_device(anc_blocks, anc_links, parent_links, pivot_inverse, pattern):
    size = lax.axis_size("row")
    rows, nodes, width = anc_links.shape
    whole_bytes = 4 * size * rows * (nodes * width + size * rows)
    plan = gather_plan if size == 2 * PCOL and whole_bytes <= GATHER_LIMIT else spread_plan
    return plan(anc_blocks, anc_links, parent_links, pivot_inverse, pattern)


def solution(mesh):
    return jax.shard_map(
        on_device,
        mesh=mesh,
        in_specs=(
            P(("pole", "row"), None, None),
            P(("pole", "row"), None, None),
            P("pole", None, None),
            P("pole", None, None),
            P(),
        ),
        out_specs=(P(("pole", "row"), None, None), P("pole", None, None), P("pole", None, None)),
        check_vma=False,
    )
```

```python
import jax
import jax.numpy as jnp
from jax import lax
from jax.experimental import pallas as pl
from jax.experimental.pallas import tpu as pltpu
from jax.sharding import PartitionSpec as P

PCOL = 8
TILE = 128
BORDER_FLOPS = 0
GATHER_LIMIT = 16 * 2**20
LINK_LIMIT = 65_600_000


def product(left, right):
    return jnp.dot(left, right, precision=lax.Precision.HIGH, preferred_element_type=jnp.float32)


def inner_product(left, right):
    return lax.dot_general(
        left,
        right,
        (((0,), (0,)), ((), ())),
        precision=lax.Precision.HIGH,
        preferred_element_type=jnp.float32,
    )


def swap_bit(value, bit):
    mask = 2**bit
    return lax.ppermute(value, "row", [(i, i ^ mask) for i in range(lax.axis_size("row"))])


def ring_chips(count):
    return list(range(0, count, 2)) + list(range(count - 1, 0, -2))


def ring_pairs(count, shift):
    order = ring_chips(count)
    pairs = []
    for place, chip in enumerate(order):
        target = order[(place + shift) % count]
        pairs += [(2 * chip + core, 2 * target + core) for core in range(2)]
    return pairs


def masked_links(my_index, anc_links, pattern):
    rows_here = anc_links.shape[0]
    tile_index = (my_index * rows_here + jnp.arange(rows_here, dtype=jnp.int32)) // TILE
    row_keep = jnp.take(pattern, tile_index, axis=1) != 0
    return jnp.where(row_keep[:, :, None], jnp.swapaxes(anc_links, 0, 1), 0.0)


def reduced_links(links, parent_links):
    reduced = [links[0]]
    for node in range(1, links.shape[0]):
        reduced.append(links[node] - product(reduced[-1], parent_links[node - 1]))
    return reduced


def local_chain(parent_links, pivot_inverse):
    inner = [pivot_inverse[0]]
    cross = []
    for node in range(1, pivot_inverse.shape[0]):
        link = parent_links[node - 1]
        cross.append(product(inner[-1], link))
        inner.append(pivot_inverse[node] + inner_product(link, cross[-1]))
    return inner, cross


def halves(value):
    high = value.astype(jnp.bfloat16)
    return high, (value - high.astype(jnp.float32)).astype(jnp.bfloat16)


def dot_halves(left, right, dims=((1,), (0,))):
    def one(a, b):
        return lax.dot_general(a, b, (dims, ((), ())), preferred_element_type=jnp.float32)

    return one(left[0], right[0]) + (one(left[0], right[1]) + one(left[1], right[0]))


def stacked_dot(left, right):
    height = left[0].shape[0]
    both = jnp.dot(jnp.concatenate(left, axis=0), right[0], preferred_element_type=jnp.float32)
    cross = jnp.dot(left[0], right[1], preferred_element_type=jnp.float32)
    return both[:height] + (both[height:] + cross)


def kernel_call(kernel, name, limit=16 * 2**20, flops=0, **more):
    return pl.pallas_call(
        kernel,
        name=name,
        compiler_params=pltpu.CompilerParams(vmem_limit_bytes=limit),
        cost_estimate=pl.CostEstimate(flops=flops, bytes_accessed=0, transcendentals=0),
        **more,
    )


def in_vmem(count):
    return [pl.BlockSpec(memory_space=pltpu.VMEM)] * count


def after(value, *others):
    return lax.optimization_barrier((value, *others))[0]


def at_home(count):
    return [pl.BlockSpec(memory_space=pltpu.HBM)] * count


def partner_rows(turned):
    rows, columns = turned.shape[0] // 2, turned.shape[1]

    def kernel(turned_ref, out_ref):
        out_ref[...] = jnp.where(lax.axis_index("row") < PCOL, turned_ref[rows:], turned_ref[:rows])

    return kernel_call(
        kernel,
        "partner_rows",
        out_shape=jax.ShapeDtypeStruct((rows, columns), jnp.float32),
        in_specs=in_vmem(1),
        out_specs=in_vmem(1)[0],
    )(turned)


def pick(pair):
    def kernel(first_ref, second_ref, out_ref):
        out_ref[...] = jnp.where(lax.rem(lax.axis_index("row"), 2) == 0, first_ref[...], second_ref[...])

    return kernel_call(
        kernel,
        "pick",
        out_shape=jax.ShapeDtypeStruct(pair[0].shape, jnp.float32),
        in_specs=in_vmem(2),
        out_specs=in_vmem(1)[0],
    )(*pair)


def link_chain(anc_links, parent_links, pattern):
    rows, nodes, width = anc_links.shape
    tiles = pattern.shape[1]

    def kernel(links_home, parent_home, pattern_ref, out_ref, links_ref, parent_ref, sems):
        fetches = [pltpu.make_async_copy(links_home, links_ref, sems.at[0])]
        for node in range(1, nodes):
            fetches.append(
                pltpu.make_async_copy(parent_home.at[node - 1], parent_ref.at[node - 1], sems.at[node])
            )
        for fetch in fetches:
            fetch.start()
        first = lax.axis_index("row") * rows
        tile = first // TILE
        next_tile = jnp.minimum(tile + 1, tiles - 1)
        row = first + lax.broadcasted_iota(jnp.int32, (rows, width), 0)
        in_first = row < (tile + 1) * TILE
        reduced = None
        for node in range(nodes):
            fetches[node].wait()
            keep = jnp.where(in_first, pattern_ref[node, tile], pattern_ref[node, next_tile])
            links = jnp.where(keep != 0, links_ref[:, node, :], 0.0)
            if node > 0:
                links = links - dot_halves(halves(reduced), halves(parent_ref[node - 1]))
            out_ref[:, node * width : (node + 1) * width] = links
            reduced = links

    return kernel_call(
        kernel,
        "link_chain",
        limit=LINK_LIMIT,
        out_shape=jax.ShapeDtypeStruct((rows, nodes * width), jnp.float32),
        in_specs=at_home(2) + [pl.BlockSpec(memory_space=pltpu.SMEM)],
        out_specs=in_vmem(1)[0],
        scratch_shapes=[
            pltpu.VMEM(anc_links.shape, jnp.float32),
            pltpu.VMEM(parent_links.shape, jnp.float32),
            pltpu.SemaphoreType.DMA((nodes,)),
        ],
    )(anc_links, parent_links, pattern)


def whole_message(turned, theirs, links):
    rows, columns = theirs.shape

    def kernel(turned_ref, theirs_ref, links_ref, out_ref):
        low = lax.axis_index("row") < PCOL
        out_ref[:, :columns] = jnp.where(low, turned_ref[:rows], theirs_ref[...])
        out_ref[:, columns : 2 * columns] = jnp.where(low, theirs_ref[...], turned_ref[rows:])
        out_ref[:, 2 * columns :] = links_ref[...]

    return kernel_call(
        kernel,
        "whole_message",
        out_shape=jax.ShapeDtypeStruct((rows, 2 * columns + links.shape[1]), jnp.float32),
        in_specs=in_vmem(3),
        out_specs=in_vmem(1)[0],
    )(turned, theirs, links)


def inner_chain(parent_links, pivot_inverse):
    nodes, width, _ = pivot_inverse.shape

    def kernel(parent_ref, pivot_ref, cross_ref, inner_ref):
        inner = pivot_ref[0]
        inner_ref[0] = inner
        for node in range(1, nodes):
            link = halves(parent_ref[node - 1])
            cross = dot_halves(halves(inner), link)
            cross_ref[node - 1] = -cross
            inner = pivot_ref[node] + dot_halves(link, halves(cross), ((0,), (0,)))
            inner_ref[node] = inner

    return kernel_call(
        kernel,
        "inner_chain",
        out_shape=[jax.ShapeDtypeStruct(array.shape, jnp.float32) for array in (parent_links, pivot_inverse)],
        in_specs=in_vmem(2),
        out_specs=in_vmem(2),
    )(parent_links, pivot_inverse)


def ring_owner(my_index, count, shift, other):
    core = lax.rem(my_index, 2)
    chip = my_index // 2
    place = jnp.where(lax.rem(chip, 2) == 0, chip // 2, count - 1 - chip // 2)
    place = lax.rem(place + shift + count, count)
    chip = jnp.where(place < count // 2, 2 * place, 2 * (count - 1 - place) + 1)
    return 2 * chip + (1 - core if other else core)


def border(arrivals, held, parents, diagonals, chips, last=False):
    nodes, width, _ = diagonals.shape
    rows = arrivals[0][2].shape[0]
    order = arrivals[0][2].shape[1] - nodes * width
    count = len(arrivals)
    fresh = rows * count
    bf16 = jnp.bfloat16

    def kernel(*refs):
        refs = list(refs)
        take = lambda number: [refs.pop(0) for _ in range(number)]
        part_refs = take(count)
        own_ref = take(1)[0] if last else None
        held_before = take(2) if held else None
        parents_ref, diagonals_ref, parents_out, diagonals_out = take(4)
        copies = []

        def finish(place, source, target):
            if last:
                copies.append(pltpu.make_async_copy(source, target, sems.at[place]))
                copies[-1].start()

        parents_end, diagonals_end = parents_out, diagonals_out
        if last:
            (panel_end,) = take(1)
        held_now = take(2)
        turned = take(2)
        if last:
            parents_out, diagonals_out, panel_out, sems = take(4)
        me = lax.axis_index("row")
        owners = [ring_owner(me, chips, shift, other) for shift, other, _ in arrivals]

        for part, whole in enumerate(held_now):
            whole[...] = held_before[part][...] if held else jnp.zeros(whole.shape, bf16)
        for owner, ref in zip(owners, part_refs):
            start = pl.multiple_of(owner * rows, 16)
            for whole, part in zip(held_now, halves(ref[:, order:])):
                whole[pl.ds(start, rows), :] = part
        piece = lax.broadcasted_iota(jnp.int32, (1, order), 1) // rows
        weight = jnp.ones((1, order), jnp.float32)
        for owner in owners:
            weight = jnp.where(piece == owner, 0.5, weight)
        left = [ref[:, :order] * weight for ref in part_refs]
        if last:
            left.append(own_ref[:, :order])
        left = halves(jnp.concatenate(left, axis=0))
        right = []

        def multiply(node):
            columns = slice(node * width, (node + 1) * width)
            image = stacked_dot(left, [whole[:, columns] for whole in held_now])
            if last:
                panel_out[:, node, :] = -image[fresh:]
            image = image[:fresh]
            there = slice(order + node * width, order + (node + 1) * width)
            new = jnp.concatenate([ref[:, there] for ref in part_refs], axis=0)
            for whole, part in zip(turned, halves(jnp.concatenate([new, image], axis=0).T)):
                whole[columns, :] = part
            right.append([jnp.concatenate(pair, axis=0) for pair in zip(halves(image), halves(new))])

        def add(node):
            lower = max(node - 1, 0) * width
            total = stacked_dot([whole[lower : (node + 1) * width, :] for whole in turned], right[node])
            diagonals_out[node] = diagonals_ref[node] + total[-width:]
            finish(node, diagonals_out.at[node], diagonals_end.at[node])
            if node > 0:
                parents_out[node - 1] = parents_ref[node - 1] + total[:width]
                finish(nodes + node, parents_out.at[node - 1], parents_end.at[node - 1])

        for node in range(nodes):
            multiply(node)
            if node > 0:
                add(node - 1)
        if last:
            finish(2 * nodes, panel_out, panel_end)
        add(nodes - 1)
        for copy in copies:
            copy.wait()

    operands = [part for _, _, part in arrivals]
    operands += [last] if last is not False else []
    operands += [*(held or []), parents, diagonals]
    last = last is not False
    state = [(order, nodes * width)] * 2
    shapes = [jax.ShapeDtypeStruct(array.shape, jnp.float32) for array in (parents, diagonals)]
    scratch = [pltpu.VMEM((nodes * width, 2 * fresh), bf16)] * 2
    if last:
        shapes.append(jax.ShapeDtypeStruct((rows, nodes, width), jnp.float32))
        scratch = [pltpu.VMEM(shape, bf16) for shape in state] + scratch
        scratch += [pltpu.VMEM(array.shape, jnp.float32) for array in shapes]
        scratch.append(pltpu.SemaphoreType.DMA((2 * nodes + 1,)))
    else:
        shapes += [jax.ShapeDtypeStruct(shape, bf16) for shape in state]
    results = kernel_call(
        kernel,
        "border" + ("_end" if last else "" if held else "_start"),
        out_shape=shapes,
        in_specs=in_vmem(len(operands)),
        out_specs=at_home(len(shapes)) if last else in_vmem(len(shapes)),
        scratch_shapes=scratch,
        limit=24 * 2**20 if last else 16 * 2**20,
        flops=BORDER_FLOPS,
    )(*operands)
    return results[:2], results[2:]


def gather_plan(anc_blocks, anc_links, parent_links, pivot_inverse, pattern):
    chips = lax.axis_size("row") // 2
    far = chips // 2
    ahead, behind = ring_pairs(chips, 1), ring_pairs(chips, -1)
    across = [p for p in ahead if p[0] % 2 == 0] + [p for p in behind if p[0] % 2 == 1]

    def move(pair):
        return [lax.ppermute(value, "row", way) for value, way in zip(pair, (ahead, behind))]

    def both(shift, value):
        return [(shift, False, value), (shift, True, swap_bit(value, 0))]

    turned = anc_blocks[0].T
    theirs = partner_rows(turned)
    links = link_chain(after(anc_links, theirs), parent_links, pattern)
    own = whole_message(turned, swap_bit(theirs, PCOL.bit_length() - 1), links)
    totals, held = inner_chain(after(parent_links, own), pivot_inverse), None
    arrivals, pair = both(0, own), [own] * 2
    for step in range(1, far):
        pair = move(pair)
        totals, held = border(arrivals, held, *totals, chips)
        pair = [after(value, *totals) for value in pair]
        arrivals = both(-step, pair[0]) + both(step, pair[1])
    last, totals = lax.optimization_barrier((pick(pair), totals))
    totals, held = border(arrivals, held, *totals, chips)
    last, totals = lax.optimization_barrier((lax.ppermute(last, "row", across), totals))
    totals, panels = border(both(far, last), held, *totals, chips, last=own)
    return panels[0], *totals


def spread_plan(anc_blocks, anc_links, parent_links, pivot_inverse, pattern):
    my_index = lax.axis_index("row")
    total_bits = lax.axis_size("row").bit_length() - 1
    low_bits = PCOL.bit_length() - 1
    rows, nodes, width = anc_links.shape
    links = jnp.concatenate(reduced_links(masked_links(my_index, anc_links, pattern), parent_links), axis=1)
    segment = links
    for bit in range(low_bits, total_bits):
        partner = swap_bit(segment, bit)
        upper = my_index >> bit & 1
        segment = lax.dynamic_update_slice_in_dim(
            jnp.concatenate([partner, partner], 0), segment, upper * segment.shape[0], 0
        )
    image = product(anc_blocks[0], segment)
    for bit in reversed(range(low_bits)):
        half_rows = image.shape[0] // 2
        upper = my_index >> bit & 1
        retained = lax.dynamic_slice_in_dim(image, upper * half_rows, half_rows, 0)
        outgoing = lax.dynamic_slice_in_dim(image, (1 - upper) * half_rows, half_rows, 0)
        image = retained + swap_bit(outgoing, bit)
    column = lambda array, node: array[:, node * width : (node + 1) * width]
    terms = [inner_product(column(links, node), column(image, node)) for node in range(nodes)]
    terms += [inner_product(column(links, node - 1), column(image, node)) for node in range(1, nodes)]
    totals = lax.psum(jnp.stack(terms), "row")
    inner, cross = local_chain(parent_links, pivot_inverse)
    diagonals = jnp.stack(inner) + totals[:nodes]
    parents = totals[nodes:] - jnp.stack(cross)
    return -image.reshape(rows, nodes, width), parents, diagonals


def on_device(anc_blocks, anc_links, parent_links, pivot_inverse, pattern):
    size = lax.axis_size("row")
    rows, nodes, width = anc_links.shape
    whole_bytes = 4 * size * rows * (nodes * width + size * rows)
    plan = gather_plan if size == 2 * PCOL and whole_bytes <= GATHER_LIMIT else spread_plan
    return plan(anc_blocks, anc_links, parent_links, pivot_inverse, pattern)


def solution(mesh):
    return jax.shard_map(
        on_device,
        mesh=mesh,
        in_specs=(
            P(("pole", "row"), None, None),
            P(("pole", "row"), None, None),
            P("pole", None, None),
            P("pole", None, None),
            P(),
        ),
        out_specs=(P(("pole", "row"), None, None), P("pole", None, None), P("pole", None, None)),
        check_vma=False,
    )
```

```python
import jax
import jax.numpy as jnp
from jax import lax
from jax.experimental import pallas as pl
from jax.experimental.pallas import tpu as pltpu
from jax.sharding import PartitionSpec as P

PCOL = 8
TILE = 128
GATHER_LIMIT = 16 * 2**20
LINK_LIMIT = 65_600_000


def product(left, right):
    return jnp.dot(left, right, precision=lax.Precision.HIGH, preferred_element_type=jnp.float32)


def inner_product(left, right):
    return lax.dot_general(
        left,
        right,
        (((0,), (0,)), ((), ())),
        precision=lax.Precision.HIGH,
        preferred_element_type=jnp.float32,
    )


def swap_bit(value, bit):
    mask = 2**bit
    return lax.ppermute(value, "row", [(i, i ^ mask) for i in range(lax.axis_size("row"))])


def ring_chips(count):
    return list(range(0, count, 2)) + list(range(count - 1, 0, -2))


def ring_pairs(count, shift):
    order = ring_chips(count)
    pairs = []
    for place, chip in enumerate(order):
        target = order[(place + shift) % count]
        pairs += [(2 * chip + core, 2 * target + core) for core in range(2)]
    return pairs


def masked_links(my_index, anc_links, pattern):
    rows_here = anc_links.shape[0]
    tile_index = (my_index * rows_here + jnp.arange(rows_here, dtype=jnp.int32)) // TILE
    row_keep = jnp.take(pattern, tile_index, axis=1) != 0
    return jnp.where(row_keep[:, :, None], jnp.swapaxes(anc_links, 0, 1), 0.0)


def reduced_links(links, parent_links):
    reduced = [links[0]]
    for node in range(1, links.shape[0]):
        reduced.append(links[node] - product(reduced[-1], parent_links[node - 1]))
    return reduced


def local_chain(parent_links, pivot_inverse):
    inner = [pivot_inverse[0]]
    cross = []
    for node in range(1, pivot_inverse.shape[0]):
        link = parent_links[node - 1]
        cross.append(product(inner[-1], link))
        inner.append(pivot_inverse[node] + inner_product(link, cross[-1]))
    return inner, cross


def halves(value):
    high = value.astype(jnp.bfloat16)
    return high, (value - high.astype(jnp.float32)).astype(jnp.bfloat16)


def dot_halves(left, right, dims=((1,), (0,))):
    def one(a, b):
        return lax.dot_general(a, b, (dims, ((), ())), preferred_element_type=jnp.float32)

    return one(left[0], right[0]) + (one(left[0], right[1]) + one(left[1], right[0]))


def stacked_dot(left, right):
    height = left[0].shape[0]
    both = jnp.dot(jnp.concatenate(left, axis=0), right[0], preferred_element_type=jnp.float32)
    cross = jnp.dot(left[0], right[1], preferred_element_type=jnp.float32)
    return both[:height] + (both[height:] + cross)


def kernel_call(kernel, name, limit=16 * 2**20, flops=0, **more):
    return pl.pallas_call(
        kernel,
        name=name,
        compiler_params=pltpu.CompilerParams(vmem_limit_bytes=limit),
        cost_estimate=pl.CostEstimate(flops=flops, bytes_accessed=0, transcendentals=0),
        **more,
    )


def in_vmem(count):
    return [pl.BlockSpec(memory_space=pltpu.VMEM)] * count


def after(value, *others):
    return lax.optimization_barrier((value, *others))[0]


def at_home(count):
    return [pl.BlockSpec(memory_space=pltpu.HBM)] * count


def partner_rows(turned):
    rows, columns = turned.shape[0] // 2, turned.shape[1]

    def kernel(turned_ref, out_ref):
        out_ref[...] = jnp.where(lax.axis_index("row") < PCOL, turned_ref[rows:], turned_ref[:rows])

    return kernel_call(
        kernel,
        "partner_rows",
        out_shape=jax.ShapeDtypeStruct((rows, columns), jnp.float32),
        in_specs=in_vmem(1),
        out_specs=in_vmem(1)[0],
    )(turned)


def pick(pair):
    def kernel(first_ref, second_ref, out_ref):
        out_ref[...] = jnp.where(lax.rem(lax.axis_index("row"), 2) == 0, first_ref[...], second_ref[...])

    return kernel_call(
        kernel,
        "pick",
        out_shape=jax.ShapeDtypeStruct(pair[0].shape, jnp.float32),
        in_specs=in_vmem(2),
        out_specs=in_vmem(1)[0],
    )(*pair)


def link_chain(anc_links, parent_links, pattern):
    rows, nodes, width = anc_links.shape
    tiles = pattern.shape[1]

    def kernel(links_home, parent_home, pattern_ref, out_ref, links_ref, parent_ref, sems):
        fetches = [pltpu.make_async_copy(links_home, links_ref, sems.at[0])]
        for node in range(1, nodes):
            fetches.append(
                pltpu.make_async_copy(parent_home.at[node - 1], parent_ref.at[node - 1], sems.at[node])
            )
        for fetch in fetches:
            fetch.start()
        first = lax.axis_index("row") * rows
        tile = first // TILE
        next_tile = jnp.minimum(tile + 1, tiles - 1)
        row = first + lax.broadcasted_iota(jnp.int32, (rows, width), 0)
        in_first = row < (tile + 1) * TILE
        reduced = None
        for node in range(nodes):
            fetches[node].wait()
            keep = jnp.where(in_first, pattern_ref[node, tile], pattern_ref[node, next_tile])
            links = jnp.where(keep != 0, links_ref[:, node, :], 0.0)
            if node > 0:
                links = links - dot_halves(halves(reduced), halves(parent_ref[node - 1]))
            out_ref[:, node * width : (node + 1) * width] = links
            reduced = links

    return kernel_call(
        kernel,
        "link_chain",
        limit=LINK_LIMIT,
        out_shape=jax.ShapeDtypeStruct((rows, nodes * width), jnp.float32),
        in_specs=at_home(2) + [pl.BlockSpec(memory_space=pltpu.SMEM)],
        out_specs=in_vmem(1)[0],
        scratch_shapes=[
            pltpu.VMEM(anc_links.shape, jnp.float32),
            pltpu.VMEM(parent_links.shape, jnp.float32),
            pltpu.SemaphoreType.DMA((nodes,)),
        ],
    )(anc_links, parent_links, pattern)


def window_of(count, rows):
    columns = (count // 2 + 1) * rows
    return columns, -(-columns // 128) * 128


def whole_message(turned, theirs, links):
    rows, half = theirs.shape
    columns, lanes = window_of(2 * half // rows, rows)

    def kernel(turned_ref, theirs_ref, links_ref, own_ref, out_ref):
        me = lax.axis_index("row")
        low = me < PCOL
        own_ref[:, :half] = jnp.where(low, turned_ref[:rows], theirs_ref[...])
        own_ref[:, half:] = jnp.where(low, theirs_ref[...], turned_ref[rows:])
        lane = lax.broadcasted_iota(jnp.int32, (1, lanes), 1)
        weight = jnp.where((lane < rows) | (lane >= columns - rows), 0.5, 1.0)
        weight = jnp.where(lane < columns, weight, 0.0)
        out_ref[:, :lanes] = pltpu.roll(own_ref[...], lax.rem(2 * half - me * rows, 2 * half), 1)[:, :lanes] * weight
        out_ref[:, lanes:] = links_ref[...]

    shapes = [(rows, 2 * half), (rows, lanes + links.shape[1])]
    return kernel_call(
        kernel,
        "whole_message",
        out_shape=[jax.ShapeDtypeStruct(shape, jnp.float32) for shape in shapes],
        in_specs=in_vmem(3),
        out_specs=in_vmem(2),
    )(turned, theirs, links)


def inner_chain(parent_links, pivot_inverse):
    nodes, width, _ = pivot_inverse.shape

    def kernel(parent_ref, pivot_ref, cross_ref, inner_ref):
        inner = pivot_ref[0]
        inner_ref[0] = inner
        for node in range(1, nodes):
            link = halves(parent_ref[node - 1])
            cross = dot_halves(halves(inner), link)
            cross_ref[node - 1] = -cross
            inner = pivot_ref[node] + dot_halves(link, halves(cross), ((0,), (0,)))
            inner_ref[node] = inner

    return kernel_call(
        kernel,
        "inner_chain",
        out_shape=[jax.ShapeDtypeStruct(array.shape, jnp.float32) for array in (parent_links, pivot_inverse)],
        in_specs=in_vmem(2),
        out_specs=in_vmem(2),
    )(parent_links, pivot_inverse)


def ring_owner(my_index, count, shift, other):
    core = lax.rem(my_index, 2)
    chip = my_index // 2
    place = jnp.where(lax.rem(chip, 2) == 0, chip // 2, count - 1 - chip // 2)
    place = lax.rem(place + shift + count, count)
    chip = jnp.where(place < count // 2, 2 * place, 2 * (count - 1 - place) + 1)
    return 2 * chip + (1 - core if other else core)


def border(arrivals, state, parents, diagonals, chips, own=None):
    last, begin = own is not None, state is None
    nodes, width, _ = diagonals.shape
    rows, total_lanes = arrivals[0][2].shape
    lanes = total_lanes - nodes * width
    order = 2 * chips * rows
    count = len(arrivals)
    fresh = rows * count
    bf16 = jnp.bfloat16

    def kernel(*refs):
        refs = list(refs)
        take = lambda number: [refs.pop(0) for _ in range(number)]
        part_refs, own_ref = take(count), take(last)
        kept_before = take(0 if begin else 1)
        held_before = take(0 if begin else 2)
        parents_ref, diagonals_ref, parents_out, diagonals_out = take(4)
        copies = []

        def finish(place, source, target):
            if last:
                copies.append(pltpu.make_async_copy(source, target, sems.at[place]))
                copies[-1].start()

        parents_end, diagonals_end = parents_out, diagonals_out
        panel_end = take(last)
        kept_now = take(not last)
        held_now = take(2)
        turned = take(2)
        if last:
            parents_out, diagonals_out, panel_out, sems = take(4)
        me = lax.axis_index("row")
        owners = [ring_owner(me, chips, shift, other) for shift, other, _ in arrivals]
        starts = [pl.multiple_of(owner * rows, 16) for owner in owners]

        for part, whole in enumerate(held_now):
            whole[...] = jnp.zeros(whole.shape, bf16) if begin else held_before[part][...]
        for start, ref in zip(starts, part_refs):
            for whole, part in zip(held_now, halves(ref[:, lanes:])):
                whole[pl.ds(start, rows), :] = part
        rest = jnp.zeros((rows, order - lanes), jnp.float32)
        sent = [pltpu.roll(jnp.concatenate([ref[:, :lanes], rest], axis=1), start, 1) for start, ref in zip(starts, part_refs)]
        left = list(sent)
        if not begin:
            core = lax.rem(me, 2)
            for pair in range(0, count, 2):
                start = lax.div(owners[pair], 2) * (2 * rows)
                base = pl.multiple_of(lax.div(start, 128) * 128, 128)
                window = pltpu.roll(kept_before[0][:, pl.ds(base, 256)], lax.rem(256 + base - start, 256), 1)
                back = window[:, :128].T
                first, second = back[:rows], back[rows : 2 * rows]
                left[pair] += jnp.where(core == 0, first, second)
                left[pair + 1] += jnp.where(core == 0, second, first)
        if not last:
            kept_now[0][...] = jnp.zeros(kept_now[0].shape, jnp.float32) if begin else kept_before[0][...]
            for start, part in zip(starts, sent):
                kept_now[0][pl.ds(start, rows), :order] = part
        left = halves(jnp.concatenate(left + [ref[...] for ref in own_ref], axis=0))
        right = []
        for node in range(nodes):
            columns = slice(node * width, (node + 1) * width)
            image = stacked_dot(left, [whole[:, columns] for whole in held_now])
            if last:
                panel_out[:, node, :] = -image[fresh:]
            image = image[:fresh]
            there = slice(lanes + node * width, lanes + (node + 1) * width)
            new = jnp.concatenate([ref[:, there] for ref in part_refs], axis=0)
            for whole, part in zip(turned, halves(jnp.concatenate([new, image], axis=0).T)):
                whole[columns, :] = part
            right.append([jnp.concatenate(pair, axis=0) for pair in zip(halves(image), halves(new))])
        if last:
            finish(2 * nodes, panel_out, panel_end[0])
        for node in range(nodes):
            lower = max(node - 1, 0) * width
            total = stacked_dot([whole[lower : (node + 1) * width, :] for whole in turned], right[node])
            diagonals_out[node] = diagonals_ref[node] + total[-width:]
            finish(node, diagonals_out.at[node], diagonals_end.at[node])
            if node > 0:
                parents_out[node - 1] = parents_ref[node - 1] + total[:width]
                finish(nodes + node, parents_out.at[node - 1], parents_end.at[node - 1])
        for copy in copies:
            copy.wait()

    operands = [part for _, _, part in arrivals] + ([own] if last else []) + list(state or [])
    operands += [parents, diagonals]
    shapes = [jax.ShapeDtypeStruct(array.shape, jnp.float32) for array in (parents, diagonals)]
    held = [jax.ShapeDtypeStruct((order, nodes * width), bf16)] * 2
    scratch = [pltpu.VMEM((nodes * width, 2 * fresh), bf16)] * 2
    if last:
        shapes.append(jax.ShapeDtypeStruct((rows, nodes, width), jnp.float32))
        scratch = [pltpu.VMEM(shape.shape, bf16) for shape in held] + scratch
        scratch += [pltpu.VMEM(array.shape, jnp.float32) for array in shapes]
        scratch.append(pltpu.SemaphoreType.DMA((2 * nodes + 1,)))
    else:
        shapes += [jax.ShapeDtypeStruct((order, order + 128), jnp.float32)] + held
    results = kernel_call(
        kernel,
        "border" + ("_end" if last else "_begin" if begin else ""),
        out_shape=shapes,
        in_specs=in_vmem(len(operands)),
        out_specs=at_home(len(shapes)) if last else in_vmem(len(shapes)),
        scratch_shapes=scratch,
        limit=24 * 2**20 if last else 16 * 2**20,
    )(*operands)
    return results[:2], results[2:]


def gather_plan(anc_blocks, anc_links, parent_links, pivot_inverse, pattern):
    chips = lax.axis_size("row") // 2
    far = chips // 2
    ahead, behind = ring_pairs(chips, 1), ring_pairs(chips, -1)
    across = [p for p in ahead if p[0] % 2 == 0] + [p for p in behind if p[0] % 2 == 1]

    def move(pair):
        return [lax.ppermute(value, "row", way) for value, way in zip(pair, (ahead, behind))]

    def both(shift, value):
        return [(shift, False, value), (shift, True, swap_bit(value, 0))]

    turned = anc_blocks[0].T
    theirs = partner_rows(turned)
    links = link_chain(after(anc_links, theirs), parent_links, pattern)
    rows, own = whole_message(turned, swap_bit(theirs, PCOL.bit_length() - 1), links)
    totals, state = inner_chain(after(parent_links, own), pivot_inverse), None
    arrivals, pair = both(0, own), [own] * 2
    for step in range(1, far):
        pair = move(pair)
        totals, state = border(arrivals, state, *totals, chips)
        pair = [after(value, *totals) for value in pair]
        arrivals = both(-step, pair[0]) + both(step, pair[1])
    last, totals = lax.optimization_barrier((pick(pair), totals))
    totals, state = border(arrivals, state, *totals, chips)
    last, totals = lax.optimization_barrier((lax.ppermute(last, "row", across), totals))
    totals, panels = border(both(far, last), state, *totals, chips, rows)
    return panels[0], *totals


def spread_plan(anc_blocks, anc_links, parent_links, pivot_inverse, pattern):
    my_index = lax.axis_index("row")
    total_bits = lax.axis_size("row").bit_length() - 1
    low_bits = PCOL.bit_length() - 1
    rows, nodes, width = anc_links.shape
    links = jnp.concatenate(reduced_links(masked_links(my_index, anc_links, pattern), parent_links), axis=1)
    segment = links
    for bit in range(low_bits, total_bits):
        partner = swap_bit(segment, bit)
        upper = my_index >> bit & 1
        segment = lax.dynamic_update_slice_in_dim(
            jnp.concatenate([partner, partner], 0), segment, upper * segment.shape[0], 0
        )
    image = product(anc_blocks[0], segment)
    for bit in reversed(range(low_bits)):
        half_rows = image.shape[0] // 2
        upper = my_index >> bit & 1
        retained = lax.dynamic_slice_in_dim(image, upper * half_rows, half_rows, 0)
        outgoing = lax.dynamic_slice_in_dim(image, (1 - upper) * half_rows, half_rows, 0)
        image = retained + swap_bit(outgoing, bit)
    column = lambda array, node: array[:, node * width : (node + 1) * width]
    terms = [inner_product(column(links, node), column(image, node)) for node in range(nodes)]
    terms += [inner_product(column(links, node - 1), column(image, node)) for node in range(1, nodes)]
    totals = lax.psum(jnp.stack(terms), "row")
    inner, cross = local_chain(parent_links, pivot_inverse)
    diagonals = jnp.stack(inner) + totals[:nodes]
    parents = totals[nodes:] - jnp.stack(cross)
    return -image.reshape(rows, nodes, width), parents, diagonals


def on_device(anc_blocks, anc_links, parent_links, pivot_inverse, pattern):
    size = lax.axis_size("row")
    rows, nodes, width = anc_links.shape
    whole_bytes = 4 * size * rows * (nodes * width + size * rows)
    plan = gather_plan if size == 2 * PCOL and whole_bytes <= GATHER_LIMIT else spread_plan
    return plan(anc_blocks, anc_links, parent_links, pivot_inverse, pattern)


def solution(mesh):
    return jax.shard_map(
        on_device,
        mesh=mesh,
        in_specs=(
            P(("pole", "row"), None, None),
            P(("pole", "row"), None, None),
            P("pole", None, None),
            P("pole", None, None),
            P(),
        ),
        out_specs=(P(("pole", "row"), None, None), P("pole", None, None), P("pole", None, None)),
        check_vma=False,
    )
```

```python
import jax
import jax.numpy as jnp
from jax import lax
from jax.experimental import pallas as pl
from jax.experimental.pallas import tpu as pltpu
from jax.sharding import PartitionSpec as P

PCOL = 8
TILE = 128
GATHER_LIMIT = 16 * 2**20
FIRST_FLOPS = 4_000_000_000


def product(left, right):
    return jnp.dot(left, right, precision=lax.Precision.HIGH, preferred_element_type=jnp.float32)


def inner_product(left, right):
    return lax.dot_general(
        left,
        right,
        (((0,), (0,)), ((), ())),
        precision=lax.Precision.HIGH,
        preferred_element_type=jnp.float32,
    )


def swap_bit(value, bit):
    mask = 2**bit
    return lax.ppermute(value, "row", [(i, i ^ mask) for i in range(lax.axis_size("row"))])


def ring_chips(count):
    return list(range(0, count, 2)) + list(range(count - 1, 0, -2))


def ring_pairs(count, shift):
    order = ring_chips(count)
    pairs = []
    for place, chip in enumerate(order):
        target = order[(place + shift) % count]
        pairs += [(2 * chip + core, 2 * target + core) for core in range(2)]
    return pairs


def masked_links(my_index, anc_links, pattern):
    rows_here = anc_links.shape[0]
    tile_index = (my_index * rows_here + jnp.arange(rows_here, dtype=jnp.int32)) // TILE
    row_keep = jnp.take(pattern, tile_index, axis=1) != 0
    return jnp.where(row_keep[:, :, None], jnp.swapaxes(anc_links, 0, 1), 0.0)


def reduced_links(links, parent_links):
    reduced = [links[0]]
    for node in range(1, links.shape[0]):
        reduced.append(links[node] - product(reduced[-1], parent_links[node - 1]))
    return reduced


def local_chain(parent_links, pivot_inverse):
    inner = [pivot_inverse[0]]
    cross = []
    for node in range(1, pivot_inverse.shape[0]):
        link = parent_links[node - 1]
        cross.append(product(inner[-1], link))
        inner.append(pivot_inverse[node] + inner_product(link, cross[-1]))
    return inner, cross


def halves(value):
    high = value.astype(jnp.bfloat16)
    return high, (value - high.astype(jnp.float32)).astype(jnp.bfloat16)


def dot_halves(left, right, dims=((1,), (0,))):
    def one(a, b):
        return lax.dot_general(a, b, (dims, ((), ())), preferred_element_type=jnp.float32)

    return one(left[0], right[0]) + (one(left[0], right[1]) + one(left[1], right[0]))


def stacked_dot(left, right):
    height = left[0].shape[0]
    both = jnp.dot(jnp.concatenate(left, axis=0), right[0], preferred_element_type=jnp.float32)
    cross = jnp.dot(left[0], right[1], preferred_element_type=jnp.float32)
    return both[:height] + (both[height:] + cross)


def kernel_call(kernel, name, limit=16 * 2**20, flops=0, **more):
    return pl.pallas_call(
        kernel,
        name=name,
        compiler_params=pltpu.CompilerParams(vmem_limit_bytes=limit),
        cost_estimate=pl.CostEstimate(flops=flops, bytes_accessed=0, transcendentals=0),
        **more,
    )


def in_vmem(count):
    return [pl.BlockSpec(memory_space=pltpu.VMEM)] * count


def after(value, *others):
    return lax.optimization_barrier((value, *others))[0]


def at_home(count):
    return [pl.BlockSpec(memory_space=pltpu.HBM)] * count


def partner_rows(turned):
    rows, columns = turned.shape[0] // 2, turned.shape[1]

    def kernel(turned_ref, out_ref):
        out_ref[...] = jnp.where(lax.axis_index("row") < PCOL, turned_ref[rows:], turned_ref[:rows])

    return kernel_call(
        kernel,
        "partner_rows",
        flops=FIRST_FLOPS,
        out_shape=jax.ShapeDtypeStruct((rows, columns), jnp.float32),
        in_specs=in_vmem(1),
        out_specs=in_vmem(1)[0],
    )(turned)


def pick(pair):
    def kernel(first_ref, second_ref, out_ref):
        out_ref[...] = jnp.where(lax.rem(lax.axis_index("row"), 2) == 0, first_ref[...], second_ref[...])

    return kernel_call(
        kernel,
        "pick",
        out_shape=jax.ShapeDtypeStruct(pair[0].shape, jnp.float32),
        in_specs=in_vmem(2),
        out_specs=in_vmem(1)[0],
    )(*pair)


def link_chain(anc_links, parent_links, pattern):
    rows, nodes, width = anc_links.shape
    tiles = pattern.shape[1]

    def kernel(links_ref, parent_ref, pattern_ref, out_ref):
        first = lax.axis_index("row") * rows
        tile = first // TILE
        next_tile = jnp.minimum(tile + 1, tiles - 1)
        row = first + lax.broadcasted_iota(jnp.int32, (rows, width), 0)
        in_first = row < (tile + 1) * TILE
        reduced = None
        for node in range(nodes):
            keep = jnp.where(in_first, pattern_ref[node, tile], pattern_ref[node, next_tile])
            links = jnp.where(keep != 0, links_ref[:, node, :], 0.0)
            if node > 0:
                links = links - dot_halves(halves(reduced), halves(parent_ref[node - 1]))
            out_ref[:, node * width : (node + 1) * width] = links
            reduced = links

    return kernel_call(
        kernel,
        "link_chain",
        out_shape=jax.ShapeDtypeStruct((rows, nodes * width), jnp.float32),
        in_specs=in_vmem(2) + [pl.BlockSpec(memory_space=pltpu.SMEM)],
        out_specs=in_vmem(1)[0],
    )(anc_links, parent_links, pattern)


def window_of(count, rows):
    columns = (count // 2 + 1) * rows
    return columns, -(-columns // 128) * 128


def whole_message(turned, theirs, links):
    rows, half = theirs.shape
    columns, lanes = window_of(2 * half // rows, rows)

    def kernel(turned_ref, theirs_ref, links_ref, own_ref, out_ref):
        me = lax.axis_index("row")
        low = me < PCOL
        own_ref[:, :half] = jnp.where(low, turned_ref[:rows], theirs_ref[...])
        own_ref[:, half:] = jnp.where(low, theirs_ref[...], turned_ref[rows:])
        lane = lax.broadcasted_iota(jnp.int32, (1, lanes), 1)
        weight = jnp.where((lane < rows) | (lane >= columns - rows), 0.5, 1.0)
        weight = jnp.where(lane < columns, weight, 0.0)
        out_ref[:, :lanes] = pltpu.roll(own_ref[...], lax.rem(2 * half - me * rows, 2 * half), 1)[:, :lanes] * weight
        out_ref[:, lanes:] = links_ref[...]

    shapes = [(rows, 2 * half), (rows, lanes + links.shape[1])]
    return kernel_call(
        kernel,
        "whole_message",
        out_shape=[jax.ShapeDtypeStruct(shape, jnp.float32) for shape in shapes],
        in_specs=in_vmem(3),
        out_specs=in_vmem(2),
    )(turned, theirs, links)


def inner_chain(parent_links, pivot_inverse):
    nodes, width, _ = pivot_inverse.shape

    def kernel(parent_ref, pivot_ref, cross_ref, inner_ref):
        inner = pivot_ref[0]
        inner_ref[0] = inner
        for node in range(1, nodes):
            link = halves(parent_ref[node - 1])
            cross = dot_halves(halves(inner), link)
            cross_ref[node - 1] = -cross
            inner = pivot_ref[node] + dot_halves(link, halves(cross), ((0,), (0,)))
            inner_ref[node] = inner

    return kernel_call(
        kernel,
        "inner_chain",
        out_shape=[jax.ShapeDtypeStruct(array.shape, jnp.float32) for array in (parent_links, pivot_inverse)],
        in_specs=in_vmem(2),
        out_specs=in_vmem(2),
    )(parent_links, pivot_inverse)


def ring_owner(my_index, count, shift, other):
    core = lax.rem(my_index, 2)
    chip = my_index // 2
    place = jnp.where(lax.rem(chip, 2) == 0, chip // 2, count - 1 - chip // 2)
    place = lax.rem(place + shift + count, count)
    chip = jnp.where(place < count // 2, 2 * place, 2 * (count - 1 - place) + 1)
    return 2 * chip + (1 - core if other else core)


def border(arrivals, state, parents, diagonals, chips, own=None):
    last, begin = own is not None, state is None
    nodes, width, _ = diagonals.shape
    rows, total_lanes = arrivals[0][2].shape
    lanes = total_lanes - nodes * width
    order = 2 * chips * rows
    count = len(arrivals)
    fresh = rows * count
    bf16 = jnp.bfloat16

    def kernel(*refs):
        refs = list(refs)
        take = lambda number: [refs.pop(0) for _ in range(number)]
        part_refs, own_ref = take(count), take(last)
        kept_before = take(0 if begin else 1)
        held_before = take(0 if begin else 2)
        parents_ref, diagonals_ref, parents_out, diagonals_out = take(4)
        copies = []

        def finish(place, source, target):
            if last:
                copies.append(pltpu.make_async_copy(source, target, sems.at[place]))
                copies[-1].start()

        parents_end, diagonals_end = parents_out, diagonals_out
        panel_end = take(last)
        kept_now = take(not last)
        held_now = take(2)
        turned = take(2)
        if last:
            parents_out, diagonals_out, panel_out, sems = take(4)
        me = lax.axis_index("row")
        owners = [ring_owner(me, chips, shift, other) for shift, other, _ in arrivals]
        starts = [pl.multiple_of(owner * rows, 16) for owner in owners]

        for part, whole in enumerate(held_now):
            whole[...] = jnp.zeros(whole.shape, bf16) if begin else held_before[part][...]
        for start, ref in zip(starts, part_refs):
            for whole, part in zip(held_now, halves(ref[:, lanes:])):
                whole[pl.ds(start, rows), :] = part
        rest = jnp.zeros((rows, order - lanes), jnp.float32)
        sent = [pltpu.roll(jnp.concatenate([ref[:, :lanes], rest], axis=1), start, 1) for start, ref in zip(starts, part_refs)]
        left = list(sent)
        if not begin:
            core = lax.rem(me, 2)
            for pair in range(0, count, 2):
                start = lax.div(owners[pair], 2) * (2 * rows)
                base = pl.multiple_of(lax.div(start, 128) * 128, 128)
                window = pltpu.roll(kept_before[0][:, pl.ds(base, 256)], lax.rem(256 + base - start, 256), 1)
                back = window[:, :128].T
                first, second = back[:rows], back[rows : 2 * rows]
                left[pair] += jnp.where(core == 0, first, second)
                left[pair + 1] += jnp.where(core == 0, second, first)
        if not last:
            kept_now[0][...] = jnp.zeros(kept_now[0].shape, jnp.float32) if begin else kept_before[0][...]
            for start, part in zip(starts, sent):
                kept_now[0][pl.ds(start, rows), :order] = part
        left = halves(jnp.concatenate(left + [ref[...] for ref in own_ref], axis=0))
        right = []
        for node in range(nodes):
            columns = slice(node * width, (node + 1) * width)
            image = stacked_dot(left, [whole[:, columns] for whole in held_now])
            if last:
                panel_out[:, node, :] = -image[fresh:]
            image = image[:fresh]
            there = slice(lanes + node * width, lanes + (node + 1) * width)
            new = jnp.concatenate([ref[:, there] for ref in part_refs], axis=0)
            for whole, part in zip(turned, halves(jnp.concatenate([new, image], axis=0).T)):
                whole[columns, :] = part
            right.append([jnp.concatenate(pair, axis=0) for pair in zip(halves(image), halves(new))])
        if last:
            finish(2 * nodes, panel_out, panel_end[0])
        for node in range(nodes):
            lower = max(node - 1, 0) * width
            total = stacked_dot([whole[lower : (node + 1) * width, :] for whole in turned], right[node])
            diagonals_out[node] = diagonals_ref[node] + total[-width:]
            finish(node, diagonals_out.at[node], diagonals_end.at[node])
            if node > 0:
                parents_out[node - 1] = parents_ref[node - 1] + total[:width]
                finish(nodes + node, parents_out.at[node - 1], parents_end.at[node - 1])
        for copy in copies:
            copy.wait()

    operands = [part for _, _, part in arrivals] + ([own] if last else []) + list(state or [])
    operands += [parents, diagonals]
    shapes = [jax.ShapeDtypeStruct(array.shape, jnp.float32) for array in (parents, diagonals)]
    held = [jax.ShapeDtypeStruct((order, nodes * width), bf16)] * 2
    scratch = [pltpu.VMEM((nodes * width, 2 * fresh), bf16)] * 2
    if last:
        shapes.append(jax.ShapeDtypeStruct((rows, nodes, width), jnp.float32))
        scratch = [pltpu.VMEM(shape.shape, bf16) for shape in held] + scratch
        scratch += [pltpu.VMEM(array.shape, jnp.float32) for array in shapes]
        scratch.append(pltpu.SemaphoreType.DMA((2 * nodes + 1,)))
    else:
        shapes += [jax.ShapeDtypeStruct((order, order + 128), jnp.float32)] + held
    results = kernel_call(
        kernel,
        "border" + ("_end" if last else "_begin" if begin else ""),
        out_shape=shapes,
        in_specs=in_vmem(len(operands)),
        out_specs=at_home(len(shapes)) if last else in_vmem(len(shapes)),
        scratch_shapes=scratch,
        limit=24 * 2**20 if last else 16 * 2**20,
    )(*operands)
    return results[:2], results[2:]


def gather_plan(anc_blocks, anc_links, parent_links, pivot_inverse, pattern):
    chips = lax.axis_size("row") // 2
    far = chips // 2
    ahead, behind = ring_pairs(chips, 1), ring_pairs(chips, -1)
    across = [p for p in ahead if p[0] % 2 == 0] + [p for p in behind if p[0] % 2 == 1]

    def move(pair):
        return [lax.ppermute(value, "row", way) for value, way in zip(pair, (ahead, behind))]

    def both(shift, value):
        return [(shift, False, value), (shift, True, swap_bit(value, 0))]

    turned = anc_blocks[0].T
    theirs = partner_rows(turned)
    links = link_chain(after(anc_links, theirs), parent_links, pattern)
    rows, own = whole_message(turned, swap_bit(theirs, PCOL.bit_length() - 1), links)
    totals, state = inner_chain(after(parent_links, own), pivot_inverse), None
    arrivals, pair = both(0, own), [own] * 2
    for step in range(1, far):
        pair = move(pair)
        totals, state = border(arrivals, state, *totals, chips)
        pair = [after(value, *totals) for value in pair]
        arrivals = both(-step, pair[0]) + both(step, pair[1])
    last, totals = lax.optimization_barrier((pick(pair), totals))
    totals, state = border(arrivals, state, *totals, chips)
    last, totals = lax.optimization_barrier((lax.ppermute(last, "row", across), totals))
    totals, panels = border(both(far, last), state, *totals, chips, rows)
    return panels[0], *totals


def spread_plan(anc_blocks, anc_links, parent_links, pivot_inverse, pattern):
    my_index = lax.axis_index("row")
    total_bits = lax.axis_size("row").bit_length() - 1
    low_bits = PCOL.bit_length() - 1
    rows, nodes, width = anc_links.shape
    links = jnp.concatenate(reduced_links(masked_links(my_index, anc_links, pattern), parent_links), axis=1)
    segment = links
    for bit in range(low_bits, total_bits):
        partner = swap_bit(segment, bit)
        upper = my_index >> bit & 1
        segment = lax.dynamic_update_slice_in_dim(
            jnp.concatenate([partner, partner], 0), segment, upper * segment.shape[0], 0
        )
    image = product(anc_blocks[0], segment)
    for bit in reversed(range(low_bits)):
        half_rows = image.shape[0] // 2
        upper = my_index >> bit & 1
        retained = lax.dynamic_slice_in_dim(image, upper * half_rows, half_rows, 0)
        outgoing = lax.dynamic_slice_in_dim(image, (1 - upper) * half_rows, half_rows, 0)
        image = retained + swap_bit(outgoing, bit)
    column = lambda array, node: array[:, node * width : (node + 1) * width]
    terms = [inner_product(column(links, node), column(image, node)) for node in range(nodes)]
    terms += [inner_product(column(links, node - 1), column(image, node)) for node in range(1, nodes)]
    totals = lax.psum(jnp.stack(terms), "row")
    inner, cross = local_chain(parent_links, pivot_inverse)
    diagonals = jnp.stack(inner) + totals[:nodes]
    parents = totals[nodes:] - jnp.stack(cross)
    return -image.reshape(rows, nodes, width), parents, diagonals


def on_device(anc_blocks, anc_links, parent_links, pivot_inverse, pattern):
    size = lax.axis_size("row")
    rows, nodes, width = anc_links.shape
    whole_bytes = 4 * size * rows * (nodes * width + size * rows)
    plan = gather_plan if size == 2 * PCOL and whole_bytes <= GATHER_LIMIT else spread_plan
    return plan(anc_blocks, anc_links, parent_links, pivot_inverse, pattern)


def solution(mesh):
    return jax.shard_map(
        on_device,
        mesh=mesh,
        in_specs=(
            P(("pole", "row"), None, None),
            P(("pole", "row"), None, None),
            P("pole", None, None),
            P("pole", None, None),
            P(),
        ),
        out_specs=(P(("pole", "row"), None, None), P("pole", None, None), P("pole", None, None)),
        check_vma=False,
    )
```

```python
import jax
import jax.numpy as jnp
from jax import lax
from jax.experimental import pallas as pl
from jax.experimental.pallas import tpu as pltpu
from jax.sharding import PartitionSpec as P

PCOL = 8
TILE = 128
GATHER_LIMIT = 16 * 2**20
SIDE = 256
FIRST_FLOPS = 4_000_000_000


def product(left, right):
    return jnp.dot(left, right, precision=lax.Precision.HIGH, preferred_element_type=jnp.float32)


def inner_product(left, right):
    return lax.dot_general(
        left,
        right,
        (((0,), (0,)), ((), ())),
        precision=lax.Precision.HIGH,
        preferred_element_type=jnp.float32,
    )


def swap_bit(value, bit):
    mask = 2**bit
    return lax.ppermute(value, "row", [(i, i ^ mask) for i in range(lax.axis_size("row"))])


def ring_chips(count):
    return list(range(0, count, 2)) + list(range(count - 1, 0, -2))


def ring_pairs(count, shift):
    order = ring_chips(count)
    pairs = []
    for place, chip in enumerate(order):
        target = order[(place + shift) % count]
        pairs += [(2 * chip + core, 2 * target + core) for core in range(2)]
    return pairs


def masked_links(my_index, anc_links, pattern):
    rows_here = anc_links.shape[0]
    tile_index = (my_index * rows_here + jnp.arange(rows_here, dtype=jnp.int32)) // TILE
    row_keep = jnp.take(pattern, tile_index, axis=1) != 0
    return jnp.where(row_keep[:, :, None], jnp.swapaxes(anc_links, 0, 1), 0.0)


def reduced_links(links, parent_links):
    reduced = [links[0]]
    for node in range(1, links.shape[0]):
        reduced.append(links[node] - product(reduced[-1], parent_links[node - 1]))
    return reduced


def local_chain(parent_links, pivot_inverse):
    inner = [pivot_inverse[0]]
    cross = []
    for node in range(1, pivot_inverse.shape[0]):
        link = parent_links[node - 1]
        cross.append(product(inner[-1], link))
        inner.append(pivot_inverse[node] + inner_product(link, cross[-1]))
    return inner, cross


def halves(value):
    high = value.astype(jnp.bfloat16)
    return high, (value - high.astype(jnp.float32)).astype(jnp.bfloat16)


def dot_halves(left, right, dims=((1,), (0,))):
    def one(a, b):
        return lax.dot_general(a, b, (dims, ((), ())), preferred_element_type=jnp.float32)

    return one(left[0], right[0]) + (one(left[0], right[1]) + one(left[1], right[0]))


def stacked_dot(left, right):
    height = left[0].shape[0]
    both = jnp.dot(jnp.concatenate(left, axis=0), right[0], preferred_element_type=jnp.float32)
    cross = jnp.dot(left[0], right[1], preferred_element_type=jnp.float32)
    return both[:height] + (both[height:] + cross)


def kernel_call(kernel, name, limit=16 * 2**20, flops=0, **more):
    return pl.pallas_call(
        kernel,
        name=name,
        compiler_params=pltpu.CompilerParams(vmem_limit_bytes=limit),
        cost_estimate=pl.CostEstimate(flops=flops, bytes_accessed=0, transcendentals=0),
        **more,
    )


def in_vmem(count):
    return [pl.BlockSpec(memory_space=pltpu.VMEM)] * count


def after(value, *others):
    return lax.optimization_barrier((value, *others))[0]


def at_home(count):
    return [pl.BlockSpec(memory_space=pltpu.HBM)] * count


def far_rows(turned):
    rows, columns = turned.shape[0] // 2, turned.shape[1]

    def kernel(turned_ref, out_ref):
        me = lax.axis_index("row")
        low = me < PCOL
        theirs = jnp.where(low, turned_ref[rows:], turned_ref[:rows])
        first = lax.rem(me, PCOL) + jnp.where(low, 1, 0)
        out_ref[...] = pltpu.roll(theirs, lax.rem(columns - lax.rem(first, PCOL) * rows, columns), 1)[:, : columns // 2]

    return kernel_call(
        kernel,
        "far_rows",
        flops=FIRST_FLOPS,
        out_shape=jax.ShapeDtypeStruct((rows, columns // 2), jnp.float32),
        in_specs=in_vmem(1),
        out_specs=in_vmem(1)[0],
    )(turned)


def pick(pair):
    def kernel(first_ref, second_ref, out_ref):
        out_ref[...] = jnp.where(lax.rem(lax.axis_index("row"), 2) == 0, first_ref[...], second_ref[...])

    return kernel_call(
        kernel,
        "pick",
        out_shape=jax.ShapeDtypeStruct(pair[0].shape, jnp.float32),
        in_specs=in_vmem(2),
        out_specs=in_vmem(1)[0],
    )(*pair)


def link_chain(anc_links, parent_links, pattern):
    rows, nodes, width = anc_links.shape
    tiles = pattern.shape[1]

    def kernel(links_ref, parent_ref, pattern_ref, out_ref):
        first = lax.axis_index("row") * rows
        tile = first // TILE
        next_tile = jnp.minimum(tile + 1, tiles - 1)
        row = first + lax.broadcasted_iota(jnp.int32, (rows, width), 0)
        in_first = row < (tile + 1) * TILE
        reduced = None
        for node in range(nodes):
            keep = jnp.where(in_first, pattern_ref[node, tile], pattern_ref[node, next_tile])
            links = jnp.where(keep != 0, links_ref[:, node, :], 0.0)
            if node > 0:
                links = links - dot_halves(halves(reduced), halves(parent_ref[node - 1]))
            out_ref[:, node * width : (node + 1) * width] = links
            reduced = links

    return kernel_call(
        kernel,
        "link_chain",
        out_shape=jax.ShapeDtypeStruct((rows, nodes * width), jnp.float32),
        in_specs=in_vmem(2) + [pl.BlockSpec(memory_space=pltpu.SMEM)],
        out_specs=in_vmem(1)[0],
    )(anc_links, parent_links, pattern)


def message_of(turned, far, links):
    rows, columns = turned.shape[0] // 2, turned.shape[1]
    near = columns // 2 + rows

    def kernel(turned_ref, far_ref, links_ref, out_ref):
        me = lax.axis_index("row")
        mine = jnp.where(me < PCOL, turned_ref[:rows], turned_ref[rows:])
        mine = pltpu.roll(mine, lax.rem(columns - lax.rem(me, PCOL) * rows, columns), 1)[:, :SIDE]
        lane = lax.broadcasted_iota(jnp.int32, (1, SIDE), 1)
        weight = jnp.where((lane < rows) | (lane >= near - rows), 0.5, 1.0)
        out_ref[:, :SIDE] = mine * jnp.where(lane < near, weight, 0.0)
        out_ref[:, SIDE : 2 * SIDE] = jnp.zeros((rows, SIDE), jnp.float32)
        out_ref[:, SIDE : SIDE + columns // 2] = far_ref[...]
        out_ref[:, 2 * SIDE :] = links_ref[...]

    return kernel_call(
        kernel,
        "message",
        out_shape=jax.ShapeDtypeStruct((rows, 2 * SIDE + links.shape[1]), jnp.float32),
        in_specs=in_vmem(3),
        out_specs=in_vmem(1)[0],
    )(turned, far, links)


def sent_rows(sides, owner, rows):
    columns = PCOL * rows
    rest = jnp.zeros((rows, columns - SIDE), jnp.float32)
    piece, low = lax.rem(owner, PCOL), owner < PCOL
    first = lax.rem(piece + jnp.where(low, 0, 1), PCOL)
    near = pltpu.roll(jnp.concatenate([sides[:, :SIDE], rest], axis=1), piece * rows, 1)
    far = pltpu.roll(jnp.concatenate([sides[:, SIDE:], rest], axis=1), first * rows, 1)
    return jnp.concatenate([jnp.where(low, near, far), jnp.where(low, far, near)], axis=1)


def columns_at(ref, start, count):
    base = pl.multiple_of(lax.div(start, 128) * 128, 128)
    return pltpu.roll(ref[:, pl.ds(base, 256)], lax.rem(256 + base - start, 256), 1)[:, :128]


def inner_chain(parent_links, pivot_inverse):
    nodes, width, _ = pivot_inverse.shape

    def kernel(parent_ref, pivot_ref, cross_ref, inner_ref):
        inner = pivot_ref[0]
        inner_ref[0] = inner
        for node in range(1, nodes):
            link = halves(parent_ref[node - 1])
            cross = dot_halves(halves(inner), link)
            cross_ref[node - 1] = -cross
            inner = pivot_ref[node] + dot_halves(link, halves(cross), ((0,), (0,)))
            inner_ref[node] = inner

    return kernel_call(
        kernel,
        "inner_chain",
        out_shape=[jax.ShapeDtypeStruct(array.shape, jnp.float32) for array in (parent_links, pivot_inverse)],
        in_specs=in_vmem(2),
        out_specs=in_vmem(2),
    )(parent_links, pivot_inverse)


def ring_owner(my_index, count, shift, other):
    core = lax.rem(my_index, 2)
    chip = my_index // 2
    place = jnp.where(lax.rem(chip, 2) == 0, chip // 2, count - 1 - chip // 2)
    place = lax.rem(place + shift + count, count)
    chip = jnp.where(place < count // 2, 2 * place, 2 * (count - 1 - place) + 1)
    return 2 * chip + (1 - core if other else core)


def border(arrivals, state, parents, diagonals, chips, last=False):
    begin = state is None
    nodes, width, _ = diagonals.shape
    rows = arrivals[0][2].shape[0]
    lanes = 2 * SIDE
    order = 2 * chips * rows
    count = len(arrivals)
    fresh = rows * count
    bf16, f32 = jnp.bfloat16, jnp.float32

    def kernel(*refs):
        refs = list(refs)
        take = lambda number: [refs.pop(0) for _ in range(number)]
        part_refs = take(count)
        panel_before, kept_before, *held_before = take(4) if not begin else [None] * 4
        parents_ref, diagonals_ref, parents_out, diagonals_out, panel_out = take(5)
        copies = []

        def finish(place, source, target):
            if last:
                copies.append(pltpu.make_async_copy(source, target, sems.at[place]))
                copies[-1].start()

        parents_end, diagonals_end, panel_end = parents_out, diagonals_out, panel_out
        kept_now = None if last else take(1)[0]
        held_now = take(2)
        turned, beside, aside = take(3)
        if last:
            parents_out, diagonals_out, panel_out, sems = take(4)
        me = lax.axis_index("row")
        core = lax.rem(me, 2)
        owners = [ring_owner(me, chips, shift, other) for shift, other, _ in arrivals]
        starts = [pl.multiple_of(owner * rows, 16) for owner in owners]

        for part, whole in enumerate(held_now):
            whole[...] = jnp.zeros(whole.shape, bf16) if begin else held_before[part][...]
        for start, ref in zip(starts, part_refs):
            for whole, part in zip(held_now, halves(ref[:, lanes:])):
                whole[pl.ds(start, rows), :] = part
        sent = [sent_rows(ref[:, :lanes], owner, rows) for owner, ref in zip(owners, part_refs)]
        if not last:
            kept_now[...] = jnp.zeros(kept_now.shape, f32) if begin else kept_before[...]
            for start, part in zip(starts, sent):
                kept_now[pl.ds(start, rows), :order] = part
        if not begin:
            for pair in range(0, count, 2):
                back = columns_at(kept_before, lax.div(owners[pair], 2) * (2 * rows), 2 * rows).T
                first, second = back[:rows], back[rows : 2 * rows]
                sent[pair] += jnp.where(core == 0, first, second)
                sent[pair + 1] += jnp.where(core == 0, second, first)
        left = jnp.concatenate(sent, axis=0)
        aside[:, :order] = left
        aside[:, order:] = jnp.zeros((fresh, 128), f32)
        across = columns_at(aside, me * rows, rows).T[:rows]
        if begin:
            pair = columns_at(aside, lax.div(me, 2) * (2 * rows), 2 * rows)[:rows]
            swapped = jnp.concatenate([pair[:, rows : 2 * rows], pair[:, :rows]], axis=1)
            across += jnp.where(core == 0, pair[:, : 2 * rows], swapped)
        left, across = halves(left), halves(across)
        for node in range(nodes):
            columns = slice(node * width, (node + 1) * width)
            image = stacked_dot(left, [whole[:, columns] for whole in held_now])
            there = slice(lanes + node * width, lanes + (node + 1) * width)
            new = jnp.concatenate([ref[:, there] for ref in part_refs], axis=0)
            new_high, new_low = halves(new)
            image_high, image_low = halves(image)
            own = stacked_dot(across, [new_high, new_low])
            if not begin:
                own += panel_before[:, columns]
            if last:
                panel_out[:, node, :] = -own
            else:
                panel_out[:, columns] = own
            high, low = halves(jnp.concatenate([new, image], axis=0).T)
            for place, part in enumerate((high, low, high)):
                turned[columns, 2 * fresh * place : 2 * fresh * (place + 1)] = part
            for place, part in enumerate((image_high, new_high, image_high, new_high, image_low, new_low)):
                beside[fresh * place : fresh * (place + 1), columns] = part
        if last:
            finish(2 * nodes, panel_out, panel_end)
        for node in range(nodes):
            lower = max(node - 1, 0) * width
            columns = slice(node * width, (node + 1) * width)
            total = jnp.dot(turned[lower : columns.stop, :], beside[:, columns], preferred_element_type=f32)
            diagonals_out[node] = diagonals_ref[node] + total[-width:]
            finish(node, diagonals_out.at[node], diagonals_end.at[node])
            if node > 0:
                parents_out[node - 1] = parents_ref[node - 1] + total[:width]
                finish(nodes + node, parents_out.at[node - 1], parents_end.at[node - 1])
        for copy in copies:
            copy.wait()

    operands = [part for _, _, part in arrivals] + list(state or []) + [parents, diagonals]
    shape_of = jax.ShapeDtypeStruct
    shapes = [shape_of(parents.shape, f32), shape_of(diagonals.shape, f32)]
    held = [shape_of((order, nodes * width), bf16)] * 2
    scratch = [((nodes * width, 6 * fresh), bf16), ((6 * fresh, nodes * width), bf16), ((fresh, order + 128), f32)]
    scratch = [pltpu.VMEM(*shape) for shape in scratch]
    if last:
        shapes.append(shape_of((rows, nodes, width), f32))
        scratch = [pltpu.VMEM(shape.shape, bf16) for shape in held] + scratch
        scratch += [pltpu.VMEM(shape.shape, f32) for shape in shapes]
        scratch.append(pltpu.SemaphoreType.DMA((2 * nodes + 1,)))
    else:
        shapes += [shape_of((rows, nodes * width), f32), shape_of((order, order + 128), f32)] + held
    results = kernel_call(
        kernel,
        "border" + ("_end" if last else "_begin" if begin else ""),
        out_shape=shapes,
        in_specs=in_vmem(len(operands)),
        out_specs=at_home(len(shapes)) if last else in_vmem(len(shapes)),
        scratch_shapes=scratch,
        limit=(24 if last else 16) * 2**20,
    )(*operands)
    return results[:2], results[2:]


def gather_plan(anc_blocks, anc_links, parent_links, pivot_inverse, pattern):
    chips = lax.axis_size("row") // 2
    far = chips // 2
    ahead, behind = ring_pairs(chips, 1), ring_pairs(chips, -1)
    across = [p for p in ahead if p[0] % 2 == 0] + [p for p in behind if p[0] % 2 == 1]

    def move(pair):
        return [lax.ppermute(value, "row", way) for value, way in zip(pair, (ahead, behind))]

    def both(shift, value):
        return [(shift, False, value), (shift, True, swap_bit(value, 0))]

    turned = anc_blocks[0].T
    far_part = far_rows(turned)
    links = link_chain(after(anc_links, far_part), parent_links, pattern)
    own = message_of(turned, swap_bit(far_part, PCOL.bit_length() - 1), links)
    totals, state = inner_chain(after(parent_links, own), pivot_inverse), None
    arrivals, pair = both(0, own), [own] * 2
    for step in range(1, far):
        pair = move(pair)
        totals, state = border(arrivals, state, *totals, chips)
        pair = [after(value, *totals) for value in pair]
        arrivals = both(-step, pair[0]) + both(step, pair[1])
    last, totals = lax.optimization_barrier((pick(pair), totals))
    totals, state = border(arrivals, state, *totals, chips)
    last, totals = lax.optimization_barrier((lax.ppermute(last, "row", across), totals))
    totals, panels = border(both(far, last), state, *totals, chips, True)
    return panels[0], *totals


def spread_plan(anc_blocks, anc_links, parent_links, pivot_inverse, pattern):
    my_index = lax.axis_index("row")
    total_bits = lax.axis_size("row").bit_length() - 1
    low_bits = PCOL.bit_length() - 1
    rows, nodes, width = anc_links.shape
    links = jnp.concatenate(reduced_links(masked_links(my_index, anc_links, pattern), parent_links), axis=1)
    segment = links
    for bit in range(low_bits, total_bits):
        partner = swap_bit(segment, bit)
        upper = my_index >> bit & 1
        segment = lax.dynamic_update_slice_in_dim(
            jnp.concatenate([partner, partner], 0), segment, upper * segment.shape[0], 0
        )
    image = product(anc_blocks[0], segment)
    for bit in reversed(range(low_bits)):
        half_rows = image.shape[0] // 2
        upper = my_index >> bit & 1
        retained = lax.dynamic_slice_in_dim(image, upper * half_rows, half_rows, 0)
        outgoing = lax.dynamic_slice_in_dim(image, (1 - upper) * half_rows, half_rows, 0)
        image = retained + swap_bit(outgoing, bit)
    column = lambda array, node: array[:, node * width : (node + 1) * width]
    terms = [inner_product(column(links, node), column(image, node)) for node in range(nodes)]
    terms += [inner_product(column(links, node - 1), column(image, node)) for node in range(1, nodes)]
    totals = lax.psum(jnp.stack(terms), "row")
    inner, cross = local_chain(parent_links, pivot_inverse)
    diagonals = jnp.stack(inner) + totals[:nodes]
    parents = totals[nodes:] - jnp.stack(cross)
    return -image.reshape(rows, nodes, width), parents, diagonals


def on_device(anc_blocks, anc_links, parent_links, pivot_inverse, pattern):
    size = lax.axis_size("row")
    rows, nodes, width = anc_links.shape
    whole_bytes = 4 * size * rows * (nodes * width + size * rows)
    plan = gather_plan if size == 2 * PCOL and whole_bytes <= GATHER_LIMIT else spread_plan
    return plan(anc_blocks, anc_links, parent_links, pivot_inverse, pattern)


def solution(mesh):
    return jax.shard_map(
        on_device,
        mesh=mesh,
        in_specs=(
            P(("pole", "row"), None, None),
            P(("pole", "row"), None, None),
            P("pole", None, None),
            P("pole", None, None),
            P(),
        ),
        out_specs=(P(("pole", "row"), None, None), P("pole", None, None), P("pole", None, None)),
        check_vma=False,
    )
```

```python
import jax
import jax.numpy as jnp
from jax import lax
from jax.experimental import pallas as pl
from jax.experimental.pallas import tpu as pltpu
from jax.sharding import PartitionSpec as P

PCOL = 8
TILE = 128
GATHER_LIMIT = 16 * 2**20
SIDE = 256
FIRST_FLOPS = 4_000_000_000


def product(left, right):
    return jnp.dot(left, right, precision=lax.Precision.HIGH, preferred_element_type=jnp.float32)


def inner_product(left, right):
    return lax.dot_general(
        left,
        right,
        (((0,), (0,)), ((), ())),
        precision=lax.Precision.HIGH,
        preferred_element_type=jnp.float32,
    )


def swap_bit(value, bit):
    mask = 2**bit
    return lax.ppermute(value, "row", [(i, i ^ mask) for i in range(lax.axis_size("row"))])


def ring_chips(count):
    return list(range(0, count, 2)) + list(range(count - 1, 0, -2))


def ring_pairs(count, shift):
    order = ring_chips(count)
    pairs = []
    for place, chip in enumerate(order):
        target = order[(place + shift) % count]
        pairs += [(2 * chip + core, 2 * target + core) for core in range(2)]
    return pairs


def masked_links(my_index, anc_links, pattern):
    rows_here = anc_links.shape[0]
    tile_index = (my_index * rows_here + jnp.arange(rows_here, dtype=jnp.int32)) // TILE
    row_keep = jnp.take(pattern, tile_index, axis=1) != 0
    return jnp.where(row_keep[:, :, None], jnp.swapaxes(anc_links, 0, 1), 0.0)


def reduced_links(links, parent_links):
    reduced = [links[0]]
    for node in range(1, links.shape[0]):
        reduced.append(links[node] - product(reduced[-1], parent_links[node - 1]))
    return reduced


def local_chain(parent_links, pivot_inverse):
    inner = [pivot_inverse[0]]
    cross = []
    for node in range(1, pivot_inverse.shape[0]):
        link = parent_links[node - 1]
        cross.append(product(inner[-1], link))
        inner.append(pivot_inverse[node] + inner_product(link, cross[-1]))
    return inner, cross


def halves(value):
    high = value.astype(jnp.bfloat16)
    return high, (value - high.astype(jnp.float32)).astype(jnp.bfloat16)


def dot_halves(left, right, dims=((1,), (0,))):
    def one(a, b):
        return lax.dot_general(a, b, (dims, ((), ())), preferred_element_type=jnp.float32)

    return one(left[0], right[0]) + (one(left[0], right[1]) + one(left[1], right[0]))


def stacked_dot(left, right):
    height = left[0].shape[0]
    both = jnp.dot(jnp.concatenate(left, axis=0), right[0], preferred_element_type=jnp.float32)
    cross = jnp.dot(left[0], right[1], preferred_element_type=jnp.float32)
    return both[:height] + (both[height:] + cross)


def kernel_call(kernel, name, limit=16 * 2**20, flops=0, **more):
    return pl.pallas_call(
        kernel,
        name=name,
        compiler_params=pltpu.CompilerParams(vmem_limit_bytes=limit),
        cost_estimate=pl.CostEstimate(flops=flops, bytes_accessed=0, transcendentals=0),
        **more,
    )


def in_vmem(count):
    return [pl.BlockSpec(memory_space=pltpu.VMEM)] * count


def after(value, *others):
    return lax.optimization_barrier((value, *others))[0]


def at_home(count):
    return [pl.BlockSpec(memory_space=pltpu.HBM)] * count


def far_rows(turned):
    rows, columns = turned.shape[0] // 2, turned.shape[1]

    def kernel(turned_ref, out_ref):
        me = lax.axis_index("row")
        low = me < PCOL
        theirs = jnp.where(low, turned_ref[rows:], turned_ref[:rows])
        first = lax.rem(me, PCOL) + jnp.where(low, 1, 0)
        out_ref[...] = pltpu.roll(theirs, lax.rem(columns - lax.rem(first, PCOL) * rows, columns), 1)[:, : columns // 2]

    return kernel_call(
        kernel,
        "far_rows",
        flops=FIRST_FLOPS,
        out_shape=jax.ShapeDtypeStruct((rows, columns // 2), jnp.float32),
        in_specs=in_vmem(1),
        out_specs=in_vmem(1)[0],
    )(turned)


def split(pair):
    rows, columns = pair[0].shape

    def kernel(*refs):
        for place, ref in enumerate(refs[:2]):
            refs[2 + 2 * place][...] = ref[:, : columns // 2]
            refs[3 + 2 * place][...] = ref[:, columns // 2 :]

    shape = jax.ShapeDtypeStruct((rows, columns // 2), jnp.float32)
    parts = kernel_call(kernel, "split", out_shape=[shape] * 4, in_specs=in_vmem(2), out_specs=in_vmem(4))(*pair)
    return parts[:2], parts[2:]


def pick(pair):
    def kernel(first_ref, second_ref, out_ref):
        out_ref[...] = jnp.where(lax.rem(lax.axis_index("row"), 2) == 0, first_ref[...], second_ref[...])

    return kernel_call(
        kernel,
        "pick",
        out_shape=jax.ShapeDtypeStruct(pair[0].shape, jnp.float32),
        in_specs=in_vmem(2),
        out_specs=in_vmem(1)[0],
    )(*pair)


def link_chain(anc_links, parent_links, pattern):
    rows, nodes, width = anc_links.shape
    tiles = pattern.shape[1]

    def kernel(links_ref, parent_ref, pattern_ref, out_ref):
        first = lax.axis_index("row") * rows
        tile = first // TILE
        next_tile = jnp.minimum(tile + 1, tiles - 1)
        row = first + lax.broadcasted_iota(jnp.int32, (rows, width), 0)
        in_first = row < (tile + 1) * TILE
        reduced = None
        for node in range(nodes):
            keep = jnp.where(in_first, pattern_ref[node, tile], pattern_ref[node, next_tile])
            links = jnp.where(keep != 0, links_ref[:, node, :], 0.0)
            if node > 0:
                links = links - dot_halves(halves(reduced), halves(parent_ref[node - 1]))
            out_ref[:, node * width : (node + 1) * width] = links
            reduced = links

    return kernel_call(
        kernel,
        "link_chain",
        out_shape=jax.ShapeDtypeStruct((rows, nodes * width), jnp.float32),
        in_specs=in_vmem(2) + [pl.BlockSpec(memory_space=pltpu.SMEM)],
        out_specs=in_vmem(1)[0],
    )(anc_links, parent_links, pattern)


def message_of(turned, far, links):
    rows, columns = turned.shape[0] // 2, turned.shape[1]
    near = columns // 2 + rows

    def kernel(turned_ref, far_ref, links_ref, out_ref):
        me = lax.axis_index("row")
        mine = jnp.where(me < PCOL, turned_ref[:rows], turned_ref[rows:])
        mine = pltpu.roll(mine, lax.rem(columns - lax.rem(me, PCOL) * rows, columns), 1)[:, :SIDE]
        lane = lax.broadcasted_iota(jnp.int32, (1, SIDE), 1)
        weight = jnp.where((lane < rows) | (lane >= near - rows), 0.5, 1.0)
        out_ref[:, :SIDE] = mine * jnp.where(lane < near, weight, 0.0)
        out_ref[:, SIDE : 2 * SIDE] = jnp.zeros((rows, SIDE), jnp.float32)
        out_ref[:, SIDE : SIDE + columns // 2] = far_ref[...]
        out_ref[:, 2 * SIDE :] = links_ref[...]

    return kernel_call(
        kernel,
        "message",
        out_shape=jax.ShapeDtypeStruct((rows, 2 * SIDE + links.shape[1]), jnp.float32),
        in_specs=in_vmem(3),
        out_specs=in_vmem(1)[0],
    )(turned, far, links)


def sent_rows(sides, owner, rows):
    columns = PCOL * rows
    rest = jnp.zeros((rows, columns - SIDE), jnp.float32)
    piece, low = lax.rem(owner, PCOL), owner < PCOL
    first = lax.rem(piece + jnp.where(low, 0, 1), PCOL)
    near = pltpu.roll(jnp.concatenate([sides[:, :SIDE], rest], axis=1), piece * rows, 1)
    far = pltpu.roll(jnp.concatenate([sides[:, SIDE:], rest], axis=1), first * rows, 1)
    return jnp.concatenate([jnp.where(low, near, far), jnp.where(low, far, near)], axis=1)


def columns_at(ref, start, count):
    base = pl.multiple_of(lax.div(start, 128) * 128, 128)
    return pltpu.roll(ref[:, pl.ds(base, 256)], lax.rem(256 + base - start, 256), 1)[:, :128]


def inner_chain(parent_links, pivot_inverse):
    nodes, width, _ = pivot_inverse.shape

    def kernel(parent_ref, pivot_ref, cross_ref, inner_ref):
        inner = pivot_ref[0]
        inner_ref[0] = inner
        for node in range(1, nodes):
            link = halves(parent_ref[node - 1])
            cross = dot_halves(halves(inner), link)
            cross_ref[node - 1] = -cross
            inner = pivot_ref[node] + dot_halves(link, halves(cross), ((0,), (0,)))
            inner_ref[node] = inner

    return kernel_call(
        kernel,
        "inner_chain",
        out_shape=[jax.ShapeDtypeStruct(array.shape, jnp.float32) for array in (parent_links, pivot_inverse)],
        in_specs=in_vmem(2),
        out_specs=in_vmem(2),
    )(parent_links, pivot_inverse)


def ring_owner(my_index, count, shift, other):
    core = lax.rem(my_index, 2)
    chip = my_index // 2
    place = jnp.where(lax.rem(chip, 2) == 0, chip // 2, count - 1 - chip // 2)
    place = lax.rem(place + shift + count, count)
    chip = jnp.where(place < count // 2, 2 * place, 2 * (count - 1 - place) + 1)
    return 2 * chip + (1 - core if other else core)


class Parts:
    def __init__(self, refs):
        self.refs = refs

    def columns(self, first, stop):
        for ref in self.refs:
            if first < ref.shape[1]:
                return ref[:, first:stop]
            first, stop = first - ref.shape[1], stop - ref.shape[1]

    def pieces(self, skip):
        first = -skip
        for ref in self.refs:
            yield max(first, 0), ref[:, max(-first, 0) :]
            first += ref.shape[1]


def border(arrivals, state, parents, diagonals, chips, last=False):
    begin = state is None
    nodes, width, _ = diagonals.shape
    rows = arrivals[0][2][0].shape[0]
    lanes = 2 * SIDE
    order = 2 * chips * rows
    count = len(arrivals)
    fresh = rows * count
    bf16, f32 = jnp.bfloat16, jnp.float32

    def kernel(*refs):
        refs = list(refs)
        take = lambda number: [refs.pop(0) for _ in range(number)]
        part_refs = [Parts(take(len(parts))) for _, _, parts in arrivals]
        panel_before, kept_before, *held_before = take(4) if not begin else [None] * 4
        parents_ref, diagonals_ref, parents_out, diagonals_out, panel_out = take(5)
        copies = []

        def finish(place, source, target):
            if last:
                copies.append(pltpu.make_async_copy(source, target, sems.at[place]))
                copies[-1].start()

        parents_end, diagonals_end, panel_end = parents_out, diagonals_out, panel_out
        kept_now = None if last else take(1)[0]
        held_now = take(2)
        turned, beside, aside = take(3)
        if last:
            parents_out, diagonals_out, panel_out, sems = take(4)
        me = lax.axis_index("row")
        core = lax.rem(me, 2)
        owners = [ring_owner(me, chips, shift, other) for shift, other, _ in arrivals]
        starts = [pl.multiple_of(owner * rows, 16) for owner in owners]

        for part, whole in enumerate(held_now):
            whole[...] = jnp.zeros(whole.shape, bf16) if begin else held_before[part][...]
        for start, ref in zip(starts, part_refs):
            for first, part in ref.pieces(lanes):
                for whole, half in zip(held_now, halves(part)):
                    whole[pl.ds(start, rows), first : first + part.shape[1]] = half
        sent = [sent_rows(ref.columns(0, lanes), owner, rows) for owner, ref in zip(owners, part_refs)]
        if not last:
            kept_now[...] = jnp.zeros(kept_now.shape, f32) if begin else kept_before[...]
            for start, part in zip(starts, sent):
                kept_now[pl.ds(start, rows), :order] = part
        if not begin:
            for pair in range(0, count, 2):
                back = columns_at(kept_before, lax.div(owners[pair], 2) * (2 * rows), 2 * rows).T
                first, second = back[:rows], back[rows : 2 * rows]
                sent[pair] += jnp.where(core == 0, first, second)
                sent[pair + 1] += jnp.where(core == 0, second, first)
        left = jnp.concatenate(sent, axis=0)
        aside[:, :order] = left
        aside[:, order:] = jnp.zeros((fresh, 128), f32)
        across = columns_at(aside, me * rows, rows).T[:rows]
        if begin:
            pair = columns_at(aside, lax.div(me, 2) * (2 * rows), 2 * rows)[:rows]
            swapped = jnp.concatenate([pair[:, rows : 2 * rows], pair[:, :rows]], axis=1)
            across += jnp.where(core == 0, pair[:, : 2 * rows], swapped)
        left, across = halves(left), halves(across)
        for node in range(nodes):
            columns = slice(node * width, (node + 1) * width)
            image = stacked_dot(left, [whole[:, columns] for whole in held_now])
            first = lanes + node * width
            new = jnp.concatenate([ref.columns(first, first + width) for ref in part_refs], axis=0)
            new_high, new_low = halves(new)
            image_high, image_low = halves(image)
            own = stacked_dot(across, [new_high, new_low])
            if not begin:
                own += panel_before[:, columns]
            if last:
                panel_out[:, node, :] = -own
            else:
                panel_out[:, columns] = own
            high, low = halves(jnp.concatenate([new, image], axis=0).T)
            for place, part in enumerate((high, low, high)):
                turned[columns, 2 * fresh * place : 2 * fresh * (place + 1)] = part
            for place, part in enumerate((image_high, new_high, image_high, new_high, image_low, new_low)):
                beside[fresh * place : fresh * (place + 1), columns] = part
        if last:
            finish(2 * nodes, panel_out, panel_end)
        for node in range(nodes):
            lower = max(node - 1, 0) * width
            columns = slice(node * width, (node + 1) * width)
            total = jnp.dot(turned[lower : columns.stop, :], beside[:, columns], preferred_element_type=f32)
            diagonals_out[node] = diagonals_ref[node] + total[-width:]
            finish(node, diagonals_out.at[node], diagonals_end.at[node])
            if node > 0:
                parents_out[node - 1] = parents_ref[node - 1] + total[:width]
                finish(nodes + node, parents_out.at[node - 1], parents_end.at[node - 1])
        for copy in copies:
            copy.wait()

    operands = [part for _, _, parts in arrivals for part in parts] + list(state or []) + [parents, diagonals]
    shape_of = jax.ShapeDtypeStruct
    shapes = [shape_of(parents.shape, f32), shape_of(diagonals.shape, f32)]
    held = [shape_of((order, nodes * width), bf16)] * 2
    scratch = [((nodes * width, 6 * fresh), bf16), ((6 * fresh, nodes * width), bf16), ((fresh, order + 128), f32)]
    scratch = [pltpu.VMEM(*shape) for shape in scratch]
    if last:
        shapes.append(shape_of((rows, nodes, width), f32))
        scratch = [pltpu.VMEM(shape.shape, bf16) for shape in held] + scratch
        scratch += [pltpu.VMEM(shape.shape, f32) for shape in shapes]
        scratch.append(pltpu.SemaphoreType.DMA((2 * nodes + 1,)))
    else:
        shapes += [shape_of((rows, nodes * width), f32), shape_of((order, order + 128), f32)] + held
    results = kernel_call(
        kernel,
        "border" + ("_end" if last else "_begin" if begin else ""),
        out_shape=shapes,
        in_specs=in_vmem(len(operands)),
        out_specs=at_home(len(shapes)) if last else in_vmem(len(shapes)),
        scratch_shapes=scratch,
        limit=(24 if last else 16) * 2**20,
    )(*operands)
    return results[:2], results[2:]


def gather_plan(anc_blocks, anc_links, parent_links, pivot_inverse, pattern):
    chips = lax.axis_size("row") // 2
    far = chips // 2
    ahead, behind = ring_pairs(chips, 1), ring_pairs(chips, -1)
    across = [p for p in ahead if p[0] % 2 == 0] + [p for p in behind if p[0] % 2 == 1]

    def move(pair):
        return [lax.ppermute(value, "row", way) for value, way in zip(pair, (ahead, behind))]

    def both(shift, value, parts=None):
        parts = [swap_bit(part, 0) for part in parts or [value]]
        return [(shift, False, [value]), (shift, True, parts)]

    turned = anc_blocks[0].T
    far_part = far_rows(turned)
    links = link_chain(after(anc_links, far_part), parent_links, pattern)
    own = message_of(turned, swap_bit(far_part, PCOL.bit_length() - 1), links)
    totals, state = inner_chain(after(parent_links, own), pivot_inverse), None
    arrivals, pair = both(0, own), [own] * 2
    for step in range(1, far):
        pair = move(pair)
        totals, state = border(arrivals, state, *totals, chips)
        pair = [after(value, *totals) for value in pair]
        parts = split(pair)
        arrivals = both(-step, pair[0], parts[0]) + both(step, pair[1], parts[1])
    last, totals = lax.optimization_barrier((pick(pair), totals))
    totals, state = border(arrivals, state, *totals, chips)
    last, totals = lax.optimization_barrier((lax.ppermute(last, "row", across), totals))
    totals, panels = border(both(far, last), state, *totals, chips, True)
    return panels[0], *totals


def spread_plan(anc_blocks, anc_links, parent_links, pivot_inverse, pattern):
    my_index = lax.axis_index("row")
    total_bits = lax.axis_size("row").bit_length() - 1
    low_bits = PCOL.bit_length() - 1
    rows, nodes, width = anc_links.shape
    links = jnp.concatenate(reduced_links(masked_links(my_index, anc_links, pattern), parent_links), axis=1)
    segment = links
    for bit in range(low_bits, total_bits):
        partner = swap_bit(segment, bit)
        upper = my_index >> bit & 1
        segment = lax.dynamic_update_slice_in_dim(
            jnp.concatenate([partner, partner], 0), segment, upper * segment.shape[0], 0
        )
    image = product(anc_blocks[0], segment)
    for bit in reversed(range(low_bits)):
        half_rows = image.shape[0] // 2
        upper = my_index >> bit & 1
        retained = lax.dynamic_slice_in_dim(image, upper * half_rows, half_rows, 0)
        outgoing = lax.dynamic_slice_in_dim(image, (1 - upper) * half_rows, half_rows, 0)
        image = retained + swap_bit(outgoing, bit)
    column = lambda array, node: array[:, node * width : (node + 1) * width]
    terms = [inner_product(column(links, node), column(image, node)) for node in range(nodes)]
    terms += [inner_product(column(links, node - 1), column(image, node)) for node in range(1, nodes)]
    totals = lax.psum(jnp.stack(terms), "row")
    inner, cross = local_chain(parent_links, pivot_inverse)
    diagonals = jnp.stack(inner) + totals[:nodes]
    parents = totals[nodes:] - jnp.stack(cross)
    return -image.reshape(rows, nodes, width), parents, diagonals


def on_device(anc_blocks, anc_links, parent_links, pivot_inverse, pattern):
    size = lax.axis_size("row")
    rows, nodes, width = anc_links.shape
    whole_bytes = 4 * size * rows * (nodes * width + size * rows)
    plan = gather_plan if size == 2 * PCOL and whole_bytes <= GATHER_LIMIT else spread_plan
    return plan(anc_blocks, anc_links, parent_links, pivot_inverse, pattern)


def solution(mesh):
    return jax.shard_map(
        on_device,
        mesh=mesh,
        in_specs=(
            P(("pole", "row"), None, None),
            P(("pole", "row"), None, None),
            P("pole", None, None),
            P("pole", None, None),
            P(),
        ),
        out_specs=(P(("pole", "row"), None, None), P("pole", None, None), P("pole", None, None)),
        check_vma=False,
    )
```

```python
import jax
import jax.numpy as jnp
from jax import lax
from jax.experimental import pallas as pl
from jax.experimental.pallas import tpu as pltpu
from jax.sharding import PartitionSpec as P

PCOL = 8
TILE = 128
GATHER_LIMIT = 16 * 2**20
SIDE = 256
FIRST_FLOPS = 4_000_000_000


def product(left, right):
    return jnp.dot(left, right, precision=lax.Precision.HIGH, preferred_element_type=jnp.float32)


def inner_product(left, right):
    return lax.dot_general(
        left,
        right,
        (((0,), (0,)), ((), ())),
        precision=lax.Precision.HIGH,
        preferred_element_type=jnp.float32,
    )


def swap_bit(value, bit):
    mask = 2**bit
    return lax.ppermute(value, "row", [(i, i ^ mask) for i in range(lax.axis_size("row"))])


def ring_chips(count):
    return list(range(0, count, 2)) + list(range(count - 1, 0, -2))


def ring_pairs(count, shift):
    order = ring_chips(count)
    pairs = []
    for place, chip in enumerate(order):
        target = order[(place + shift) % count]
        pairs += [(2 * chip + core, 2 * target + core) for core in range(2)]
    return pairs


def masked_links(my_index, anc_links, pattern):
    rows_here = anc_links.shape[0]
    tile_index = (my_index * rows_here + jnp.arange(rows_here, dtype=jnp.int32)) // TILE
    row_keep = jnp.take(pattern, tile_index, axis=1) != 0
    return jnp.where(row_keep[:, :, None], jnp.swapaxes(anc_links, 0, 1), 0.0)


def reduced_links(links, parent_links):
    reduced = [links[0]]
    for node in range(1, links.shape[0]):
        reduced.append(links[node] - product(reduced[-1], parent_links[node - 1]))
    return reduced


def local_chain(parent_links, pivot_inverse):
    inner = [pivot_inverse[0]]
    cross = []
    for node in range(1, pivot_inverse.shape[0]):
        link = parent_links[node - 1]
        cross.append(product(inner[-1], link))
        inner.append(pivot_inverse[node] + inner_product(link, cross[-1]))
    return inner, cross


def halves(value):
    high = value.astype(jnp.bfloat16)
    return high, (value - high.astype(jnp.float32)).astype(jnp.bfloat16)


def dot_halves(left, right, dims=((1,), (0,))):
    def one(a, b):
        return lax.dot_general(a, b, (dims, ((), ())), preferred_element_type=jnp.float32)

    return one(left[0], right[0]) + (one(left[0], right[1]) + one(left[1], right[0]))


def stacked_dot(left, right):
    height = left[0].shape[0]
    both = jnp.dot(jnp.concatenate(left, axis=0), right[0], preferred_element_type=jnp.float32)
    cross = jnp.dot(left[0], right[1], preferred_element_type=jnp.float32)
    return both[:height] + (both[height:] + cross)


def kernel_call(kernel, name, limit=16 * 2**20, flops=0, **more):
    return pl.pallas_call(
        kernel,
        name=name,
        compiler_params=pltpu.CompilerParams(vmem_limit_bytes=limit),
        cost_estimate=pl.CostEstimate(flops=flops, bytes_accessed=0, transcendentals=0),
        **more,
    )


def in_vmem(count):
    return [pl.BlockSpec(memory_space=pltpu.VMEM)] * count


def after(value, *others):
    return lax.optimization_barrier((value, *others))[0]


def at_home(count):
    return [pl.BlockSpec(memory_space=pltpu.HBM)] * count


def far_rows(turned):
    rows, columns = turned.shape[0] // 2, turned.shape[1]

    def kernel(turned_ref, out_ref):
        me = lax.axis_index("row")
        low = me < PCOL
        theirs = jnp.where(low, turned_ref[rows:], turned_ref[:rows])
        first = lax.rem(me, PCOL) + jnp.where(low, 1, 0)
        out_ref[...] = pltpu.roll(theirs, lax.rem(columns - lax.rem(first, PCOL) * rows, columns), 1)[:, : columns // 2]

    return kernel_call(
        kernel,
        "far_rows",
        flops=FIRST_FLOPS,
        out_shape=jax.ShapeDtypeStruct((rows, columns // 2), jnp.float32),
        in_specs=in_vmem(1),
        out_specs=in_vmem(1)[0],
    )(turned)


def pick(pair):
    def kernel(first_ref, second_ref, out_ref):
        out_ref[...] = jnp.where(lax.rem(lax.axis_index("row"), 2) == 0, first_ref[...], second_ref[...])

    return kernel_call(
        kernel,
        "pick",
        out_shape=jax.ShapeDtypeStruct(pair[0].shape, jnp.float32),
        in_specs=in_vmem(2),
        out_specs=in_vmem(1)[0],
    )(*pair)


def link_chain(anc_links, parent_links, pattern):
    rows, nodes, width = anc_links.shape
    tiles = pattern.shape[1]

    def kernel(links_ref, parent_ref, pattern_ref, out_ref):
        first = lax.axis_index("row") * rows
        tile = first // TILE
        next_tile = jnp.minimum(tile + 1, tiles - 1)
        row = first + lax.broadcasted_iota(jnp.int32, (rows, width), 0)
        in_first = row < (tile + 1) * TILE
        reduced = None
        for node in range(nodes):
            keep = jnp.where(in_first, pattern_ref[node, tile], pattern_ref[node, next_tile])
            links = jnp.where(keep != 0, links_ref[:, node, :], 0.0)
            if node > 0:
                links = links - dot_halves(halves(reduced), halves(parent_ref[node - 1]))
            out_ref[:, node * width : (node + 1) * width] = links
            reduced = links

    return kernel_call(
        kernel,
        "link_chain",
        out_shape=jax.ShapeDtypeStruct((rows, nodes * width), jnp.float32),
        in_specs=in_vmem(2) + [pl.BlockSpec(memory_space=pltpu.SMEM)],
        out_specs=in_vmem(1)[0],
    )(anc_links, parent_links, pattern)


def message_of(turned, far, links):
    rows, columns = turned.shape[0] // 2, turned.shape[1]
    near = columns // 2 + rows

    def kernel(turned_ref, far_ref, links_ref, out_ref):
        me = lax.axis_index("row")
        mine = jnp.where(me < PCOL, turned_ref[:rows], turned_ref[rows:])
        mine = pltpu.roll(mine, lax.rem(columns - lax.rem(me, PCOL) * rows, columns), 1)[:, :SIDE]
        lane = lax.broadcasted_iota(jnp.int32, (1, SIDE), 1)
        weight = jnp.where((lane < rows) | (lane >= near - rows), 0.5, 1.0)
        out_ref[:, :SIDE] = mine * jnp.where(lane < near, weight, 0.0)
        out_ref[:, SIDE : 2 * SIDE] = jnp.zeros((rows, SIDE), jnp.float32)
        out_ref[:, SIDE : SIDE + columns // 2] = far_ref[...]
        out_ref[:, 2 * SIDE :] = links_ref[...]

    return kernel_call(
        kernel,
        "message",
        out_shape=jax.ShapeDtypeStruct((rows, 2 * SIDE + links.shape[1]), jnp.float32),
        in_specs=in_vmem(3),
        out_specs=in_vmem(1)[0],
    )(turned, far, links)


def sent_rows(sides, owner, rows):
    columns = PCOL * rows
    rest = jnp.zeros((rows, columns - SIDE), jnp.float32)
    piece, low = lax.rem(owner, PCOL), owner < PCOL
    first = lax.rem(piece + jnp.where(low, 0, 1), PCOL)
    near = pltpu.roll(jnp.concatenate([sides[:, :SIDE], rest], axis=1), piece * rows, 1)
    far = pltpu.roll(jnp.concatenate([sides[:, SIDE:], rest], axis=1), first * rows, 1)
    return jnp.concatenate([jnp.where(low, near, far), jnp.where(low, far, near)], axis=1)


def columns_at(ref, start, count):
    base = pl.multiple_of(lax.div(start, 128) * 128, 128)
    return pltpu.roll(ref[:, pl.ds(base, 256)], lax.rem(256 + base - start, 256), 1)[:, :128]


def inner_chain(parent_links, pivot_inverse):
    nodes, width, _ = pivot_inverse.shape

    def kernel(parent_ref, pivot_ref, cross_ref, inner_ref):
        inner = pivot_ref[0]
        inner_ref[0] = inner
        for node in range(1, nodes):
            link = halves(parent_ref[node - 1])
            cross = dot_halves(halves(inner), link)
            cross_ref[node - 1] = -cross
            inner = pivot_ref[node] + dot_halves(link, halves(cross), ((0,), (0,)))
            inner_ref[node] = inner

    return kernel_call(
        kernel,
        "inner_chain",
        out_shape=[jax.ShapeDtypeStruct(array.shape, jnp.float32) for array in (parent_links, pivot_inverse)],
        in_specs=in_vmem(2),
        out_specs=in_vmem(2),
    )(parent_links, pivot_inverse)


def ring_owner(my_index, count, shift, other):
    core = lax.rem(my_index, 2)
    chip = my_index // 2
    place = jnp.where(lax.rem(chip, 2) == 0, chip // 2, count - 1 - chip // 2)
    place = lax.rem(place + shift + count, count)
    chip = jnp.where(place < count // 2, 2 * place, 2 * (count - 1 - place) + 1)
    return 2 * chip + (1 - core if other else core)


def border(arrivals, state, parents, diagonals, chips, last=False):
    begin = state is None
    nodes, width, _ = diagonals.shape
    rows = arrivals[0][2].shape[0]
    lanes = 2 * SIDE
    order = 2 * chips * rows
    count = len(arrivals)
    fresh = rows * count
    bf16, f32 = jnp.bfloat16, jnp.float32

    def kernel(*refs):
        refs = list(refs)
        take = lambda number: [refs.pop(0) for _ in range(number)]
        part_refs = take(count)
        panel_before, kept_before, *held_before = take(4) if not begin else [None] * 4
        parents_ref, diagonals_ref, parents_out, diagonals_out, panel_out = take(5)
        copies = []

        def finish(place, source, target):
            if last:
                copies.append(pltpu.make_async_copy(source, target, sems.at[place]))
                copies[-1].start()

        parents_end, diagonals_end, panel_end = parents_out, diagonals_out, panel_out
        kept_now = None if last else take(1)[0]
        held_now = take(2)
        turned, beside, aside = take(3)
        if last:
            parents_out, diagonals_out, panel_out, sems = take(4)
        me = lax.axis_index("row")
        core = lax.rem(me, 2)
        owners = [ring_owner(me, chips, shift, other) for shift, other, _ in arrivals]
        starts = [pl.multiple_of(owner * rows, 16) for owner in owners]

        sent = [sent_rows(ref[:, :lanes], owner, rows) for owner, ref in zip(owners, part_refs)]
        ahead = list(sent)
        if not begin:
            for pair in range(0, count, 2):
                back = columns_at(kept_before, lax.div(owners[pair], 2) * (2 * rows), 2 * rows).T
                first, second = back[:rows], back[rows : 2 * rows]
                sent[pair] = sent[pair] + jnp.where(core == 0, first, second)
                sent[pair + 1] = sent[pair + 1] + jnp.where(core == 0, second, first)
        left = jnp.concatenate(sent, axis=0)
        aside[:, :order] = left
        aside[:, order:] = jnp.zeros((fresh, 128), f32)
        across = columns_at(aside, me * rows, rows).T[:rows]
        if begin:
            pair = columns_at(aside, lax.div(me, 2) * (2 * rows), 2 * rows)[:rows]
            swapped = jnp.concatenate([pair[:, rows : 2 * rows], pair[:, :rows]], axis=1)
            across += jnp.where(core == 0, pair[:, : 2 * rows], swapped)
        left, across = halves(left), halves(across)
        for node in range(nodes):
            columns = slice(node * width, (node + 1) * width)
            there = slice(lanes + node * width, lanes + (node + 1) * width)
            new = jnp.concatenate([ref[:, there] for ref in part_refs], axis=0)
            new_high, new_low = halves(new)
            for part, (whole, values) in enumerate(zip(held_now, (new_high, new_low))):
                whole[:, columns] = jnp.zeros((order, width), bf16) if begin else held_before[part][:, columns]
                for place, start in enumerate(starts):
                    whole[pl.ds(start, rows), columns] = values[place * rows : (place + 1) * rows]
            image = stacked_dot(left, [whole[:, columns] for whole in held_now])
            image_high, image_low = halves(image)
            own = stacked_dot(across, [new_high, new_low])
            if not begin:
                own += panel_before[:, columns]
            if last:
                panel_out[:, node, :] = -own
            else:
                panel_out[:, columns] = own
            high, low = halves(jnp.concatenate([new, image], axis=0).T)
            for place, part in enumerate((high, low, high)):
                turned[columns, 2 * fresh * place : 2 * fresh * (place + 1)] = part
            for place, part in enumerate((image_high, new_high, image_high, new_high, image_low, new_low)):
                beside[fresh * place : fresh * (place + 1), columns] = part
        if last:
            finish(2 * nodes, panel_out, panel_end)
        else:
            kept_now[...] = jnp.zeros(kept_now.shape, f32) if begin else kept_before[...]
            for start, part in zip(starts, ahead):
                kept_now[pl.ds(start, rows), :order] = part
        for node in range(nodes):
            lower = max(node - 1, 0) * width
            columns = slice(node * width, (node + 1) * width)
            total = jnp.dot(turned[lower : columns.stop, :], beside[:, columns], preferred_element_type=f32)
            diagonals_out[node] = diagonals_ref[node] + total[-width:]
            finish(node, diagonals_out.at[node], diagonals_end.at[node])
            if node > 0:
                parents_out[node - 1] = parents_ref[node - 1] + total[:width]
                finish(nodes + node, parents_out.at[node - 1], parents_end.at[node - 1])
        for copy in copies:
            copy.wait()

    operands = [part for _, _, part in arrivals] + list(state or []) + [parents, diagonals]
    shape_of = jax.ShapeDtypeStruct
    shapes = [shape_of(parents.shape, f32), shape_of(diagonals.shape, f32)]
    held = [shape_of((order, nodes * width), bf16)] * 2
    scratch = [((nodes * width, 6 * fresh), bf16), ((6 * fresh, nodes * width), bf16), ((fresh, order + 128), f32)]
    scratch = [pltpu.VMEM(*shape) for shape in scratch]
    if last:
        shapes.append(shape_of((rows, nodes, width), f32))
        scratch = [pltpu.VMEM(shape.shape, bf16) for shape in held] + scratch
        scratch += [pltpu.VMEM(shape.shape, f32) for shape in shapes]
        scratch.append(pltpu.SemaphoreType.DMA((2 * nodes + 1,)))
    else:
        shapes += [shape_of((rows, nodes * width), f32), shape_of((order, order + 128), f32)] + held
    results = kernel_call(
        kernel,
        "border" + ("_end" if last else "_begin" if begin else ""),
        out_shape=shapes,
        in_specs=in_vmem(len(operands)),
        out_specs=at_home(len(shapes)) if last else in_vmem(len(shapes)),
        scratch_shapes=scratch,
        limit=(24 if last else 16) * 2**20,
    )(*operands)
    return results[:2], results[2:]


def gather_plan(anc_blocks, anc_links, parent_links, pivot_inverse, pattern):
    chips = lax.axis_size("row") // 2
    far = chips // 2
    ahead, behind = ring_pairs(chips, 1), ring_pairs(chips, -1)
    across = [p for p in ahead if p[0] % 2 == 0] + [p for p in behind if p[0] % 2 == 1]

    def move(pair):
        return [lax.ppermute(value, "row", way) for value, way in zip(pair, (ahead, behind))]

    def both(shift, value):
        return [(shift, False, value), (shift, True, swap_bit(value, 0))]

    turned = anc_blocks[0].T
    far_part = far_rows(turned)
    links = link_chain(after(anc_links, far_part), parent_links, pattern)
    own = message_of(turned, swap_bit(far_part, PCOL.bit_length() - 1), links)
    totals, state = inner_chain(after(parent_links, own), pivot_inverse), None
    arrivals, pair = both(0, own), [own] * 2
    for step in range(1, far):
        pair = move(pair)
        totals, state = border(arrivals, state, *totals, chips)
        pair = [after(value, *totals) for value in pair]
        arrivals = both(-step, pair[0]) + both(step, pair[1])
    last, totals = lax.optimization_barrier((pick(pair), totals))
    totals, state = border(arrivals, state, *totals, chips)
    last, totals = lax.optimization_barrier((lax.ppermute(last, "row", across), totals))
    totals, panels = border(both(far, last), state, *totals, chips, True)
    return panels[0], *totals


def spread_plan(anc_blocks, anc_links, parent_links, pivot_inverse, pattern):
    my_index = lax.axis_index("row")
    total_bits = lax.axis_size("row").bit_length() - 1
    low_bits = PCOL.bit_length() - 1
    rows, nodes, width = anc_links.shape
    links = jnp.concatenate(reduced_links(masked_links(my_index, anc_links, pattern), parent_links), axis=1)
    segment = links
    for bit in range(low_bits, total_bits):
        partner = swap_bit(segment, bit)
        upper = my_index >> bit & 1
        segment = lax.dynamic_update_slice_in_dim(
            jnp.concatenate([partner, partner], 0), segment, upper * segment.shape[0], 0
        )
    image = product(anc_blocks[0], segment)
    for bit in reversed(range(low_bits)):
        half_rows = image.shape[0] // 2
        upper = my_index >> bit & 1
        retained = lax.dynamic_slice_in_dim(image, upper * half_rows, half_rows, 0)
        outgoing = lax.dynamic_slice_in_dim(image, (1 - upper) * half_rows, half_rows, 0)
        image = retained + swap_bit(outgoing, bit)
    column = lambda array, node: array[:, node * width : (node + 1) * width]
    terms = [inner_product(column(links, node), column(image, node)) for node in range(nodes)]
    terms += [inner_product(column(links, node - 1), column(image, node)) for node in range(1, nodes)]
    totals = lax.psum(jnp.stack(terms), "row")
    inner, cross = local_chain(parent_links, pivot_inverse)
    diagonals = jnp.stack(inner) + totals[:nodes]
    parents = totals[nodes:] - jnp.stack(cross)
    return -image.reshape(rows, nodes, width), parents, diagonals


def on_device(anc_blocks, anc_links, parent_links, pivot_inverse, pattern):
    size = lax.axis_size("row")
    rows, nodes, width = anc_links.shape
    whole_bytes = 4 * size * rows * (nodes * width + size * rows)
    plan = gather_plan if size == 2 * PCOL and whole_bytes <= GATHER_LIMIT else spread_plan
    return plan(anc_blocks, anc_links, parent_links, pivot_inverse, pattern)


def solution(mesh):
    return jax.shard_map(
        on_device,
        mesh=mesh,
        in_specs=(
            P(("pole", "row"), None, None),
            P(("pole", "row"), None, None),
            P("pole", None, None),
            P("pole", None, None),
            P(),
        ),
        out_specs=(P(("pole", "row"), None, None), P("pole", None, None), P("pole", None, None)),
        check_vma=False,
    )
```

```python
import jax
import jax.numpy as jnp
from jax import lax
from jax.experimental import pallas as pl
from jax.experimental.pallas import tpu as pltpu
from jax.sharding import PartitionSpec as P

PCOL = 8
TILE = 128
GATHER_LIMIT = 16 * 2**20
SIDE = 256
BORDER_LIMIT = 20 * 2**20
FIRST_FLOPS = 4_000_000_000


def product(left, right):
    return jnp.dot(left, right, precision=lax.Precision.HIGH, preferred_element_type=jnp.float32)


def inner_product(left, right):
    return lax.dot_general(
        left,
        right,
        (((0,), (0,)), ((), ())),
        precision=lax.Precision.HIGH,
        preferred_element_type=jnp.float32,
    )


def swap_bit(value, bit):
    mask = 2**bit
    return lax.ppermute(value, "row", [(i, i ^ mask) for i in range(lax.axis_size("row"))])


def ring_chips(count):
    return list(range(0, count, 2)) + list(range(count - 1, 0, -2))


def ring_pairs(count, shift):
    order = ring_chips(count)
    pairs = []
    for place, chip in enumerate(order):
        target = order[(place + shift) % count]
        pairs += [(2 * chip + core, 2 * target + core) for core in range(2)]
    return pairs


def masked_links(my_index, anc_links, pattern):
    rows_here = anc_links.shape[0]
    tile_index = (my_index * rows_here + jnp.arange(rows_here, dtype=jnp.int32)) // TILE
    row_keep = jnp.take(pattern, tile_index, axis=1) != 0
    return jnp.where(row_keep[:, :, None], jnp.swapaxes(anc_links, 0, 1), 0.0)


def reduced_links(links, parent_links):
    reduced = [links[0]]
    for node in range(1, links.shape[0]):
        reduced.append(links[node] - product(reduced[-1], parent_links[node - 1]))
    return reduced


def local_chain(parent_links, pivot_inverse):
    inner = [pivot_inverse[0]]
    cross = []
    for node in range(1, pivot_inverse.shape[0]):
        link = parent_links[node - 1]
        cross.append(product(inner[-1], link))
        inner.append(pivot_inverse[node] + inner_product(link, cross[-1]))
    return inner, cross


def halves(value):
    high = value.astype(jnp.bfloat16)
    return high, (value - high.astype(jnp.float32)).astype(jnp.bfloat16)


def dot_halves(left, right, dims=((1,), (0,))):
    def one(a, b):
        return lax.dot_general(a, b, (dims, ((), ())), preferred_element_type=jnp.float32)

    return one(left[0], right[0]) + (one(left[0], right[1]) + one(left[1], right[0]))


def stacked_dot(left, right):
    height = left[0].shape[0]
    both = jnp.dot(jnp.concatenate(left, axis=0), right[0], preferred_element_type=jnp.float32)
    cross = jnp.dot(left[0], right[1], preferred_element_type=jnp.float32)
    return both[:height] + (both[height:] + cross)


def kernel_call(kernel, name, limit=16 * 2**20, flops=0, **more):
    return pl.pallas_call(
        kernel,
        name=name,
        compiler_params=pltpu.CompilerParams(vmem_limit_bytes=limit),
        cost_estimate=pl.CostEstimate(flops=flops, bytes_accessed=0, transcendentals=0),
        **more,
    )


def in_vmem(count):
    return [pl.BlockSpec(memory_space=pltpu.VMEM)] * count


def after(value, *others):
    return lax.optimization_barrier((value, *others))[0]


def at_home(count):
    return [pl.BlockSpec(memory_space=pltpu.HBM)] * count


def far_rows(turned):
    rows, columns = turned.shape[0] // 2, turned.shape[1]

    def kernel(turned_ref, out_ref):
        me = lax.axis_index("row")
        low = me < PCOL
        theirs = jnp.where(low, turned_ref[rows:], turned_ref[:rows])
        first = lax.rem(me, PCOL) + jnp.where(low, 1, 0)
        out_ref[...] = pltpu.roll(theirs, lax.rem(columns - lax.rem(first, PCOL) * rows, columns), 1)[:, : columns // 2]

    return kernel_call(
        kernel,
        "far_rows",
        flops=FIRST_FLOPS,
        out_shape=jax.ShapeDtypeStruct((rows, columns // 2), jnp.float32),
        in_specs=in_vmem(1),
        out_specs=in_vmem(1)[0],
    )(turned)


def pick(pair):
    def kernel(first_ref, second_ref, out_ref):
        out_ref[...] = jnp.where(lax.rem(lax.axis_index("row"), 2) == 0, first_ref[...], second_ref[...])

    return kernel_call(
        kernel,
        "pick",
        out_shape=jax.ShapeDtypeStruct(pair[0].shape, jnp.float32),
        in_specs=in_vmem(2),
        out_specs=in_vmem(1)[0],
    )(*pair)


def link_chain(anc_links, parent_links, pattern):
    rows, nodes, width = anc_links.shape
    tiles = pattern.shape[1]

    def kernel(links_ref, parent_ref, pattern_ref, out_ref):
        first = lax.axis_index("row") * rows
        tile = first // TILE
        next_tile = jnp.minimum(tile + 1, tiles - 1)
        row = first + lax.broadcasted_iota(jnp.int32, (rows, width), 0)
        in_first = row < (tile + 1) * TILE
        reduced = None
        for node in range(nodes):
            keep = jnp.where(in_first, pattern_ref[node, tile], pattern_ref[node, next_tile])
            links = jnp.where(keep != 0, links_ref[:, node, :], 0.0)
            if node > 0:
                links = links - dot_halves(halves(reduced), halves(parent_ref[node - 1]))
            out_ref[:, node * width : (node + 1) * width] = links
            reduced = links

    return kernel_call(
        kernel,
        "link_chain",
        out_shape=jax.ShapeDtypeStruct((rows, nodes * width), jnp.float32),
        in_specs=in_vmem(2) + [pl.BlockSpec(memory_space=pltpu.SMEM)],
        out_specs=in_vmem(1)[0],
    )(anc_links, parent_links, pattern)


def message_of(turned, far, links):
    rows, columns = turned.shape[0] // 2, turned.shape[1]
    near = columns // 2 + rows

    def kernel(turned_ref, far_ref, links_ref, out_ref):
        me = lax.axis_index("row")
        mine = jnp.where(me < PCOL, turned_ref[:rows], turned_ref[rows:])
        mine = pltpu.roll(mine, lax.rem(columns - lax.rem(me, PCOL) * rows, columns), 1)[:, :SIDE]
        lane = lax.broadcasted_iota(jnp.int32, (1, SIDE), 1)
        weight = jnp.where((lane < rows) | (lane >= near - rows), 0.5, 1.0)
        out_ref[:, :SIDE] = mine * jnp.where(lane < near, weight, 0.0)
        out_ref[:, SIDE : 2 * SIDE] = jnp.zeros((rows, SIDE), jnp.float32)
        out_ref[:, SIDE : SIDE + columns // 2] = far_ref[...]
        out_ref[:, 2 * SIDE :] = links_ref[...]

    return kernel_call(
        kernel,
        "message",
        out_shape=jax.ShapeDtypeStruct((rows, 2 * SIDE + links.shape[1]), jnp.float32),
        in_specs=in_vmem(3),
        out_specs=in_vmem(1)[0],
    )(turned, far, links)


def sent_rows(sides, owner, rows):
    columns = PCOL * rows
    rest = jnp.zeros((rows, columns - SIDE), jnp.float32)
    piece, low = lax.rem(owner, PCOL), owner < PCOL
    first = lax.rem(piece + jnp.where(low, 0, 1), PCOL)
    near = pltpu.roll(jnp.concatenate([sides[:, :SIDE], rest], axis=1), piece * rows, 1)
    far = pltpu.roll(jnp.concatenate([sides[:, SIDE:], rest], axis=1), first * rows, 1)
    return jnp.concatenate([jnp.where(low, near, far), jnp.where(low, far, near)], axis=1)


def columns_at(ref, start, count):
    base = pl.multiple_of(lax.div(start, 128) * 128, 128)
    return pltpu.roll(ref[:, pl.ds(base, 256)], lax.rem(256 + base - start, 256), 1)[:, :128]


def inner_chain(parent_links, pivot_inverse):
    nodes, width, _ = pivot_inverse.shape

    def kernel(parent_ref, pivot_ref, cross_ref, inner_ref):
        inner = pivot_ref[0]
        inner_ref[0] = inner
        for node in range(1, nodes):
            link = halves(parent_ref[node - 1])
            cross = dot_halves(halves(inner), link)
            cross_ref[node - 1] = -cross
            inner = pivot_ref[node] + dot_halves(link, halves(cross), ((0,), (0,)))
            inner_ref[node] = inner

    return kernel_call(
        kernel,
        "inner_chain",
        out_shape=[jax.ShapeDtypeStruct(array.shape, jnp.float32) for array in (parent_links, pivot_inverse)],
        in_specs=in_vmem(2),
        out_specs=in_vmem(2),
    )(parent_links, pivot_inverse)


def ring_owner(my_index, count, shift, other):
    core = lax.rem(my_index, 2)
    chip = my_index // 2
    place = jnp.where(lax.rem(chip, 2) == 0, chip // 2, count - 1 - chip // 2)
    place = lax.rem(place + shift + count, count)
    chip = jnp.where(place < count // 2, 2 * place, 2 * (count - 1 - place) + 1)
    return 2 * chip + (1 - core if other else core)


def border(arrivals, state, parents, diagonals, chips, last=False):
    begin = state is None
    nodes, width, _ = diagonals.shape
    rows = arrivals[0][2].shape[0]
    lanes = 2 * SIDE
    order = 2 * chips * rows
    count = len(arrivals)
    fresh = rows * count
    bf16, f32 = jnp.bfloat16, jnp.float32

    def kernel(*refs):
        refs = list(refs)
        take = lambda number: [refs.pop(0) for _ in range(number)]
        part_refs = take(count)
        panel_before, kept_before, *held_before = take(4) if not begin else [None] * 4
        parents_ref, diagonals_ref, parents_out, diagonals_out, panel_out = take(5)
        copies = []

        def finish(place, source, target):
            if last:
                copies.append(pltpu.make_async_copy(source, target, sems.at[place]))
                copies[-1].start()

        parents_end, diagonals_end, panel_end = parents_out, diagonals_out, panel_out
        kept_now = None if last else take(1)[0]
        held_now = take(2)
        turned, beside, aside = take(3)
        if last:
            parents_out, diagonals_out, panel_out, sems = take(4)
        me = lax.axis_index("row")
        core = lax.rem(me, 2)
        owners = [ring_owner(me, chips, shift, other) for shift, other, _ in arrivals]
        starts = [pl.multiple_of(owner * rows, 16) for owner in owners]

        for part, whole in enumerate(held_now):
            whole[...] = jnp.zeros(whole.shape, bf16) if begin else held_before[part][...]
        for start, ref in zip(starts, part_refs):
            for whole, part in zip(held_now, halves(ref[:, lanes:])):
                whole[pl.ds(start, rows), :] = part
        sent = [sent_rows(ref[:, :lanes], owner, rows) for owner, ref in zip(owners, part_refs)]
        if not last:
            kept_now[...] = jnp.zeros(kept_now.shape, f32) if begin else kept_before[...]
            for start, part in zip(starts, sent):
                kept_now[pl.ds(start, rows), :order] = part
        if not begin:
            for pair in range(0, count, 2):
                back = columns_at(kept_before, lax.div(owners[pair], 2) * (2 * rows), 2 * rows).T
                first, second = back[:rows], back[rows : 2 * rows]
                sent[pair] += jnp.where(core == 0, first, second)
                sent[pair + 1] += jnp.where(core == 0, second, first)
        left = jnp.concatenate(sent, axis=0)
        aside[:, :order] = left
        aside[:, order:] = jnp.zeros((fresh, 128), f32)
        across = columns_at(aside, me * rows, rows).T[:rows]
        if begin:
            pair = columns_at(aside, lax.div(me, 2) * (2 * rows), 2 * rows)[:rows]
            swapped = jnp.concatenate([pair[:, rows : 2 * rows], pair[:, :rows]], axis=1)
            across += jnp.where(core == 0, pair[:, : 2 * rows], swapped)
        left, across = halves(left), halves(across)
        new = jnp.concatenate([ref[:, lanes:] for ref in part_refs], axis=0)
        new_high, new_low = halves(new)
        image = stacked_dot(left, [whole[...] for whole in held_now])
        image_high, image_low = halves(image)
        own = stacked_dot(across, [new_high, new_low])
        if not begin:
            own = own + panel_before[...]
        if last:
            for node in range(nodes):
                panel_out[:, node, :] = -own[:, node * width : (node + 1) * width]
        else:
            panel_out[...] = own
        high, low = halves(jnp.concatenate([new, image], axis=0).T)
        for place, part in enumerate((high, low, high)):
            turned[:, 2 * fresh * place : 2 * fresh * (place + 1)] = part
        for place, part in enumerate((image_high, new_high, image_high, new_high, image_low, new_low)):
            beside[fresh * place : fresh * (place + 1), :] = part
        if last:
            finish(2 * nodes, panel_out, panel_end)
        for node in range(nodes):
            lower = max(node - 1, 0) * width
            columns = slice(node * width, (node + 1) * width)
            total = jnp.dot(turned[lower : columns.stop, :], beside[:, columns], preferred_element_type=f32)
            diagonals_out[node] = diagonals_ref[node] + total[-width:]
            finish(node, diagonals_out.at[node], diagonals_end.at[node])
            if node > 0:
                parents_out[node - 1] = parents_ref[node - 1] + total[:width]
                finish(nodes + node, parents_out.at[node - 1], parents_end.at[node - 1])
        for copy in copies:
            copy.wait()

    operands = [part for _, _, part in arrivals] + list(state or []) + [parents, diagonals]
    shape_of = jax.ShapeDtypeStruct
    shapes = [shape_of(parents.shape, f32), shape_of(diagonals.shape, f32)]
    held = [shape_of((order, nodes * width), bf16)] * 2
    scratch = [((nodes * width, 6 * fresh), bf16), ((6 * fresh, nodes * width), bf16), ((fresh, order + 128), f32)]
    scratch = [pltpu.VMEM(*shape) for shape in scratch]
    if last:
        shapes.append(shape_of((rows, nodes, width), f32))
        scratch = [pltpu.VMEM(shape.shape, bf16) for shape in held] + scratch
        scratch += [pltpu.VMEM(shape.shape, f32) for shape in shapes]
        scratch.append(pltpu.SemaphoreType.DMA((2 * nodes + 1,)))
    else:
        shapes += [shape_of((rows, nodes * width), f32), shape_of((order, order + 128), f32)] + held
    results = kernel_call(
        kernel,
        "border" + ("_end" if last else "_begin" if begin else ""),
        out_shape=shapes,
        in_specs=in_vmem(len(operands)),
        out_specs=at_home(len(shapes)) if last else in_vmem(len(shapes)),
        scratch_shapes=scratch,
        limit=24 * 2**20 if last else BORDER_LIMIT,
    )(*operands)
    return results[:2], results[2:]


def gather_plan(anc_blocks, anc_links, parent_links, pivot_inverse, pattern):
    chips = lax.axis_size("row") // 2
    far = chips // 2
    ahead, behind = ring_pairs(chips, 1), ring_pairs(chips, -1)
    across = [p for p in ahead if p[0] % 2 == 0] + [p for p in behind if p[0] % 2 == 1]

    def move(pair):
        return [lax.ppermute(value, "row", way) for value, way in zip(pair, (ahead, behind))]

    def both(shift, value):
        return [(shift, False, value), (shift, True, swap_bit(value, 0))]

    turned = anc_blocks[0].T
    far_part = far_rows(turned)
    links = link_chain(after(anc_links, far_part), parent_links, pattern)
    own = message_of(turned, swap_bit(far_part, PCOL.bit_length() - 1), links)
    totals, state = inner_chain(after(parent_links, own), pivot_inverse), None
    arrivals, pair = both(0, own), [own] * 2
    for step in range(1, far):
        pair = move(pair)
        totals, state = border(arrivals, state, *totals, chips)
        pair = [after(value, *totals) for value in pair]
        arrivals = both(-step, pair[0]) + both(step, pair[1])
    last, totals = lax.optimization_barrier((pick(pair), totals))
    totals, state = border(arrivals, state, *totals, chips)
    last, totals = lax.optimization_barrier((lax.ppermute(last, "row", across), totals))
    totals, panels = border(both(far, last), state, *totals, chips, True)
    return panels[0], *totals


def spread_plan(anc_blocks, anc_links, parent_links, pivot_inverse, pattern):
    my_index = lax.axis_index("row")
    total_bits = lax.axis_size("row").bit_length() - 1
    low_bits = PCOL.bit_length() - 1
    rows, nodes, width = anc_links.shape
    links = jnp.concatenate(reduced_links(masked_links(my_index, anc_links, pattern), parent_links), axis=1)
    segment = links
    for bit in range(low_bits, total_bits):
        partner = swap_bit(segment, bit)
        upper = my_index >> bit & 1
        segment = lax.dynamic_update_slice_in_dim(
            jnp.concatenate([partner, partner], 0), segment, upper * segment.shape[0], 0
        )
    image = product(anc_blocks[0], segment)
    for bit in reversed(range(low_bits)):
        half_rows = image.shape[0] // 2
        upper = my_index >> bit & 1
        retained = lax.dynamic_slice_in_dim(image, upper * half_rows, half_rows, 0)
        outgoing = lax.dynamic_slice_in_dim(image, (1 - upper) * half_rows, half_rows, 0)
        image = retained + swap_bit(outgoing, bit)
    column = lambda array, node: array[:, node * width : (node + 1) * width]
    terms = [inner_product(column(links, node), column(image, node)) for node in range(nodes)]
    terms += [inner_product(column(links, node - 1), column(image, node)) for node in range(1, nodes)]
    totals = lax.psum(jnp.stack(terms), "row")
    inner, cross = local_chain(parent_links, pivot_inverse)
    diagonals = jnp.stack(inner) + totals[:nodes]
    parents = totals[nodes:] - jnp.stack(cross)
    return -image.reshape(rows, nodes, width), parents, diagonals


def on_device(anc_blocks, anc_links, parent_links, pivot_inverse, pattern):
    size = lax.axis_size("row")
    rows, nodes, width = anc_links.shape
    whole_bytes = 4 * size * rows * (nodes * width + size * rows)
    plan = gather_plan if size == 2 * PCOL and whole_bytes <= GATHER_LIMIT else spread_plan
    return plan(anc_blocks, anc_links, parent_links, pivot_inverse, pattern)


def solution(mesh):
    return jax.shard_map(
        on_device,
        mesh=mesh,
        in_specs=(
            P(("pole", "row"), None, None),
            P(("pole", "row"), None, None),
            P("pole", None, None),
            P("pole", None, None),
            P(),
        ),
        out_specs=(P(("pole", "row"), None, None), P("pole", None, None), P("pole", None, None)),
        check_vma=False,
    )
```

```python
import jax
import jax.numpy as jnp
from jax import lax
from jax.experimental import pallas as pl
from jax.experimental.pallas import tpu as pltpu
from jax.sharding import PartitionSpec as P

PCOL = 8
TILE = 128
GATHER_LIMIT = 16 * 2**20
SIDE = 256
LATE_PANELS = 3
FIRST_FLOPS = 4_000_000_000


def product(left, right):
    return jnp.dot(left, right, precision=lax.Precision.HIGH, preferred_element_type=jnp.float32)


def inner_product(left, right):
    return lax.dot_general(
        left,
        right,
        (((0,), (0,)), ((), ())),
        precision=lax.Precision.HIGH,
        preferred_element_type=jnp.float32,
    )


def swap_bit(value, bit):
    mask = 2**bit
    return lax.ppermute(value, "row", [(i, i ^ mask) for i in range(lax.axis_size("row"))])


def ring_chips(count):
    return list(range(0, count, 2)) + list(range(count - 1, 0, -2))


def ring_pairs(count, shift):
    order = ring_chips(count)
    pairs = []
    for place, chip in enumerate(order):
        target = order[(place + shift) % count]
        pairs += [(2 * chip + core, 2 * target + core) for core in range(2)]
    return pairs


def masked_links(my_index, anc_links, pattern):
    rows_here = anc_links.shape[0]
    tile_index = (my_index * rows_here + jnp.arange(rows_here, dtype=jnp.int32)) // TILE
    row_keep = jnp.take(pattern, tile_index, axis=1) != 0
    return jnp.where(row_keep[:, :, None], jnp.swapaxes(anc_links, 0, 1), 0.0)


def reduced_links(links, parent_links):
    reduced = [links[0]]
    for node in range(1, links.shape[0]):
        reduced.append(links[node] - product(reduced[-1], parent_links[node - 1]))
    return reduced


def local_chain(parent_links, pivot_inverse):
    inner = [pivot_inverse[0]]
    cross = []
    for node in range(1, pivot_inverse.shape[0]):
        link = parent_links[node - 1]
        cross.append(product(inner[-1], link))
        inner.append(pivot_inverse[node] + inner_product(link, cross[-1]))
    return inner, cross


def halves(value):
    high = value.astype(jnp.bfloat16)
    return high, (value - high.astype(jnp.float32)).astype(jnp.bfloat16)


def dot_halves(left, right, dims=((1,), (0,))):
    def one(a, b):
        return lax.dot_general(a, b, (dims, ((), ())), preferred_element_type=jnp.float32)

    return one(left[0], right[0]) + (one(left[0], right[1]) + one(left[1], right[0]))


def stacked_dot(left, right):
    height = left[0].shape[0]
    both = jnp.dot(jnp.concatenate(left, axis=0), right[0], preferred_element_type=jnp.float32)
    cross = jnp.dot(left[0], right[1], preferred_element_type=jnp.float32)
    return both[:height] + (both[height:] + cross)


def kernel_call(kernel, name, limit=16 * 2**20, flops=0, **more):
    return pl.pallas_call(
        kernel,
        name=name,
        compiler_params=pltpu.CompilerParams(vmem_limit_bytes=limit),
        cost_estimate=pl.CostEstimate(flops=flops, bytes_accessed=0, transcendentals=0),
        **more,
    )


def in_vmem(count):
    return [pl.BlockSpec(memory_space=pltpu.VMEM)] * count


def after(value, *others):
    return lax.optimization_barrier((value, *others))[0]


def at_home(count):
    return [pl.BlockSpec(memory_space=pltpu.HBM)] * count


def far_rows(turned):
    rows, columns = turned.shape[0] // 2, turned.shape[1]

    def kernel(turned_ref, out_ref):
        me = lax.axis_index("row")
        low = me < PCOL
        theirs = jnp.where(low, turned_ref[rows:], turned_ref[:rows])
        first = lax.rem(me, PCOL) + jnp.where(low, 1, 0)
        out_ref[...] = pltpu.roll(theirs, lax.rem(columns - lax.rem(first, PCOL) * rows, columns), 1)[:, : columns // 2]

    return kernel_call(
        kernel,
        "far_rows",
        flops=FIRST_FLOPS,
        out_shape=jax.ShapeDtypeStruct((rows, columns // 2), jnp.float32),
        in_specs=in_vmem(1),
        out_specs=in_vmem(1)[0],
    )(turned)


def pick(pair):
    def kernel(first_ref, second_ref, out_ref):
        out_ref[...] = jnp.where(lax.rem(lax.axis_index("row"), 2) == 0, first_ref[...], second_ref[...])

    return kernel_call(
        kernel,
        "pick",
        out_shape=jax.ShapeDtypeStruct(pair[0].shape, jnp.float32),
        in_specs=in_vmem(2),
        out_specs=in_vmem(1)[0],
    )(*pair)


def link_chain(anc_links, parent_links, pattern):
    rows, nodes, width = anc_links.shape
    tiles = pattern.shape[1]

    def kernel(links_ref, parent_ref, pattern_ref, out_ref):
        first = lax.axis_index("row") * rows
        tile = first // TILE
        next_tile = jnp.minimum(tile + 1, tiles - 1)
        row = first + lax.broadcasted_iota(jnp.int32, (rows, width), 0)
        in_first = row < (tile + 1) * TILE
        reduced = None
        for node in range(nodes):
            keep = jnp.where(in_first, pattern_ref[node, tile], pattern_ref[node, next_tile])
            links = jnp.where(keep != 0, links_ref[:, node, :], 0.0)
            if node > 0:
                links = links - dot_halves(halves(reduced), halves(parent_ref[node - 1]))
            out_ref[:, node * width : (node + 1) * width] = links
            reduced = links

    return kernel_call(
        kernel,
        "link_chain",
        out_shape=jax.ShapeDtypeStruct((rows, nodes * width), jnp.float32),
        in_specs=in_vmem(2) + [pl.BlockSpec(memory_space=pltpu.SMEM)],
        out_specs=in_vmem(1)[0],
    )(anc_links, parent_links, pattern)


def message_of(turned, far, links):
    rows, columns = turned.shape[0] // 2, turned.shape[1]
    near = columns // 2 + rows

    def kernel(turned_ref, far_ref, links_ref, out_ref):
        me = lax.axis_index("row")
        mine = jnp.where(me < PCOL, turned_ref[:rows], turned_ref[rows:])
        mine = pltpu.roll(mine, lax.rem(columns - lax.rem(me, PCOL) * rows, columns), 1)[:, :SIDE]
        lane = lax.broadcasted_iota(jnp.int32, (1, SIDE), 1)
        weight = jnp.where((lane < rows) | (lane >= near - rows), 0.5, 1.0)
        out_ref[:, :SIDE] = mine * jnp.where(lane < near, weight, 0.0)
        out_ref[:, SIDE : 2 * SIDE] = jnp.zeros((rows, SIDE), jnp.float32)
        out_ref[:, SIDE : SIDE + columns // 2] = far_ref[...]
        out_ref[:, 2 * SIDE :] = links_ref[...]

    return kernel_call(
        kernel,
        "message",
        out_shape=jax.ShapeDtypeStruct((rows, 2 * SIDE + links.shape[1]), jnp.float32),
        in_specs=in_vmem(3),
        out_specs=in_vmem(1)[0],
    )(turned, far, links)


def sent_rows(sides, owner, rows):
    columns = PCOL * rows
    rest = jnp.zeros((rows, columns - SIDE), jnp.float32)
    piece, low = lax.rem(owner, PCOL), owner < PCOL
    first = lax.rem(piece + jnp.where(low, 0, 1), PCOL)
    near = pltpu.roll(jnp.concatenate([sides[:, :SIDE], rest], axis=1), piece * rows, 1)
    far = pltpu.roll(jnp.concatenate([sides[:, SIDE:], rest], axis=1), first * rows, 1)
    return jnp.concatenate([jnp.where(low, near, far), jnp.where(low, far, near)], axis=1)


def columns_at(ref, start, count):
    base = pl.multiple_of(lax.div(start, 128) * 128, 128)
    return pltpu.roll(ref[:, pl.ds(base, 256)], lax.rem(256 + base - start, 256), 1)[:, :128]


def inner_chain(parent_links, pivot_inverse):
    nodes, width, _ = pivot_inverse.shape

    def kernel(parent_ref, pivot_ref, cross_ref, inner_ref):
        inner = pivot_ref[0]
        inner_ref[0] = inner
        for node in range(1, nodes):
            link = halves(parent_ref[node - 1])
            cross = dot_halves(halves(inner), link)
            cross_ref[node - 1] = -cross
            inner = pivot_ref[node] + dot_halves(link, halves(cross), ((0,), (0,)))
            inner_ref[node] = inner

    return kernel_call(
        kernel,
        "inner_chain",
        out_shape=[jax.ShapeDtypeStruct(array.shape, jnp.float32) for array in (parent_links, pivot_inverse)],
        in_specs=in_vmem(2),
        out_specs=in_vmem(2),
    )(parent_links, pivot_inverse)


def ring_owner(my_index, count, shift, other):
    core = lax.rem(my_index, 2)
    chip = my_index // 2
    place = jnp.where(lax.rem(chip, 2) == 0, chip // 2, count - 1 - chip // 2)
    place = lax.rem(place + shift + count, count)
    chip = jnp.where(place < count // 2, 2 * place, 2 * (count - 1 - place) + 1)
    return 2 * chip + (1 - core if other else core)


def border(arrivals, state, parents, diagonals, chips, last=False, late=None, defer=0):
    begin = state is None
    nodes, width, _ = diagonals.shape
    rows = arrivals[0][2].shape[0]
    lanes = 2 * SIDE
    order = 2 * chips * rows
    count = len(arrivals)
    fresh = rows * count
    bf16, f32 = jnp.bfloat16, jnp.float32

    def kernel(*refs):
        refs = list(refs)
        take = lambda number: [refs.pop(0) for _ in range(number)]
        part_refs = take(count)
        panel_before, kept_before, *held_before = take(4) if not begin else [None] * 4
        parents_ref, diagonals_ref = take(2)
        late_parents, late_diagonals = take(2) if late else [None] * 2
        parents_out, diagonals_out, panel_out = take(3)
        copies = []

        def finish(place, source, target):
            if last:
                copies.append(pltpu.make_async_copy(source, target, sems.at[place]))
                copies[-1].start()

        parents_end, diagonals_end, panel_end = parents_out, diagonals_out, panel_out
        kept_now = None if last else take(1)[0]
        held_now = take(2)
        tails = take(2 if defer else 0)
        turned, beside, aside = take(3)
        if last:
            parents_out, diagonals_out, panel_out, sems = take(4)
        me = lax.axis_index("row")
        core = lax.rem(me, 2)
        owners = [ring_owner(me, chips, shift, other) for shift, other, _ in arrivals]
        starts = [pl.multiple_of(owner * rows, 16) for owner in owners]

        for part, whole in enumerate(held_now):
            whole[...] = jnp.zeros(whole.shape, bf16) if begin else held_before[part][...]
        for start, ref in zip(starts, part_refs):
            for whole, part in zip(held_now, halves(ref[:, lanes:])):
                whole[pl.ds(start, rows), :] = part
        sent = [sent_rows(ref[:, :lanes], owner, rows) for owner, ref in zip(owners, part_refs)]
        if not last:
            kept_now[...] = jnp.zeros(kept_now.shape, f32) if begin else kept_before[...]
            for start, part in zip(starts, sent):
                kept_now[pl.ds(start, rows), :order] = part
        if not begin:
            for pair in range(0, count, 2):
                back = columns_at(kept_before, lax.div(owners[pair], 2) * (2 * rows), 2 * rows).T
                first, second = back[:rows], back[rows : 2 * rows]
                sent[pair] += jnp.where(core == 0, first, second)
                sent[pair + 1] += jnp.where(core == 0, second, first)
        left = jnp.concatenate(sent, axis=0)
        aside[:, :order] = left
        aside[:, order:] = jnp.zeros((fresh, 128), f32)
        across = columns_at(aside, me * rows, rows).T[:rows]
        if begin:
            pair = columns_at(aside, lax.div(me, 2) * (2 * rows), 2 * rows)[:rows]
            swapped = jnp.concatenate([pair[:, rows : 2 * rows], pair[:, :rows]], axis=1)
            across += jnp.where(core == 0, pair[:, : 2 * rows], swapped)
        left, across = halves(left), halves(across)
        for node in range(nodes):
            columns = slice(node * width, (node + 1) * width)
            image = stacked_dot(left, [whole[:, columns] for whole in held_now])
            there = slice(lanes + node * width, lanes + (node + 1) * width)
            new = jnp.concatenate([ref[:, there] for ref in part_refs], axis=0)
            new_high, new_low = halves(new)
            image_high, image_low = halves(image)
            own = stacked_dot(across, [new_high, new_low])
            if not begin:
                own += panel_before[:, columns]
            if last:
                panel_out[:, node, :] = -own
            else:
                panel_out[:, columns] = own
            high, low = halves(jnp.concatenate([new, image], axis=0).T)
            for place, part in enumerate((high, low, high)):
                turned[columns, 2 * fresh * place : 2 * fresh * (place + 1)] = part
            for place, part in enumerate((image_high, new_high, image_high, new_high, image_low, new_low)):
                beside[fresh * place : fresh * (place + 1), columns] = part
        if last:
            finish(2 * nodes, panel_out, panel_end)
        rest = nodes - defer
        if defer:
            tails[0][...] = turned[(rest - 1) * width :, :]
            tails[1][...] = beside[:, rest * width :]
            diagonals_out[rest:] = diagonals_ref[rest:]
            parents_out[rest - 1 :] = parents_ref[rest - 1 :]
        for node in range(rest):
            lower = max(node - 1, 0) * width
            columns = slice(node * width, (node + 1) * width)
            total = jnp.dot(turned[lower : columns.stop, :], beside[:, columns], preferred_element_type=f32)
            total_below, total_here = total[:width], total[-width:]
            if late and node >= nodes - late[0].shape[0]:
                place = node - nodes + late[0].shape[0]
                total_below = total_below + late_parents[place]
                total_here = total_here + late_diagonals[place]
            diagonals_out[node] = diagonals_ref[node] + total_here
            finish(node, diagonals_out.at[node], diagonals_end.at[node])
            if node > 0:
                parents_out[node - 1] = parents_ref[node - 1] + total_below
                finish(nodes + node, parents_out.at[node - 1], parents_end.at[node - 1])
        for copy in copies:
            copy.wait()

    operands = [part for _, _, part in arrivals] + list(state or [])
    operands += [parents, diagonals] + list(late or [])
    shape_of = jax.ShapeDtypeStruct
    shapes = [shape_of(parents.shape, f32), shape_of(diagonals.shape, f32)]
    held = [shape_of((order, nodes * width), bf16)] * 2
    scratch = [((nodes * width, 6 * fresh), bf16), ((6 * fresh, nodes * width), bf16), ((fresh, order + 128), f32)]
    scratch = [pltpu.VMEM(*shape) for shape in scratch]
    if last:
        shapes.append(shape_of((rows, nodes, width), f32))
        scratch = [pltpu.VMEM(shape.shape, bf16) for shape in held] + scratch
        scratch += [pltpu.VMEM(shape.shape, f32) for shape in shapes]
        scratch.append(pltpu.SemaphoreType.DMA((2 * nodes + 1,)))
    else:
        shapes += [shape_of((rows, nodes * width), f32), shape_of((order, order + 128), f32)] + held
    if defer:
        shapes.append(shape_of(((defer + 1) * width, 6 * fresh), bf16))
        shapes.append(shape_of((6 * fresh, defer * width), bf16))
    results = kernel_call(
        kernel,
        "border" + ("_end" if last else "_begin" if begin else ""),
        out_shape=shapes,
        in_specs=in_vmem(len(operands)),
        out_specs=at_home(len(shapes)) if last else in_vmem(len(shapes)),
        scratch_shapes=scratch,
        limit=(24 if last else 16) * 2**20,
    )(*operands)
    return (results[:2], results[2:6], results[6:]) if defer else (results[:2], results[2:])


def late_products(turned, beside, width):
    count = beside.shape[1] // width

    def kernel(turned_ref, beside_ref, parents_ref, diagonals_ref):
        for place in range(count):
            left = turned_ref[place * width : (place + 2) * width, :]
            right = beside_ref[:, place * width : (place + 1) * width]
            total = jnp.dot(left, right, preferred_element_type=jnp.float32)
            parents_ref[place] = total[:width]
            diagonals_ref[place] = total[width:]

    return kernel_call(
        kernel,
        "late_products",
        out_shape=[jax.ShapeDtypeStruct((count, width, width), jnp.float32)] * 2,
        in_specs=in_vmem(2),
        out_specs=in_vmem(2),
    )(turned, beside)


def gather_plan(anc_blocks, anc_links, parent_links, pivot_inverse, pattern):
    chips = lax.axis_size("row") // 2
    far = chips // 2
    ahead, behind = ring_pairs(chips, 1), ring_pairs(chips, -1)
    across = [p for p in ahead if p[0] % 2 == 0] + [p for p in behind if p[0] % 2 == 1]

    def move(pair):
        return [lax.ppermute(value, "row", way) for value, way in zip(pair, (ahead, behind))]

    def both(shift, value):
        return [(shift, False, value), (shift, True, swap_bit(value, 0))]

    turned = anc_blocks[0].T
    far_part = far_rows(turned)
    links = link_chain(after(anc_links, far_part), parent_links, pattern)
    own = message_of(turned, swap_bit(far_part, PCOL.bit_length() - 1), links)
    totals, state = inner_chain(after(parent_links, own), pivot_inverse), None
    arrivals, pair = both(0, own), [own] * 2
    for step in range(1, far):
        pair = move(pair)
        totals, state = border(arrivals, state, *totals, chips)
        pair = [after(value, *totals) for value in pair]
        arrivals = both(-step, pair[0]) + both(step, pair[1])
    last, totals = lax.optimization_barrier((pick(pair), totals))
    totals, state, tails = border(arrivals, state, *totals, chips, defer=LATE_PANELS)
    last, totals, tails = lax.optimization_barrier((lax.ppermute(last, "row", across), totals, tails))
    late = late_products(*tails, anc_links.shape[2])
    totals, panels = border(both(far, last), state, *totals, chips, True, late)
    return panels[0], *totals


def spread_plan(anc_blocks, anc_links, parent_links, pivot_inverse, pattern):
    my_index = lax.axis_index("row")
    total_bits = lax.axis_size("row").bit_length() - 1
    low_bits = PCOL.bit_length() - 1
    rows, nodes, width = anc_links.shape
    links = jnp.concatenate(reduced_links(masked_links(my_index, anc_links, pattern), parent_links), axis=1)
    segment = links
    for bit in range(low_bits, total_bits):
        partner = swap_bit(segment, bit)
        upper = my_index >> bit & 1
        segment = lax.dynamic_update_slice_in_dim(
            jnp.concatenate([partner, partner], 0), segment, upper * segment.shape[0], 0
        )
    image = product(anc_blocks[0], segment)
    for bit in reversed(range(low_bits)):
        half_rows = image.shape[0] // 2
        upper = my_index >> bit & 1
        retained = lax.dynamic_slice_in_dim(image, upper * half_rows, half_rows, 0)
        outgoing = lax.dynamic_slice_in_dim(image, (1 - upper) * half_rows, half_rows, 0)
        image = retained + swap_bit(outgoing, bit)
    column = lambda array, node: array[:, node * width : (node + 1) * width]
    terms = [inner_product(column(links, node), column(image, node)) for node in range(nodes)]
    terms += [inner_product(column(links, node - 1), column(image, node)) for node in range(1, nodes)]
    totals = lax.psum(jnp.stack(terms), "row")
    inner, cross = local_chain(parent_links, pivot_inverse)
    diagonals = jnp.stack(inner) + totals[:nodes]
    parents = totals[nodes:] - jnp.stack(cross)
    return -image.reshape(rows, nodes, width), parents, diagonals


def on_device(anc_blocks, anc_links, parent_links, pivot_inverse, pattern):
    size = lax.axis_size("row")
    rows, nodes, width = anc_links.shape
    whole_bytes = 4 * size * rows * (nodes * width + size * rows)
    plan = gather_plan if size == 2 * PCOL and whole_bytes <= GATHER_LIMIT else spread_plan
    return plan(anc_blocks, anc_links, parent_links, pivot_inverse, pattern)


def solution(mesh):
    return jax.shard_map(
        on_device,
        mesh=mesh,
        in_specs=(
            P(("pole", "row"), None, None),
            P(("pole", "row"), None, None),
            P("pole", None, None),
            P("pole", None, None),
            P(),
        ),
        out_specs=(P(("pole", "row"), None, None), P("pole", None, None), P("pole", None, None)),
        check_vma=False,
    )
```

```python
import jax
import jax.numpy as jnp
from jax import lax
from jax.experimental import pallas as pl
from jax.experimental.pallas import tpu as pltpu
from jax.sharding import PartitionSpec as P

PCOL = 8
TILE = 128
GATHER_LIMIT = 16 * 2**20
SIDE = 256
LATE_PANELS = 3
FIRST_FLOPS = 4_000_000_000


def product(left, right):
    return jnp.dot(left, right, precision=lax.Precision.HIGH, preferred_element_type=jnp.float32)


def inner_product(left, right):
    return lax.dot_general(
        left,
        right,
        (((0,), (0,)), ((), ())),
        precision=lax.Precision.HIGH,
        preferred_element_type=jnp.float32,
    )


def swap_bit(value, bit):
    mask = 2**bit
    return lax.ppermute(value, "row", [(i, i ^ mask) for i in range(lax.axis_size("row"))])


def ring_chips(count):
    return list(range(0, count, 2)) + list(range(count - 1, 0, -2))


def ring_pairs(count, shift):
    order = ring_chips(count)
    pairs = []
    for place, chip in enumerate(order):
        target = order[(place + shift) % count]
        pairs += [(2 * chip + core, 2 * target + core) for core in range(2)]
    return pairs


def masked_links(my_index, anc_links, pattern):
    rows_here = anc_links.shape[0]
    tile_index = (my_index * rows_here + jnp.arange(rows_here, dtype=jnp.int32)) // TILE
    row_keep = jnp.take(pattern, tile_index, axis=1) != 0
    return jnp.where(row_keep[:, :, None], jnp.swapaxes(anc_links, 0, 1), 0.0)


def reduced_links(links, parent_links):
    reduced = [links[0]]
    for node in range(1, links.shape[0]):
        reduced.append(links[node] - product(reduced[-1], parent_links[node - 1]))
    return reduced


def local_chain(parent_links, pivot_inverse):
    inner = [pivot_inverse[0]]
    cross = []
    for node in range(1, pivot_inverse.shape[0]):
        link = parent_links[node - 1]
        cross.append(product(inner[-1], link))
        inner.append(pivot_inverse[node] + inner_product(link, cross[-1]))
    return inner, cross


def halves(value):
    high = value.astype(jnp.bfloat16)
    return high, (value - high.astype(jnp.float32)).astype(jnp.bfloat16)


def dot_halves(left, right, dims=((1,), (0,))):
    def one(a, b):
        return lax.dot_general(a, b, (dims, ((), ())), preferred_element_type=jnp.float32)

    return one(left[0], right[0]) + (one(left[0], right[1]) + one(left[1], right[0]))


def stacked_dot(left, right):
    height = left[0].shape[0]
    both = jnp.dot(jnp.concatenate(left, axis=0), right[0], preferred_element_type=jnp.float32)
    cross = jnp.dot(left[0], right[1], preferred_element_type=jnp.float32)
    return both[:height] + (both[height:] + cross)


def kernel_call(kernel, name, limit=16 * 2**20, flops=0, **more):
    return pl.pallas_call(
        kernel,
        name=name,
        compiler_params=pltpu.CompilerParams(vmem_limit_bytes=limit),
        cost_estimate=pl.CostEstimate(flops=flops, bytes_accessed=0, transcendentals=0),
        **more,
    )


def in_vmem(count):
    return [pl.BlockSpec(memory_space=pltpu.VMEM)] * count


def after(value, *others):
    return lax.optimization_barrier((value, *others))[0]


def at_home(count):
    return [pl.BlockSpec(memory_space=pltpu.HBM)] * count


def far_rows(turned):
    rows, columns = turned.shape[0] // 2, turned.shape[1]

    def kernel(turned_ref, out_ref):
        me = lax.axis_index("row")
        low = me < PCOL
        theirs = jnp.where(low, turned_ref[rows:], turned_ref[:rows])
        first = lax.rem(me, PCOL) + jnp.where(low, 1, 0)
        theirs = pltpu.roll(theirs, lax.rem(columns - lax.rem(first, PCOL) * rows, columns), 1)[:, : columns // 2]
        out_ref[...] = jnp.concatenate([theirs[: rows // 2], theirs[rows // 2 :]], axis=1)

    return kernel_call(
        kernel,
        "far_rows",
        flops=FIRST_FLOPS,
        out_shape=jax.ShapeDtypeStruct((rows // 2, columns), jnp.float32),
        in_specs=in_vmem(1),
        out_specs=in_vmem(1)[0],
    )(turned)


def pick(pair):
    def kernel(first_ref, second_ref, out_ref):
        out_ref[...] = jnp.where(lax.rem(lax.axis_index("row"), 2) == 0, first_ref[...], second_ref[...])

    return kernel_call(
        kernel,
        "pick",
        out_shape=jax.ShapeDtypeStruct(pair[0].shape, jnp.float32),
        in_specs=in_vmem(2),
        out_specs=in_vmem(1)[0],
    )(*pair)


def link_chain(anc_links, parent_links, pattern):
    rows, nodes, width = anc_links.shape
    tiles = pattern.shape[1]

    def kernel(links_ref, parent_ref, pattern_ref, out_ref):
        first = lax.axis_index("row") * rows
        tile = first // TILE
        next_tile = jnp.minimum(tile + 1, tiles - 1)
        row = first + lax.broadcasted_iota(jnp.int32, (rows, width), 0)
        in_first = row < (tile + 1) * TILE
        reduced = None
        for node in range(nodes):
            keep = jnp.where(in_first, pattern_ref[node, tile], pattern_ref[node, next_tile])
            links = jnp.where(keep != 0, links_ref[:, node, :], 0.0)
            if node > 0:
                links = links - dot_halves(halves(reduced), halves(parent_ref[node - 1]))
            out_ref[:, node * width : (node + 1) * width] = links
            reduced = links

    return kernel_call(
        kernel,
        "link_chain",
        out_shape=jax.ShapeDtypeStruct((rows, nodes * width), jnp.float32),
        in_specs=in_vmem(2) + [pl.BlockSpec(memory_space=pltpu.SMEM)],
        out_specs=in_vmem(1)[0],
    )(anc_links, parent_links, pattern)


def message_of(turned, far, links):
    rows, columns = turned.shape[0] // 2, turned.shape[1]
    near = columns // 2 + rows

    def kernel(turned_ref, far_ref, links_ref, out_ref):
        me = lax.axis_index("row")
        mine = jnp.where(me < PCOL, turned_ref[:rows], turned_ref[rows:])
        mine = pltpu.roll(mine, lax.rem(columns - lax.rem(me, PCOL) * rows, columns), 1)[:, :SIDE]
        lane = lax.broadcasted_iota(jnp.int32, (1, SIDE), 1)
        weight = jnp.where((lane < rows) | (lane >= near - rows), 0.5, 1.0)
        out_ref[:, :SIDE] = mine * jnp.where(lane < near, weight, 0.0)
        out_ref[:, SIDE : 2 * SIDE] = jnp.zeros((rows, SIDE), jnp.float32)
        out_ref[: rows // 2, SIDE : SIDE + columns // 2] = far_ref[:, : columns // 2]
        out_ref[rows // 2 :, SIDE : SIDE + columns // 2] = far_ref[:, columns // 2 :]
        out_ref[:, 2 * SIDE :] = links_ref[...]

    return kernel_call(
        kernel,
        "message",
        out_shape=jax.ShapeDtypeStruct((rows, 2 * SIDE + links.shape[1]), jnp.float32),
        in_specs=in_vmem(3),
        out_specs=in_vmem(1)[0],
    )(turned, far, links)


def sent_rows(sides, owner, rows):
    columns = PCOL * rows
    rest = jnp.zeros((rows, columns - SIDE), jnp.float32)
    piece, low = lax.rem(owner, PCOL), owner < PCOL
    first = lax.rem(piece + jnp.where(low, 0, 1), PCOL)
    near = pltpu.roll(jnp.concatenate([sides[:, :SIDE], rest], axis=1), piece * rows, 1)
    far = pltpu.roll(jnp.concatenate([sides[:, SIDE:], rest], axis=1), first * rows, 1)
    return jnp.concatenate([jnp.where(low, near, far), jnp.where(low, far, near)], axis=1)


def columns_at(ref, start, count):
    base = pl.multiple_of(lax.div(start, 128) * 128, 128)
    return pltpu.roll(ref[:, pl.ds(base, 256)], lax.rem(256 + base - start, 256), 1)[:, :128]


def inner_chain(parent_links, pivot_inverse):
    nodes, width, _ = pivot_inverse.shape

    def kernel(parent_ref, pivot_ref, cross_ref, inner_ref):
        inner = pivot_ref[0]
        inner_ref[0] = inner
        for node in range(1, nodes):
            link = halves(parent_ref[node - 1])
            cross = dot_halves(halves(inner), link)
            cross_ref[node - 1] = -cross
            inner = pivot_ref[node] + dot_halves(link, halves(cross), ((0,), (0,)))
            inner_ref[node] = inner

    return kernel_call(
        kernel,
        "inner_chain",
        out_shape=[jax.ShapeDtypeStruct(array.shape, jnp.float32) for array in (parent_links, pivot_inverse)],
        in_specs=in_vmem(2),
        out_specs=in_vmem(2),
    )(parent_links, pivot_inverse)


def ring_owner(my_index, count, shift, other):
    core = lax.rem(my_index, 2)
    chip = my_index // 2
    place = jnp.where(lax.rem(chip, 2) == 0, chip // 2, count - 1 - chip // 2)
    place = lax.rem(place + shift + count, count)
    chip = jnp.where(place < count // 2, 2 * place, 2 * (count - 1 - place) + 1)
    return 2 * chip + (1 - core if other else core)


def border(arrivals, state, parents, diagonals, chips, last=False, late=None, defer=0):
    begin = state is None
    nodes, width, _ = diagonals.shape
    rows = arrivals[0][2].shape[0]
    lanes = 2 * SIDE
    order = 2 * chips * rows
    count = len(arrivals)
    fresh = rows * count
    bf16, f32 = jnp.bfloat16, jnp.float32

    def kernel(*refs):
        refs = list(refs)
        take = lambda number: [refs.pop(0) for _ in range(number)]
        part_refs = take(count)
        panel_before, kept_before, *held_before = take(4) if not begin else [None] * 4
        parents_ref, diagonals_ref = take(2)
        late_parents, late_diagonals = take(2) if late else [None] * 2
        parents_out, diagonals_out, panel_out = take(3)
        copies = []

        def finish(place, source, target):
            if last:
                copies.append(pltpu.make_async_copy(source, target, sems.at[place]))
                copies[-1].start()

        parents_end, diagonals_end, panel_end = parents_out, diagonals_out, panel_out
        kept_now = None if last else take(1)[0]
        held_now = take(0 if last else 2)
        tails = take(2 if defer else 0)
        turned, beside, aside = take(3)
        if last:
            parents_out, diagonals_out, panel_out, sems = take(4)
        me = lax.axis_index("row")
        core = lax.rem(me, 2)
        owners = [ring_owner(me, chips, shift, other) for shift, other, _ in arrivals]
        starts = [pl.multiple_of(owner * rows, 16) for owner in owners]

        for part, whole in enumerate(held_now):
            whole[...] = jnp.zeros(whole.shape, bf16) if begin else held_before[part][...]
        held = held_before if last else held_now
        for start, ref in zip(starts, part_refs):
            for whole, part in zip(held_now, halves(ref[:, lanes:])):
                whole[pl.ds(start, rows), :] = part
        sent = [sent_rows(ref[:, :lanes], owner, rows) for owner, ref in zip(owners, part_refs)]
        if not last:
            kept_now[...] = jnp.zeros(kept_now.shape, f32) if begin else kept_before[...]
            for start, part in zip(starts, sent):
                kept_now[pl.ds(start, rows), :order] = part
        if not begin:
            for pair in range(0, count, 2):
                back = columns_at(kept_before, lax.div(owners[pair], 2) * (2 * rows), 2 * rows).T
                first, second = back[:rows], back[rows : 2 * rows]
                sent[pair] += jnp.where(core == 0, first, second)
                sent[pair + 1] += jnp.where(core == 0, second, first)
        left = jnp.concatenate(sent, axis=0)
        aside[:, :order] = left
        aside[:, order:] = jnp.zeros((fresh, 128), f32)
        across = columns_at(aside, me * rows, rows).T[:rows]
        if begin:
            pair = columns_at(aside, lax.div(me, 2) * (2 * rows), 2 * rows)[:rows]
            swapped = jnp.concatenate([pair[:, rows : 2 * rows], pair[:, :rows]], axis=1)
            across += jnp.where(core == 0, pair[:, : 2 * rows], swapped)
        if last:
            pair = columns_at(aside, lax.div(owners[0], 2) * (2 * rows), 2 * rows)
            swapped = jnp.concatenate([pair[:, rows : 2 * rows], pair[:, :rows]], axis=1)
            between = halves(jnp.where(core == 0, pair[:, : 2 * rows], swapped))
        left, across = halves(left), halves(across)
        for node in range(nodes):
            columns = slice(node * width, (node + 1) * width)
            image = stacked_dot(left, [whole[:, columns] for whole in held])
            there = slice(lanes + node * width, lanes + (node + 1) * width)
            new = jnp.concatenate([ref[:, there] for ref in part_refs], axis=0)
            new_high, new_low = halves(new)
            if last:
                image = image + stacked_dot(between, [new_high, new_low])
            image_high, image_low = halves(image)
            own = stacked_dot(across, [new_high, new_low])
            if not begin:
                own += panel_before[:, columns]
            if last:
                panel_out[:, node, :] = -own
            else:
                panel_out[:, columns] = own
            high, low = halves(jnp.concatenate([new, image], axis=0).T)
            for place, part in enumerate((high, low, high)):
                turned[columns, 2 * fresh * place : 2 * fresh * (place + 1)] = part
            for place, part in enumerate((image_high, new_high, image_high, new_high, image_low, new_low)):
                beside[fresh * place : fresh * (place + 1), columns] = part
        if last:
            finish(2 * nodes, panel_out, panel_end)
        rest = nodes - defer
        if defer:
            tails[0][...] = turned[(rest - 1) * width :, :]
            tails[1][...] = beside[:, rest * width :]
            diagonals_out[rest:] = diagonals_ref[rest:]
            parents_out[rest - 1 :] = parents_ref[rest - 1 :]
        for node in range(rest):
            lower = max(node - 1, 0) * width
            columns = slice(node * width, (node + 1) * width)
            total = jnp.dot(turned[lower : columns.stop, :], beside[:, columns], preferred_element_type=f32)
            total_below, total_here = total[:width], total[-width:]
            if late and node >= nodes - late[0].shape[0]:
                place = node - nodes + late[0].shape[0]
                total_below = total_below + late_parents[place]
                total_here = total_here + late_diagonals[place]
            diagonals_out[node] = diagonals_ref[node] + total_here
            finish(node, diagonals_out.at[node], diagonals_end.at[node])
            if node > 0:
                parents_out[node - 1] = parents_ref[node - 1] + total_below
                finish(nodes + node, parents_out.at[node - 1], parents_end.at[node - 1])
        for copy in copies:
            copy.wait()

    operands = [part for _, _, part in arrivals] + list(state or [])
    operands += [parents, diagonals] + list(late or [])
    shape_of = jax.ShapeDtypeStruct
    shapes = [shape_of(parents.shape, f32), shape_of(diagonals.shape, f32)]
    held = [shape_of((order, nodes * width), bf16)] * 2
    scratch = [((nodes * width, 6 * fresh), bf16), ((6 * fresh, nodes * width), bf16), ((fresh, order + 128), f32)]
    scratch = [pltpu.VMEM(*shape) for shape in scratch]
    if last:
        shapes.append(shape_of((rows, nodes, width), f32))
        scratch += [pltpu.VMEM(shape.shape, f32) for shape in shapes]
        scratch.append(pltpu.SemaphoreType.DMA((2 * nodes + 1,)))
    else:
        shapes += [shape_of((rows, nodes * width), f32), shape_of((order, order + 128), f32)] + held
    if defer:
        shapes.append(shape_of(((defer + 1) * width, 6 * fresh), bf16))
        shapes.append(shape_of((6 * fresh, defer * width), bf16))
    results = kernel_call(
        kernel,
        "border" + ("_end" if last else "_begin" if begin else ""),
        out_shape=shapes,
        in_specs=in_vmem(len(operands)),
        out_specs=at_home(len(shapes)) if last else in_vmem(len(shapes)),
        scratch_shapes=scratch,
        limit=(24 if last else 16) * 2**20,
    )(*operands)
    return (results[:2], results[2:6], results[6:]) if defer else (results[:2], results[2:])


def late_products(turned, beside, width):
    count = beside.shape[1] // width

    def kernel(turned_ref, beside_ref, parents_ref, diagonals_ref):
        for place in range(count):
            left = turned_ref[place * width : (place + 2) * width, :]
            right = beside_ref[:, place * width : (place + 1) * width]
            total = jnp.dot(left, right, preferred_element_type=jnp.float32)
            parents_ref[place] = total[:width]
            diagonals_ref[place] = total[width:]

    return kernel_call(
        kernel,
        "late_products",
        out_shape=[jax.ShapeDtypeStruct((count, width, width), jnp.float32)] * 2,
        in_specs=in_vmem(2),
        out_specs=in_vmem(2),
    )(turned, beside)


def gather_plan(anc_blocks, anc_links, parent_links, pivot_inverse, pattern):
    chips = lax.axis_size("row") // 2
    far = chips // 2
    ahead, behind = ring_pairs(chips, 1), ring_pairs(chips, -1)
    across = [p for p in ahead if p[0] % 2 == 0] + [p for p in behind if p[0] % 2 == 1]

    def move(pair):
        return [lax.ppermute(value, "row", way) for value, way in zip(pair, (ahead, behind))]

    def both(shift, value):
        return [(shift, False, value), (shift, True, swap_bit(value, 0))]

    turned = anc_blocks[0].T
    far_part = far_rows(turned)
    links = link_chain(after(anc_links, far_part), parent_links, pattern)
    own = message_of(turned, swap_bit(far_part, PCOL.bit_length() - 1), links)
    totals, state = inner_chain(after(parent_links, own), pivot_inverse), None
    arrivals, pair = both(0, own), [own] * 2
    for step in range(1, far):
        pair = move(pair)
        totals, state = border(arrivals, state, *totals, chips)
        pair = [after(value, *totals) for value in pair]
        arrivals = both(-step, pair[0]) + both(step, pair[1])
    last, totals = lax.optimization_barrier((pick(pair), totals))
    totals, state, tails = border(arrivals, state, *totals, chips, defer=LATE_PANELS)
    last, totals, tails = lax.optimization_barrier((lax.ppermute(last, "row", across), totals, tails))
    late = late_products(*tails, anc_links.shape[2])
    totals, panels = border(both(far, last), state, *totals, chips, True, late)
    return panels[0], *totals


def spread_plan(anc_blocks, anc_links, parent_links, pivot_inverse, pattern):
    my_index = lax.axis_index("row")
    total_bits = lax.axis_size("row").bit_length() - 1
    low_bits = PCOL.bit_length() - 1
    rows, nodes, width = anc_links.shape
    links = jnp.concatenate(reduced_links(masked_links(my_index, anc_links, pattern), parent_links), axis=1)
    segment = links
    for bit in range(low_bits, total_bits):
        partner = swap_bit(segment, bit)
        upper = my_index >> bit & 1
        segment = lax.dynamic_update_slice_in_dim(
            jnp.concatenate([partner, partner], 0), segment, upper * segment.shape[0], 0
        )
    image = product(anc_blocks[0], segment)
    for bit in reversed(range(low_bits)):
        half_rows = image.shape[0] // 2
        upper = my_index >> bit & 1
        retained = lax.dynamic_slice_in_dim(image, upper * half_rows, half_rows, 0)
        outgoing = lax.dynamic_slice_in_dim(image, (1 - upper) * half_rows, half_rows, 0)
        image = retained + swap_bit(outgoing, bit)
    column = lambda array, node: array[:, node * width : (node + 1) * width]
    terms = [inner_product(column(links, node), column(image, node)) for node in range(nodes)]
    terms += [inner_product(column(links, node - 1), column(image, node)) for node in range(1, nodes)]
    totals = lax.psum(jnp.stack(terms), "row")
    inner, cross = local_chain(parent_links, pivot_inverse)
    diagonals = jnp.stack(inner) + totals[:nodes]
    parents = totals[nodes:] - jnp.stack(cross)
    return -image.reshape(rows, nodes, width), parents, diagonals


def on_device(anc_blocks, anc_links, parent_links, pivot_inverse, pattern):
    size = lax.axis_size("row")
    rows, nodes, width = anc_links.shape
    whole_bytes = 4 * size * rows * (nodes * width + size * rows)
    plan = gather_plan if size == 2 * PCOL and whole_bytes <= GATHER_LIMIT else spread_plan
    return plan(anc_blocks, anc_links, parent_links, pivot_inverse, pattern)


def solution(mesh):
    return jax.shard_map(
        on_device,
        mesh=mesh,
        in_specs=(
            P(("pole", "row"), None, None),
            P(("pole", "row"), None, None),
            P("pole", None, None),
            P("pole", None, None),
            P(),
        ),
        out_specs=(P(("pole", "row"), None, None), P("pole", None, None), P("pole", None, None)),
        check_vma=False,
    )
```

```python
import jax
import jax.numpy as jnp
from jax import lax
from jax.experimental import pallas as pl
from jax.experimental.pallas import tpu as pltpu
from jax.sharding import PartitionSpec as P

PCOL = 8
TILE = 128
GATHER_LIMIT = 16 * 2**20
SIDE = 256
LATE_PANELS = 3
FIRST_FLOPS = 4_000_000_000


def product(left, right):
    return jnp.dot(left, right, precision=lax.Precision.HIGHEST, preferred_element_type=jnp.float32)


def inner_product(left, right):
    return lax.dot_general(
        left,
        right,
        (((0,), (0,)), ((), ())),
        precision=lax.Precision.HIGHEST,
        preferred_element_type=jnp.float32,
    )


def swap_bit(value, bit):
    mask = 2**bit
    return lax.ppermute(value, "row", [(i, i ^ mask) for i in range(lax.axis_size("row"))])


def ring_chips(count):
    return list(range(0, count, 2)) + list(range(count - 1, 0, -2))


def ring_pairs(count, shift):
    order = ring_chips(count)
    pairs = []
    for place, chip in enumerate(order):
        target = order[(place + shift) % count]
        pairs += [(2 * chip + core, 2 * target + core) for core in range(2)]
    return pairs


def masked_links(my_index, anc_links, pattern):
    rows_here = anc_links.shape[0]
    tile_index = (my_index * rows_here + jnp.arange(rows_here, dtype=jnp.int32)) // TILE
    row_keep = jnp.take(pattern, tile_index, axis=1) != 0
    return jnp.where(row_keep[:, :, None], jnp.swapaxes(anc_links, 0, 1), 0.0)


def reduced_links(links, parent_links):
    reduced = [links[0]]
    for node in range(1, links.shape[0]):
        reduced.append(links[node] - product(reduced[-1], parent_links[node - 1]))
    return reduced


def local_chain(parent_links, pivot_inverse):
    inner = [pivot_inverse[0]]
    cross = []
    for node in range(1, pivot_inverse.shape[0]):
        link = parent_links[node - 1]
        cross.append(product(inner[-1], link))
        inner.append(pivot_inverse[node] + inner_product(link, cross[-1]))
    return inner, cross


def halves(value):
    high = value.astype(jnp.bfloat16)
    return high, (value - high.astype(jnp.float32)).astype(jnp.bfloat16)


def dot_halves(left, right, dims=((1,), (0,))):
    def one(a, b):
        return lax.dot_general(a, b, (dims, ((), ())), preferred_element_type=jnp.float32)

    return one(left[0], right[0]) + (one(left[0], right[1]) + one(left[1], right[0]))


def stacked_dot(left, right):
    height = left[0].shape[0]
    both = jnp.dot(jnp.concatenate(left, axis=0), right[0], preferred_element_type=jnp.float32)
    cross = jnp.dot(left[0], right[1], preferred_element_type=jnp.float32)
    return both[:height] + (both[height:] + cross)


def kernel_call(kernel, name, limit=16 * 2**20, flops=0, **more):
    return pl.pallas_call(
        kernel,
        name=name,
        compiler_params=pltpu.CompilerParams(vmem_limit_bytes=limit),
        cost_estimate=pl.CostEstimate(flops=flops, bytes_accessed=0, transcendentals=0),
        **more,
    )


def in_vmem(count):
    return [pl.BlockSpec(memory_space=pltpu.VMEM)] * count


def after(value, *others):
    return lax.optimization_barrier((value, *others))[0]


def at_home(count):
    return [pl.BlockSpec(memory_space=pltpu.HBM)] * count


def far_rows(turned):
    rows, columns = turned.shape[0] // 2, turned.shape[1]

    def kernel(turned_ref, out_ref):
        me = lax.axis_index("row")
        low = me < PCOL
        theirs = jnp.where(low, turned_ref[rows:], turned_ref[:rows])
        first = lax.rem(me, PCOL) + jnp.where(low, 1, 0)
        theirs = pltpu.roll(theirs, lax.rem(columns - lax.rem(first, PCOL) * rows, columns), 1)[:, : columns // 2]
        out_ref[...] = jnp.concatenate([theirs[: rows // 2], theirs[rows // 2 :]], axis=1)

    return kernel_call(
        kernel,
        "far_rows",
        flops=FIRST_FLOPS,
        out_shape=jax.ShapeDtypeStruct((rows // 2, columns), jnp.float32),
        in_specs=in_vmem(1),
        out_specs=in_vmem(1)[0],
    )(turned)


def pick(pair):
    def kernel(first_ref, second_ref, out_ref):
        out_ref[...] = jnp.where(lax.rem(lax.axis_index("row"), 2) == 0, first_ref[...], second_ref[...])

    return kernel_call(
        kernel,
        "pick",
        out_shape=jax.ShapeDtypeStruct(pair[0].shape, jnp.float32),
        in_specs=in_vmem(2),
        out_specs=in_vmem(1)[0],
    )(*pair)


def link_chain(anc_links, parent_links, pattern):
    rows, nodes, width = anc_links.shape
    tiles = pattern.shape[1]

    def kernel(links_ref, parent_ref, pattern_ref, out_ref):
        first = lax.axis_index("row") * rows
        tile = first // TILE
        next_tile = jnp.minimum(tile + 1, tiles - 1)
        row = first + lax.broadcasted_iota(jnp.int32, (rows, width), 0)
        in_first = row < (tile + 1) * TILE
        reduced = None
        for node in range(nodes):
            keep = jnp.where(in_first, pattern_ref[node, tile], pattern_ref[node, next_tile])
            links = jnp.where(keep != 0, links_ref[:, node, :], 0.0)
            if node > 0:
                links = links - dot_halves(halves(reduced), halves(parent_ref[node - 1]))
            out_ref[:, node * width : (node + 1) * width] = links
            reduced = links

    return kernel_call(
        kernel,
        "link_chain",
        out_shape=jax.ShapeDtypeStruct((rows, nodes * width), jnp.float32),
        in_specs=in_vmem(2) + [pl.BlockSpec(memory_space=pltpu.SMEM)],
        out_specs=in_vmem(1)[0],
    )(anc_links, parent_links, pattern)


def message_of(turned, far, links):
    rows, columns = turned.shape[0] // 2, turned.shape[1]
    near = columns // 2 + rows

    def kernel(turned_ref, far_ref, links_ref, out_ref):
        me = lax.axis_index("row")
        mine = jnp.where(me < PCOL, turned_ref[:rows], turned_ref[rows:])
        mine = pltpu.roll(mine, lax.rem(columns - lax.rem(me, PCOL) * rows, columns), 1)[:, :SIDE]
        lane = lax.broadcasted_iota(jnp.int32, (1, SIDE), 1)
        weight = jnp.where((lane < rows) | (lane >= near - rows), 0.5, 1.0)
        out_ref[:, :SIDE] = mine * jnp.where(lane < near, weight, 0.0)
        out_ref[:, SIDE : 2 * SIDE] = jnp.zeros((rows, SIDE), jnp.float32)
        out_ref[: rows // 2, SIDE : SIDE + columns // 2] = far_ref[:, : columns // 2]
        out_ref[rows // 2 :, SIDE : SIDE + columns // 2] = far_ref[:, columns // 2 :]
        out_ref[:, 2 * SIDE :] = links_ref[...]

    return kernel_call(
        kernel,
        "message",
        out_shape=jax.ShapeDtypeStruct((rows, 2 * SIDE + links.shape[1]), jnp.float32),
        in_specs=in_vmem(3),
        out_specs=in_vmem(1)[0],
    )(turned, far, links)


def sent_rows(sides, owner, rows):
    columns = PCOL * rows
    rest = jnp.zeros((rows, columns - SIDE), jnp.float32)
    piece, low = lax.rem(owner, PCOL), owner < PCOL
    first = lax.rem(piece + jnp.where(low, 0, 1), PCOL)
    near = pltpu.roll(jnp.concatenate([sides[:, :SIDE], rest], axis=1), piece * rows, 1)
    far = pltpu.roll(jnp.concatenate([sides[:, SIDE:], rest], axis=1), first * rows, 1)
    return jnp.concatenate([jnp.where(low, near, far), jnp.where(low, far, near)], axis=1)


def columns_at(ref, start, count):
    base = pl.multiple_of(lax.div(start, 128) * 128, 128)
    return pltpu.roll(ref[:, pl.ds(base, 256)], lax.rem(256 + base - start, 256), 1)[:, :128]


def inner_chain(parent_links, pivot_inverse):
    nodes, width, _ = pivot_inverse.shape

    def kernel(parent_ref, pivot_ref, cross_ref, inner_ref):
        inner = pivot_ref[0]
        inner_ref[0] = inner
        for node in range(1, nodes):
            link = halves(parent_ref[node - 1])
            cross = dot_halves(halves(inner), link)
            cross_ref[node - 1] = -cross
            inner = pivot_ref[node] + dot_halves(link, halves(cross), ((0,), (0,)))
            inner_ref[node] = inner

    return kernel_call(
        kernel,
        "inner_chain",
        out_shape=[jax.ShapeDtypeStruct(array.shape, jnp.float32) for array in (parent_links, pivot_inverse)],
        in_specs=in_vmem(2),
        out_specs=in_vmem(2),
    )(parent_links, pivot_inverse)


def ring_owner(my_index, count, shift, other):
    core = lax.rem(my_index, 2)
    chip = my_index // 2
    place = jnp.where(lax.rem(chip, 2) == 0, chip // 2, count - 1 - chip // 2)
    place = lax.rem(place + shift + count, count)
    chip = jnp.where(place < count // 2, 2 * place, 2 * (count - 1 - place) + 1)
    return 2 * chip + (1 - core if other else core)


def border(arrivals, state, parents, diagonals, chips, last=False, late=None, defer=0):
    begin = state is None
    nodes, width, _ = diagonals.shape
    rows = arrivals[0][2].shape[0]
    lanes = 2 * SIDE
    order = 2 * chips * rows
    count = len(arrivals)
    fresh = rows * count
    bf16, f32 = jnp.bfloat16, jnp.float32

    def kernel(*refs):
        refs = list(refs)
        take = lambda number: [refs.pop(0) for _ in range(number)]
        part_refs = take(count)
        panel_before, kept_before, *held_before = take(4) if not begin else [None] * 4
        parents_ref, diagonals_ref = take(2)
        late_parents, late_diagonals = take(2) if late else [None] * 2
        parents_out, diagonals_out, panel_out = take(3)
        copies = []

        def finish(place, source, target):
            if last:
                copies.append(pltpu.make_async_copy(source, target, sems.at[place]))
                copies[-1].start()

        parents_end, diagonals_end, panel_end = parents_out, diagonals_out, panel_out
        kept_now = None if last else take(1)[0]
        held_now = take(0 if last else 2)
        tails = take(2 if defer else 0)
        turned, beside, aside = take(3)
        if last:
            parents_out, diagonals_out, panel_out, sems = take(4)
        me = lax.axis_index("row")
        core = lax.rem(me, 2)
        owners = [ring_owner(me, chips, shift, other) for shift, other, _ in arrivals]
        starts = [pl.multiple_of(owner * rows, 16) for owner in owners]

        for part, whole in enumerate(held_now):
            whole[...] = jnp.zeros(whole.shape, bf16) if begin else held_before[part][...]
        held = held_before if last else held_now
        for start, ref in zip(starts, part_refs):
            for whole, part in zip(held_now, halves(ref[:, lanes:])):
                whole[pl.ds(start, rows), :] = part
        sent = [sent_rows(ref[:, :lanes], owner, rows) for owner, ref in zip(owners, part_refs)]
        if not last:
            kept_now[...] = jnp.zeros(kept_now.shape, f32) if begin else kept_before[...]
            for start, part in zip(starts, sent):
                kept_now[pl.ds(start, rows), :order] = part
        if not begin:
            for pair in range(0, count, 2):
                back = columns_at(kept_before, lax.div(owners[pair], 2) * (2 * rows), 2 * rows).T
                first, second = back[:rows], back[rows : 2 * rows]
                sent[pair] += jnp.where(core == 0, first, second)
                sent[pair + 1] += jnp.where(core == 0, second, first)
        left = jnp.concatenate(sent, axis=0)
        aside[:, :order] = left
        aside[:, order:] = jnp.zeros((fresh, 128), f32)
        across = columns_at(aside, me * rows, rows).T[:rows]
        if begin:
            pair = columns_at(aside, lax.div(me, 2) * (2 * rows), 2 * rows)[:rows]
            swapped = jnp.concatenate([pair[:, rows : 2 * rows], pair[:, :rows]], axis=1)
            across += jnp.where(core == 0, pair[:, : 2 * rows], swapped)
        if last:
            pair = columns_at(aside, lax.div(owners[0], 2) * (2 * rows), 2 * rows)
            swapped = jnp.concatenate([pair[:, rows : 2 * rows], pair[:, :rows]], axis=1)
            between = halves(jnp.where(core == 0, pair[:, : 2 * rows], swapped))
        left, across = halves(left), halves(across)
        for node in range(nodes):
            columns = slice(node * width, (node + 1) * width)
            image = stacked_dot(left, [whole[:, columns] for whole in held])
            there = slice(lanes + node * width, lanes + (node + 1) * width)
            new = jnp.concatenate([ref[:, there] for ref in part_refs], axis=0)
            new_high, new_low = halves(new)
            if last:
                image = image + stacked_dot(between, [new_high, new_low])
            image_high, image_low = halves(image)
            own = stacked_dot(across, [new_high, new_low])
            if not begin:
                own += panel_before[:, columns]
            if last:
                panel_out[:, node, :] = -own
            else:
                panel_out[:, columns] = own
            high, low = halves(jnp.concatenate([new, image], axis=0).T)
            for place, part in enumerate((high, low, high)):
                turned[columns, 2 * fresh * place : 2 * fresh * (place + 1)] = part
            for place, part in enumerate((image_high, new_high, image_high, new_high, image_low, new_low)):
                beside[fresh * place : fresh * (place + 1), columns] = part
        if last:
            finish(2 * nodes, panel_out, panel_end)
        rest = nodes - defer
        if defer:
            tails[0][...] = turned[(rest - 1) * width :, :]
            tails[1][...] = beside[:, rest * width :]
            diagonals_out[rest:] = diagonals_ref[rest:]
            parents_out[rest - 1 :] = parents_ref[rest - 1 :]
        for node in range(rest):
            lower = max(node - 1, 0) * width
            columns = slice(node * width, (node + 1) * width)
            total = jnp.dot(turned[lower : columns.stop, :], beside[:, columns], preferred_element_type=f32)
            total_below, total_here = total[:width], total[-width:]
            if late and node >= nodes - late[0].shape[0]:
                place = node - nodes + late[0].shape[0]
                total_below = total_below + late_parents[place]
                total_here = total_here + late_diagonals[place]
            diagonals_out[node] = diagonals_ref[node] + total_here
            finish(node, diagonals_out.at[node], diagonals_end.at[node])
            if node > 0:
                parents_out[node - 1] = parents_ref[node - 1] + total_below
                finish(nodes + node, parents_out.at[node - 1], parents_end.at[node - 1])
        for copy in copies:
            copy.wait()

    operands = [part for _, _, part in arrivals] + list(state or [])
    operands += [parents, diagonals] + list(late or [])
    shape_of = jax.ShapeDtypeStruct
    shapes = [shape_of(parents.shape, f32), shape_of(diagonals.shape, f32)]
    held = [shape_of((order, nodes * width), bf16)] * 2
    scratch = [((nodes * width, 6 * fresh), bf16), ((6 * fresh, nodes * width), bf16), ((fresh, order + 128), f32)]
    scratch = [pltpu.VMEM(*shape) for shape in scratch]
    if last:
        shapes.append(shape_of((rows, nodes, width), f32))
        scratch += [pltpu.VMEM(shape.shape, f32) for shape in shapes]
        scratch.append(pltpu.SemaphoreType.DMA((2 * nodes + 1,)))
    else:
        shapes += [shape_of((rows, nodes * width), f32), shape_of((order, order + 128), f32)] + held
    if defer:
        shapes.append(shape_of(((defer + 1) * width, 6 * fresh), bf16))
        shapes.append(shape_of((6 * fresh, defer * width), bf16))
    results = kernel_call(
        kernel,
        "border" + ("_end" if last else "_begin" if begin else ""),
        out_shape=shapes,
        in_specs=in_vmem(len(operands)),
        out_specs=at_home(len(shapes)) if last else in_vmem(len(shapes)),
        scratch_shapes=scratch,
        limit=(24 if last else 16) * 2**20,
    )(*operands)
    return (results[:2], results[2:6], results[6:]) if defer else (results[:2], results[2:])


def late_products(turned, beside, width):
    count = beside.shape[1] // width

    def kernel(turned_ref, beside_ref, parents_ref, diagonals_ref):
        for place in range(count):
            left = turned_ref[place * width : (place + 2) * width, :]
            right = beside_ref[:, place * width : (place + 1) * width]
            total = jnp.dot(left, right, preferred_element_type=jnp.float32)
            parents_ref[place] = total[:width]
            diagonals_ref[place] = total[width:]

    return kernel_call(
        kernel,
        "late_products",
        out_shape=[jax.ShapeDtypeStruct((count, width, width), jnp.float32)] * 2,
        in_specs=in_vmem(2),
        out_specs=in_vmem(2),
    )(turned, beside)


def gather_plan(anc_blocks, anc_links, parent_links, pivot_inverse, pattern):
    chips = lax.axis_size("row") // 2
    far = chips // 2
    ahead, behind = ring_pairs(chips, 1), ring_pairs(chips, -1)
    across = [p for p in ahead if p[0] % 2 == 0] + [p for p in behind if p[0] % 2 == 1]

    def move(pair):
        return [lax.ppermute(value, "row", way) for value, way in zip(pair, (ahead, behind))]

    def both(shift, value):
        return [(shift, False, value), (shift, True, swap_bit(value, 0))]

    turned = anc_blocks[0].T
    far_part = far_rows(turned)
    links = link_chain(after(anc_links, far_part), parent_links, pattern)
    own = message_of(turned, swap_bit(far_part, PCOL.bit_length() - 1), links)
    totals, state = inner_chain(after(parent_links, own), pivot_inverse), None
    arrivals, pair = both(0, own), [own] * 2
    for step in range(1, far):
        pair = move(pair)
        totals, state = border(arrivals, state, *totals, chips)
        pair = [after(value, *totals) for value in pair]
        arrivals = both(-step, pair[0]) + both(step, pair[1])
    last, totals = lax.optimization_barrier((pick(pair), totals))
    totals, state, tails = border(arrivals, state, *totals, chips, defer=LATE_PANELS)
    last, totals, tails = lax.optimization_barrier((lax.ppermute(last, "row", across), totals, tails))
    late = late_products(*tails, anc_links.shape[2])
    totals, panels = border(both(far, last), state, *totals, chips, True, late)
    return panels[0], *totals


def spread_plan(anc_blocks, anc_links, parent_links, pivot_inverse, pattern):
    my_index = lax.axis_index("row")
    total_bits = lax.axis_size("row").bit_length() - 1
    low_bits = PCOL.bit_length() - 1
    rows, nodes, width = anc_links.shape
    links = jnp.concatenate(reduced_links(masked_links(my_index, anc_links, pattern), parent_links), axis=1)
    segment = links
    for bit in range(low_bits, total_bits):
        partner = swap_bit(segment, bit)
        upper = my_index >> bit & 1
        segment = lax.dynamic_update_slice_in_dim(
            jnp.concatenate([partner, partner], 0), segment, upper * segment.shape[0], 0
        )
    image = product(anc_blocks[0], segment)
    for bit in reversed(range(low_bits)):
        half_rows = image.shape[0] // 2
        upper = my_index >> bit & 1
        retained = lax.dynamic_slice_in_dim(image, upper * half_rows, half_rows, 0)
        outgoing = lax.dynamic_slice_in_dim(image, (1 - upper) * half_rows, half_rows, 0)
        image = retained + swap_bit(outgoing, bit)
    column = lambda array, node: array[:, node * width : (node + 1) * width]
    terms = [inner_product(column(links, node), column(image, node)) for node in range(nodes)]
    terms += [inner_product(column(links, node - 1), column(image, node)) for node in range(1, nodes)]
    totals = lax.psum(jnp.stack(terms), "row")
    inner, cross = local_chain(parent_links, pivot_inverse)
    diagonals = jnp.stack(inner) + totals[:nodes]
    parents = totals[nodes:] - jnp.stack(cross)
    return -image.reshape(rows, nodes, width), parents, diagonals


def on_device(anc_blocks, anc_links, parent_links, pivot_inverse, pattern):
    size = lax.axis_size("row")
    rows, nodes, width = anc_links.shape
    whole_bytes = 4 * size * rows * (nodes * width + size * rows)
    plan = gather_plan if size == 2 * PCOL and whole_bytes <= GATHER_LIMIT else spread_plan
    return plan(anc_blocks, anc_links, parent_links, pivot_inverse, pattern)


def solution(mesh):
    return jax.shard_map(
        on_device,
        mesh=mesh,
        in_specs=(
            P(("pole", "row"), None, None),
            P(("pole", "row"), None, None),
            P("pole", None, None),
            P("pole", None, None),
            P(),
        ),
        out_specs=(P(("pole", "row"), None, None), P("pole", None, None), P("pole", None, None)),
        check_vma=False,
    )
```

```python
import jax
import jax.numpy as jnp
from jax import lax
from jax.experimental import pallas as pl
from jax.experimental.pallas import tpu as pltpu
from jax.sharding import PartitionSpec as P

PCOL = 8
TILE = 128
GATHER_LIMIT = 16 * 2**20
SIDE = 256
LATE_PANELS = 3
FIRST_FLOPS = 4_000_000_000


def product(left, right):
    return jnp.dot(left, right, precision=lax.Precision.HIGHEST, preferred_element_type=jnp.float32)


def inner_product(left, right):
    return lax.dot_general(
        left,
        right,
        (((0,), (0,)), ((), ())),
        precision=lax.Precision.HIGHEST,
        preferred_element_type=jnp.float32,
    )


def swap_bit(value, bit):
    mask = 2**bit
    return lax.ppermute(value, "row", [(i, i ^ mask) for i in range(lax.axis_size("row"))])


def ring_chips(count):
    return list(range(0, count, 2)) + list(range(count - 1, 0, -2))


def ring_pairs(count, shift):
    order = ring_chips(count)
    pairs = []
    for place, chip in enumerate(order):
        target = order[(place + shift) % count]
        pairs += [(2 * chip + core, 2 * target + core) for core in range(2)]
    return pairs


def masked_links(my_index, anc_links, pattern):
    rows_here = anc_links.shape[0]
    tile_index = (my_index * rows_here + jnp.arange(rows_here, dtype=jnp.int32)) // TILE
    row_keep = jnp.take(pattern, tile_index, axis=1) != 0
    return jnp.where(row_keep[:, :, None], jnp.swapaxes(anc_links, 0, 1), 0.0)


def reduced_links(links, parent_links):
    reduced = [links[0]]
    for node in range(1, links.shape[0]):
        reduced.append(links[node] - product(reduced[-1], parent_links[node - 1]))
    return reduced


def local_chain(parent_links, pivot_inverse):
    inner = [pivot_inverse[0]]
    cross = []
    for node in range(1, pivot_inverse.shape[0]):
        link = parent_links[node - 1]
        cross.append(product(inner[-1], link))
        inner.append(pivot_inverse[node] + inner_product(link, cross[-1]))
    return inner, cross


def halves(value):
    high = value.astype(jnp.bfloat16)
    return high, (value - high.astype(jnp.float32)).astype(jnp.bfloat16)


def dot_halves(left, right, dims=((1,), (0,))):
    def one(a, b):
        return lax.dot_general(a, b, (dims, ((), ())), preferred_element_type=jnp.float32)

    return one(left[0], right[0]) + (one(left[0], right[1]) + one(left[1], right[0]))


def stacked_dot(left, right):
    height = left[0].shape[0]
    both = jnp.dot(jnp.concatenate(left, axis=0), right[0], preferred_element_type=jnp.float32)
    cross = jnp.dot(left[0], right[1], preferred_element_type=jnp.float32)
    return both[:height] + (both[height:] + cross)


def kernel_call(kernel, name, limit=16 * 2**20, flops=0, **more):
    return pl.pallas_call(
        kernel,
        name=name,
        compiler_params=pltpu.CompilerParams(vmem_limit_bytes=limit),
        cost_estimate=pl.CostEstimate(flops=flops, bytes_accessed=0, transcendentals=0),
        **more,
    )


def in_vmem(count):
    return [pl.BlockSpec(memory_space=pltpu.VMEM)] * count


def after(value, *others):
    return lax.optimization_barrier((value, *others))[0]


def at_home(count):
    return [pl.BlockSpec(memory_space=pltpu.HBM)] * count


def far_rows(turned):
    rows, columns = turned.shape[0] // 2, turned.shape[1]

    def kernel(turned_ref, out_ref):
        me = lax.axis_index("row")
        low = me < PCOL
        theirs = jnp.where(low, turned_ref[rows:], turned_ref[:rows])
        first = lax.rem(me, PCOL) + jnp.where(low, 1, 0)
        theirs = pltpu.roll(theirs, lax.rem(columns - lax.rem(first, PCOL) * rows, columns), 1)[:, : columns // 2]
        out_ref[...] = jnp.concatenate([theirs[: rows // 2], theirs[rows // 2 :]], axis=1)

    return kernel_call(
        kernel,
        "far_rows",
        flops=FIRST_FLOPS,
        out_shape=jax.ShapeDtypeStruct((rows // 2, columns), jnp.float32),
        in_specs=in_vmem(1),
        out_specs=in_vmem(1)[0],
    )(turned)


def upper_and_lower(pair):
    rows, columns = pair[0].shape

    def kernel(first_ref, second_ref, upper_ref, lower_ref):
        upper_ref[...] = first_ref[: rows // 2]
        lower_ref[...] = second_ref[rows // 2 :]

    shape = jax.ShapeDtypeStruct((rows // 2, columns), jnp.float32)
    return kernel_call(kernel, "upper_lower", out_shape=[shape] * 2, in_specs=in_vmem(2), out_specs=in_vmem(2))(*pair)


def stacked(pair):
    rows, columns = pair[0].shape

    def kernel(upper_ref, lower_ref, out_ref):
        out_ref[:rows] = upper_ref[...]
        out_ref[rows:] = lower_ref[...]

    shape = jax.ShapeDtypeStruct((2 * rows, columns), jnp.float32)
    return kernel_call(kernel, "stacked", out_shape=shape, in_specs=in_vmem(2), out_specs=in_vmem(1)[0])(*pair)


def link_chain(anc_links, parent_links, pattern):
    rows, nodes, width = anc_links.shape
    tiles = pattern.shape[1]

    def kernel(links_ref, parent_ref, pattern_ref, out_ref):
        first = lax.axis_index("row") * rows
        tile = first // TILE
        next_tile = jnp.minimum(tile + 1, tiles - 1)
        row = first + lax.broadcasted_iota(jnp.int32, (rows, width), 0)
        in_first = row < (tile + 1) * TILE
        reduced = None
        for node in range(nodes):
            keep = jnp.where(in_first, pattern_ref[node, tile], pattern_ref[node, next_tile])
            links = jnp.where(keep != 0, links_ref[:, node, :], 0.0)
            if node > 0:
                links = links - dot_halves(halves(reduced), halves(parent_ref[node - 1]))
            out_ref[:, node * width : (node + 1) * width] = links
            reduced = links

    return kernel_call(
        kernel,
        "link_chain",
        out_shape=jax.ShapeDtypeStruct((rows, nodes * width), jnp.float32),
        in_specs=in_vmem(2) + [pl.BlockSpec(memory_space=pltpu.SMEM)],
        out_specs=in_vmem(1)[0],
    )(anc_links, parent_links, pattern)


def message_of(turned, far, links):
    rows, columns = turned.shape[0] // 2, turned.shape[1]
    near = columns // 2 + rows

    def kernel(turned_ref, far_ref, links_ref, out_ref):
        me = lax.axis_index("row")
        mine = jnp.where(me < PCOL, turned_ref[:rows], turned_ref[rows:])
        mine = pltpu.roll(mine, lax.rem(columns - lax.rem(me, PCOL) * rows, columns), 1)[:, :SIDE]
        lane = lax.broadcasted_iota(jnp.int32, (1, SIDE), 1)
        weight = jnp.where((lane < rows) | (lane >= near - rows), 0.5, 1.0)
        out_ref[:, :SIDE] = mine * jnp.where(lane < near, weight, 0.0)
        out_ref[:, SIDE : 2 * SIDE] = jnp.zeros((rows, SIDE), jnp.float32)
        out_ref[: rows // 2, SIDE : SIDE + columns // 2] = far_ref[:, : columns // 2]
        out_ref[rows // 2 :, SIDE : SIDE + columns // 2] = far_ref[:, columns // 2 :]
        out_ref[:, 2 * SIDE :] = links_ref[...]

    return kernel_call(
        kernel,
        "message",
        out_shape=jax.ShapeDtypeStruct((rows, 2 * SIDE + links.shape[1]), jnp.float32),
        in_specs=in_vmem(3),
        out_specs=in_vmem(1)[0],
    )(turned, far, links)


def sent_rows(sides, owner, rows):
    columns = PCOL * rows
    rest = jnp.zeros((rows, columns - SIDE), jnp.float32)
    piece, low = lax.rem(owner, PCOL), owner < PCOL
    first = lax.rem(piece + jnp.where(low, 0, 1), PCOL)
    near = pltpu.roll(jnp.concatenate([sides[:, :SIDE], rest], axis=1), piece * rows, 1)
    far = pltpu.roll(jnp.concatenate([sides[:, SIDE:], rest], axis=1), first * rows, 1)
    return jnp.concatenate([jnp.where(low, near, far), jnp.where(low, far, near)], axis=1)


def columns_at(ref, start, count):
    base = pl.multiple_of(lax.div(start, 128) * 128, 128)
    return pltpu.roll(ref[:, pl.ds(base, 256)], lax.rem(256 + base - start, 256), 1)[:, :128]


def inner_chain(parent_links, pivot_inverse):
    nodes, width, _ = pivot_inverse.shape

    def kernel(parent_ref, pivot_ref, cross_ref, inner_ref):
        inner = pivot_ref[0]
        inner_ref[0] = inner
        for node in range(1, nodes):
            link = halves(parent_ref[node - 1])
            cross = dot_halves(halves(inner), link)
            cross_ref[node - 1] = -cross
            inner = pivot_ref[node] + dot_halves(link, halves(cross), ((0,), (0,)))
            inner_ref[node] = inner

    return kernel_call(
        kernel,
        "inner_chain",
        out_shape=[jax.ShapeDtypeStruct(array.shape, jnp.float32) for array in (parent_links, pivot_inverse)],
        in_specs=in_vmem(2),
        out_specs=in_vmem(2),
    )(parent_links, pivot_inverse)


def ring_owner(my_index, count, shift, other):
    core = lax.rem(my_index, 2)
    chip = my_index // 2
    place = jnp.where(lax.rem(chip, 2) == 0, chip // 2, count - 1 - chip // 2)
    place = lax.rem(place + shift + count, count)
    chip = jnp.where(place < count // 2, 2 * place, 2 * (count - 1 - place) + 1)
    return 2 * chip + (1 - core if other else core)


def border(arrivals, state, parents, diagonals, chips, last=False, late=None, defer=0):
    begin = state is None
    nodes, width, _ = diagonals.shape
    rows = arrivals[0][2].shape[0]
    lanes = 2 * SIDE
    order = 2 * chips * rows
    count = len(arrivals)
    fresh = rows * count
    bf16, f32 = jnp.bfloat16, jnp.float32

    def kernel(*refs):
        refs = list(refs)
        take = lambda number: [refs.pop(0) for _ in range(number)]
        part_refs = take(count)
        panel_before, kept_before, *held_before = take(4) if not begin else [None] * 4
        parents_ref, diagonals_ref = take(2)
        late_parents, late_diagonals = take(2) if late else [None] * 2
        parents_out, diagonals_out, panel_out = take(3)
        copies = []

        def finish(place, source, target):
            if last:
                copies.append(pltpu.make_async_copy(source, target, sems.at[place]))
                copies[-1].start()

        parents_end, diagonals_end, panel_end = parents_out, diagonals_out, panel_out
        kept_now = None if last else take(1)[0]
        held_now = take(0 if last else 2)
        tails = take(2 if defer else 0)
        turned, beside, aside = take(3)
        if last:
            parents_out, diagonals_out, panel_out, sems = take(4)
        me = lax.axis_index("row")
        core = lax.rem(me, 2)
        owners = [ring_owner(me, chips, shift, other) for shift, other, _ in arrivals]
        starts = [pl.multiple_of(owner * rows, 16) for owner in owners]

        for part, whole in enumerate(held_now):
            whole[...] = jnp.zeros(whole.shape, bf16) if begin else held_before[part][...]
        held = held_before if last else held_now
        for start, ref in zip(starts, part_refs):
            for whole, part in zip(held_now, halves(ref[:, lanes:])):
                whole[pl.ds(start, rows), :] = part
        sent = [sent_rows(ref[:, :lanes], owner, rows) for owner, ref in zip(owners, part_refs)]
        if not last:
            kept_now[...] = jnp.zeros(kept_now.shape, f32) if begin else kept_before[...]
            for start, part in zip(starts, sent):
                kept_now[pl.ds(start, rows), :order] = part
        if not begin:
            for pair in range(0, count, 2):
                back = columns_at(kept_before, lax.div(owners[pair], 2) * (2 * rows), 2 * rows).T
                first, second = back[:rows], back[rows : 2 * rows]
                sent[pair] += jnp.where(core == 0, first, second)
                sent[pair + 1] += jnp.where(core == 0, second, first)
        left = jnp.concatenate(sent, axis=0)
        aside[:, :order] = left
        aside[:, order:] = jnp.zeros((fresh, 128), f32)
        across = columns_at(aside, me * rows, rows).T[:rows]
        if begin:
            pair = columns_at(aside, lax.div(me, 2) * (2 * rows), 2 * rows)[:rows]
            swapped = jnp.concatenate([pair[:, rows : 2 * rows], pair[:, :rows]], axis=1)
            across += jnp.where(core == 0, pair[:, : 2 * rows], swapped)
        if last:
            pair = columns_at(aside, lax.div(owners[0], 2) * (2 * rows), 2 * rows)
            swapped = jnp.concatenate([pair[:, rows : 2 * rows], pair[:, :rows]], axis=1)
            between = halves(jnp.where(core == 0, pair[:, : 2 * rows], swapped))
        left, across = halves(left), halves(across)
        for node in range(nodes):
            columns = slice(node * width, (node + 1) * width)
            image = stacked_dot(left, [whole[:, columns] for whole in held])
            there = slice(lanes + node * width, lanes + (node + 1) * width)
            new = jnp.concatenate([ref[:, there] for ref in part_refs], axis=0)
            new_high, new_low = halves(new)
            if last:
                image = image + stacked_dot(between, [new_high, new_low])
            image_high, image_low = halves(image)
            own = stacked_dot(across, [new_high, new_low])
            if not begin:
                own += panel_before[:, columns]
            if last:
                panel_out[:, node, :] = -own
            else:
                panel_out[:, columns] = own
            high, low = halves(jnp.concatenate([new, image], axis=0).T)
            for place, part in enumerate((high, low, high)):
                turned[columns, 2 * fresh * place : 2 * fresh * (place + 1)] = part
            for place, part in enumerate((image_high, new_high, image_high, new_high, image_low, new_low)):
                beside[fresh * place : fresh * (place + 1), columns] = part
        if last:
            finish(2 * nodes, panel_out, panel_end)
        rest = nodes - defer
        if defer:
            tails[0][...] = turned[(rest - 1) * width :, :]
            tails[1][...] = beside[:, rest * width :]
            diagonals_out[rest:] = diagonals_ref[rest:]
            parents_out[rest - 1 :] = parents_ref[rest - 1 :]
        for node in range(rest):
            lower = max(node - 1, 0) * width
            columns = slice(node * width, (node + 1) * width)
            total = jnp.dot(turned[lower : columns.stop, :], beside[:, columns], preferred_element_type=f32)
            total_below, total_here = total[:width], total[-width:]
            if late and node >= nodes - late[0].shape[0]:
                place = node - nodes + late[0].shape[0]
                total_below = total_below + late_parents[place]
                total_here = total_here + late_diagonals[place]
            diagonals_out[node] = diagonals_ref[node] + total_here
            finish(node, diagonals_out.at[node], diagonals_end.at[node])
            if node > 0:
                parents_out[node - 1] = parents_ref[node - 1] + total_below
                finish(nodes + node, parents_out.at[node - 1], parents_end.at[node - 1])
        for copy in copies:
            copy.wait()

    operands = [part for _, _, part in arrivals] + list(state or [])
    operands += [parents, diagonals] + list(late or [])
    shape_of = jax.ShapeDtypeStruct
    shapes = [shape_of(parents.shape, f32), shape_of(diagonals.shape, f32)]
    held = [shape_of((order, nodes * width), bf16)] * 2
    scratch = [((nodes * width, 6 * fresh), bf16), ((6 * fresh, nodes * width), bf16), ((fresh, order + 128), f32)]
    scratch = [pltpu.VMEM(*shape) for shape in scratch]
    if last:
        shapes.append(shape_of((rows, nodes, width), f32))
        scratch += [pltpu.VMEM(shape.shape, f32) for shape in shapes]
        scratch.append(pltpu.SemaphoreType.DMA((2 * nodes + 1,)))
    else:
        shapes += [shape_of((rows, nodes * width), f32), shape_of((order, order + 128), f32)] + held
    if defer:
        shapes.append(shape_of(((defer + 1) * width, 6 * fresh), bf16))
        shapes.append(shape_of((6 * fresh, defer * width), bf16))
    results = kernel_call(
        kernel,
        "border" + ("_end" if last else "_begin" if begin else ""),
        out_shape=shapes,
        in_specs=in_vmem(len(operands)),
        out_specs=at_home(len(shapes)) if last else in_vmem(len(shapes)),
        scratch_shapes=scratch,
        limit=(24 if last else 16) * 2**20,
    )(*operands)
    return (results[:2], results[2:6], results[6:]) if defer else (results[:2], results[2:])


def late_products(turned, beside, width):
    count = beside.shape[1] // width

    def kernel(turned_ref, beside_ref, parents_ref, diagonals_ref):
        for place in range(count):
            left = turned_ref[place * width : (place + 2) * width, :]
            right = beside_ref[:, place * width : (place + 1) * width]
            total = jnp.dot(left, right, preferred_element_type=jnp.float32)
            parents_ref[place] = total[:width]
            diagonals_ref[place] = total[width:]

    return kernel_call(
        kernel,
        "late_products",
        out_shape=[jax.ShapeDtypeStruct((count, width, width), jnp.float32)] * 2,
        in_specs=in_vmem(2),
        out_specs=in_vmem(2),
    )(turned, beside)


def gather_plan(anc_blocks, anc_links, parent_links, pivot_inverse, pattern):
    chips = lax.axis_size("row") // 2
    far = chips // 2
    ahead, behind = ring_pairs(chips, 1), ring_pairs(chips, -1)

    def move(pair):
        return [lax.ppermute(value, "row", way) for value, way in zip(pair, (ahead, behind))]

    def both(shift, value):
        return [(shift, False, value), (shift, True, swap_bit(value, 0))]

    turned = anc_blocks[0].T
    far_part = far_rows(turned)
    links = link_chain(after(anc_links, far_part), parent_links, pattern)
    own = message_of(turned, swap_bit(far_part, PCOL.bit_length() - 1), links)
    totals, state = inner_chain(after(parent_links, own), pivot_inverse), None
    arrivals, pair = both(0, own), [own] * 2
    for step in range(1, far):
        pair = move(pair)
        totals, state = border(arrivals, state, *totals, chips)
        pair = [after(value, *totals) for value in pair]
        arrivals = both(-step, pair[0]) + both(step, pair[1])
    halves_on, totals = lax.optimization_barrier((upper_and_lower(pair), totals))
    totals, state, tails = border(arrivals, state, *totals, chips, defer=LATE_PANELS)
    halves_on, totals, tails = lax.optimization_barrier((move(halves_on), totals, tails))
    last = stacked(halves_on)
    late = late_products(*tails, anc_links.shape[2])
    totals, panels = border(both(far, last), state, *totals, chips, True, late)
    return panels[0], *totals


def spread_plan(anc_blocks, anc_links, parent_links, pivot_inverse, pattern):
    my_index = lax.axis_index("row")
    total_bits = lax.axis_size("row").bit_length() - 1
    low_bits = PCOL.bit_length() - 1
    rows, nodes, width = anc_links.shape
    links = jnp.concatenate(reduced_links(masked_links(my_index, anc_links, pattern), parent_links), axis=1)
    segment = links
    for bit in range(low_bits, total_bits):
        partner = swap_bit(segment, bit)
        upper = my_index >> bit & 1
        segment = lax.dynamic_update_slice_in_dim(
            jnp.concatenate([partner, partner], 0), segment, upper * segment.shape[0], 0
        )
    image = product(anc_blocks[0], segment)
    for bit in reversed(range(low_bits)):
        half_rows = image.shape[0] // 2
        upper = my_index >> bit & 1
        retained = lax.dynamic_slice_in_dim(image, upper * half_rows, half_rows, 0)
        outgoing = lax.dynamic_slice_in_dim(image, (1 - upper) * half_rows, half_rows, 0)
        image = retained + swap_bit(outgoing, bit)
    column = lambda array, node: array[:, node * width : (node + 1) * width]
    terms = [inner_product(column(links, node), column(image, node)) for node in range(nodes)]
    terms += [inner_product(column(links, node - 1), column(image, node)) for node in range(1, nodes)]
    totals = lax.psum(jnp.stack(terms), "row")
    inner, cross = local_chain(parent_links, pivot_inverse)
    diagonals = jnp.stack(inner) + totals[:nodes]
    parents = totals[nodes:] - jnp.stack(cross)
    return -image.reshape(rows, nodes, width), parents, diagonals


def on_device(anc_blocks, anc_links, parent_links, pivot_inverse, pattern):
    size = lax.axis_size("row")
    rows, nodes, width = anc_links.shape
    whole_bytes = 4 * size * rows * (nodes * width + size * rows)
    plan = gather_plan if size == 2 * PCOL and whole_bytes <= GATHER_LIMIT else spread_plan
    return plan(anc_blocks, anc_links, parent_links, pivot_inverse, pattern)


def solution(mesh):
    return jax.shard_map(
        on_device,
        mesh=mesh,
        in_specs=(
            P(("pole", "row"), None, None),
            P(("pole", "row"), None, None),
            P("pole", None, None),
            P("pole", None, None),
            P(),
        ),
        out_specs=(P(("pole", "row"), None, None), P("pole", None, None), P("pole", None, None)),
        check_vma=False,
    )
```
